32 devices in a mesh: dp: 4 (over y, x), seq: 8 (over z, core).
Axes of the slice: x: 2, y: 2, z: 4, core: 2. Of those that a mesh axis runs over, the one named last changes fastest.
Arguments:
- tokens: bfloat16 [4, 1024, 512], P('dp', 'seq'), may hold values from -6 to 6
- doc_start: int32 [4, 1024], P('dp', 'seq'), may hold values from 0 to 1, as said below
- norm1_gain: float32 [512], replicated, may hold values from 0.1 to 1.9
- qkv_weight: bfloat16 [512, 1536], replicated, may hold values from -0.25 to 0.25
- out_weight: bfloat16 [512, 512], replicated, may hold values from -1 to 1
- norm2_gain: float32 [512], replicated, may hold values from 0.1 to 1.9
- up_weight: bfloat16 [512, 2048], replicated, may hold values from -0.25 to 0.25
- down_weight: bfloat16 [2048, 512], replicated, may hold values from -0.125 to 0.125
- omega: float32 [8, 64, 256], replicated, may hold values from -6 to 6
- cotangent: bfloat16 [4, 1024, 512], P('dp', 'seq'), may hold values from -6 to 6
Outputs:
- output: bfloat16 [4, 1024, 512], P('dp', 'seq')
- tokens_grad: float32 [4, 1024, 512], P('dp', 'seq')
- norm1_grad: float32 [512], replicated
- qkv_grad: float32 [512, 1536], replicated
- out_grad: float32 [512, 512], replicated
- norm2_grad: float32 [512], replicated
- up_grad: float32 [512, 2048], replicated
- down_grad: float32 [2048, 512], replicated
The draws below stay inside these ranges and needn't reach their ends.
Inputs may be any that keep to these rules, and one draw needn't show every extreme that they name: `doc_start`: every row begins with 1. One row of all 4, drawn from the seed, holds a single document of the whole row; the other rows hold documents of mean length about 1024.
All inputs are finite; a program needn't handle non-finite values.
Results may differ from the reference program's by a relative error of at most 0.012.
The reference program's roundings to bfloat16 on the way count: a program that leaves them out, or rounds other values in their place, can miss the bound.
Values sent between devices are 32-bit elements; how exact they have to be, the bound alone decides.
No kernel may reach another device: no remote copies, remote signals or barrier semaphores. Data moves between devices by JAX's collectives and lax.ppermute only.
A program may use at most 192 MiB of HBM per device.

```python
import jax
import jax.numpy as jnp
from jax import lax

D = 512
H = 8
HD = 64
M = 256
FF = 2048
CH = 128
DOC_SPAN = 1024
SEQ_LEN = 1024
ROWS_ALL = 4
N_DP = 4
N_SEQ = 8


def draw_doc_start(key, part):
    key_long = jax.random.fold_in(key, 11)
    key_marks = jax.random.fold_in(key, 23)
    chosen = jax.random.randint(key_long, (), 0, ROWS_ALL)
    marks = jax.random.randint(key_marks, (ROWS_ALL, SEQ_LEN), 0, DOC_SPAN)
    position = jnp.arange(SEQ_LEN, dtype=jnp.int32)[None, :]
    at_front = (position == 0).astype(jnp.int32)
    starts = jnp.maximum((marks == 0).astype(jnp.int32), at_front)
    row_index = jnp.arange(ROWS_ALL, dtype=jnp.int32)
    is_single = row_index == chosen
    return jnp.where(is_single[:, None], at_front, starts).astype(jnp.int32)


def levels(key, dims, shards, least, top_value):
    def one(dim, shards_of):
        steps = jax.random.uniform(jax.random.fold_in(jax.random.fold_in(key, 6), dim), (shards_of,), jnp.float32, least / len(shards), top_value / len(shards))
        return jnp.repeat(jnp.exp(steps), dims[dim] // shards_of).reshape((-1,) + (1,) * (len(dims) - dim - 1))

    level = one(*shards[0])
    for cut in shards[1:]:
        level = level * one(*cut)
    return level


def noise(own_key, dims, deviation, reach, pieces=(), held_as=jnp.bfloat16):
    factor_of = levels(own_key, dims, pieces, -0.22, 0.18) if pieces else 1.0
    values = jax.random.normal(own_key, dims, jnp.float32) * deviation * factor_of
    return jnp.minimum(jnp.maximum(values, -reach), reach).astype(held_as)


def setup_inputs(seed: int = 0) -> dict:
    key_list = jax.random.split(jax.random.key(seed), 11)
    return {
        "tokens": noise(key_list[0], (ROWS_ALL, SEQ_LEN, D), 1.0, 6.0, ((0, 4), (1, 8))),
        "doc_start": draw_doc_start(jax.random.fold_in(key_list[10], 71), 0),
        "norm1_gain": jnp.clip(1.0 + 0.18 * jax.random.normal(key_list[2], (D,), jnp.float32), 0.1, 1.9),
        "qkv_weight": noise(key_list[3], (D, 3 * D), D ** -0.5, 0.25),
        "out_weight": noise(key_list[4], (D, D), (D // 16) ** -0.5, 1.0),
        "norm2_gain": jnp.clip(1.0 + 0.18 * jax.random.normal(key_list[5], (D,), jnp.float32), 0.1, 1.9),
        "up_weight": noise(key_list[6], (D, FF), D ** -0.5, 0.25),
        "down_weight": noise(key_list[7], (FF, D), FF ** -0.5, 0.125),
        "omega": noise(key_list[8], (H, HD, M), 1.0, 6.0, (), jnp.float32),
        "cotangent": noise(key_list[9], (ROWS_ALL, SEQ_LEN, D), 1.0, 6.0, ((0, 4), (1, 8))),
    }


@jax.custom_vjp
def low(v):
    return lax.optimization_barrier(v.astype(jnp.bfloat16)).astype(jnp.float32)

@jax.custom_vjp
def low_back(v):
    return v

def low_keep(v):
    return (low(v), None)

def low_pass(kept, grad):
    return (grad,)

def back_keep(v):
    return (v, None)

def back_low(kept, grad):
    return (low(grad),)
low.defvjp(low_keep, low_pass)
low_back.defvjp(back_keep, back_low)
norm_eps = 1e-05
highest_precision = lax.Precision.HIGHEST

def layer_norm(values, gain):
    average = lax.optimization_barrier(jnp.mean(values, axis=-1, keepdims=True))
    centred = values - average
    spread_sq = lax.optimization_barrier(jnp.mean(centred * centred, axis=-1, keepdims=True))
    return centred * lax.rsqrt(spread_sq + norm_eps) * gain

def features(head_values, omega):
    width_dim = head_values.shape[-1]
    scaled = head_values * width_dim ** (-0.25)
    projection = jnp.einsum('...hd,hdm->...hm', scaled, omega, precision=highest_precision)
    half_square = 0.5 * lax.optimization_barrier(jnp.sum(scaled * scaled, axis=-1, keepdims=True))
    return jnp.exp(projection - half_square)

def exact_gelu(values):
    return jax.nn.gelu(values, approximate=False)

def block_attention(query_heads, key_heads, value_heads, omega, starts):
    block_count = query_heads.shape[0] // CH
    query_blocks = query_heads.reshape(block_count, CH, H, HD)
    key_blocks = key_heads.reshape(block_count, CH, H, HD)
    value_blocks = value_heads.reshape(block_count, CH, H, HD)
    start_blocks = starts.reshape(block_count, CH)

    def block_step(carry, block):
        running_state, carry_norm = carry
        query_block, key_block, value_tile_block, start_block = block
        query_features = features(query_block, omega)
        key_feat = features(key_block, omega)
        doc_index = jnp.cumsum(start_block).astype(jnp.int32)
        position = jnp.arange(CH, dtype=jnp.int32)
        same_doc = ((doc_index[:, None] == doc_index[None, :]) & (position[:, None] >= position[None, :])).astype(jnp.float32)
        leading_document = (doc_index == 0).astype(jnp.float32)
        last_doc = (doc_index == doc_index[-1]).astype(jnp.float32)
        document_marker = (doc_index[-1] > 0).astype(jnp.float32)
        scores = jnp.einsum('ihm,jhm->hij', query_features, key_feat, precision=highest_precision) * same_doc[None]
        attention_numerator = jnp.einsum('hij,jhd->ihd', scores, value_tile_block, precision=highest_precision)
        attention_numerator = attention_numerator + leading_document[:, None, None] * jnp.einsum('gfv,fvj->gfj', query_features, running_state, precision=highest_precision)
        denominator = jnp.transpose(lax.optimization_barrier(jnp.sum(scores, axis=-1)))
        denominator = denominator + leading_document[:, None] * jnp.einsum('ihm,hm->ih', query_features, carry_norm, precision=highest_precision)
        key_masked_rows = key_feat * last_doc[:, None, None]
        updated_state = jnp.einsum('iqy,iqu->qyu', key_masked_rows, value_tile_block, precision=highest_precision) + (1.0 - document_marker) * running_state
        new_norm = lax.optimization_barrier(jnp.sum(key_masked_rows, axis=0)) + (1.0 - document_marker) * carry_norm
        return ((updated_state, new_norm), attention_numerator / denominator[:, :, None])
    initial = (jnp.zeros((H, M, HD), jnp.float32), jnp.zeros((H, M), jnp.float32))
    unused, mixed = lax.scan(jax.checkpoint(block_step), initial, (query_blocks, key_blocks, value_blocks, start_blocks))
    return mixed.reshape(SEQ_LEN, D)

def row_forward(stream, starts, omega, norm1_gain, qkv_weight, out_weight, norm2_gain, up_weight, down_weight):
    normed_one = layer_norm(stream, norm1_gain)
    projected = low_back(jnp.dot(low(normed_one), qkv_weight, preferred_element_type=jnp.float32, precision=highest_precision))
    head_split = projected.reshape(SEQ_LEN, 3, H, HD)
    mixed = block_attention(head_split[:, 0], head_split[:, 1], head_split[:, 2], omega, starts)
    branch = low_back(jnp.dot(low(mixed), out_weight, preferred_element_type=jnp.float32, precision=highest_precision))
    middle = stream + branch
    normed_two = layer_norm(middle, norm2_gain)
    up_values = low_back(jnp.dot(low(normed_two), up_weight, preferred_element_type=jnp.float32, precision=highest_precision))
    ffn_out = low_back(jnp.dot(low(exact_gelu(up_values)), down_weight, preferred_element_type=jnp.float32, precision=highest_precision))
    return middle + ffn_out

def reference(tokens, doc_start, norm1_gain, qkv_weight, out_weight, norm2_gain, up_weight, down_weight, omega, cotangent):
    params = (norm1_gain, qkv_weight.astype(jnp.float32), out_weight.astype(jnp.float32), norm2_gain, up_weight.astype(jnp.float32), down_weight.astype(jnp.float32))

    def one_row(totals, row_data):
        row_tokens, row_starts, row_cot = row_data

        def forward(stream, gain_one, w_qkv, w_out, gain_two, w_up, w_down):
            return row_forward(stream, row_starts, omega, gain_one, w_qkv, w_out, gain_two, w_up, w_down)
        result, backward = jax.vjp(forward, row_tokens.astype(jnp.float32), *params)
        grads = backward(row_cot.astype(jnp.float32))
        totals = tuple((total + grad for total, grad in zip(totals, grads[1:])))
        return (totals, (result.astype(jnp.bfloat16), grads[0]))
    initial = tuple((jnp.zeros_like(param) for param in params))
    totals, (output, tokens_grad) = lax.scan(one_row, initial, (tokens, doc_start, cotangent))
    device_count = N_DP * N_SEQ
    return (output, tokens_grad, totals[0] / device_count, totals[1] / device_count, totals[2] / device_count, totals[3] / device_count, totals[4] / device_count, totals[5] / device_count)
```

```python
import functools

import jax
import jax.numpy as jnp
from jax import lax
from jax.experimental import pallas as pl
from jax.experimental.pallas import tpu as pltpu
from jax.sharding import PartitionSpec as P

norm_eps = 1e-05
highest_precision = lax.Precision.HIGHEST


def entering(value, axis, join, neutral, backward):
    count, mine = (lax.axis_size(axis), lax.axis_index(axis))
    pieces = jax.tree.map(lambda part: lax.all_gather(part, axis), value)
    if backward:
        pieces = jax.tree.map(lambda part: part[::-1], pieces)
        mine = count - 1 - mine
    running = jax.tree.map(
        lambda part, zero: jnp.full_like(part, 0) + jnp.asarray(zero, part.dtype), value, neutral
    )

    def hop(position, running):
        longer = join(running, jax.tree.map(lambda part: part[position], pieces))
        return jax.tree.map(lambda new, old: jnp.where(position < mine, new, old), longer, running)

    return lax.fori_loop(0, count - 1, hop, running)


def layer_norm(values, gain):
    average = jnp.mean(values, axis=-1, keepdims=True)
    centred = values - average
    spread_sq = jnp.mean(centred * centred, axis=-1, keepdims=True)
    return centred * lax.rsqrt(spread_sq + norm_eps) * gain


def features(head_values, omega):
    width_dim = head_values.shape[-1]
    scaled = head_values * width_dim ** (-0.25)
    projection = jnp.einsum("...hd,hdm->...hm", scaled, omega, precision=highest_precision)
    half_square = 0.5 * jnp.sum(scaled * scaled, axis=-1, keepdims=True)
    return jnp.exp(projection - half_square)


def exact_gelu(values):
    return jax.nn.gelu(values, approximate=False)


def row_masks(doc_start):
    stretch_len = doc_start.shape[1]
    doc_index = jnp.cumsum(doc_start, axis=1)
    position = jnp.arange(stretch_len, dtype=jnp.int32)
    same_doc = (doc_index[:, :, None] == doc_index[:, None, :]) & (
        position[None, :, None] >= position[None, None, :]
    )
    leading_document = (doc_index == 0).astype(jnp.float32)
    last_doc = (doc_index == doc_index[:, -1:]).astype(jnp.float32)
    document_marker = (doc_index[:, -1] > 0).astype(jnp.float32)
    return (same_doc.astype(jnp.float32), leading_document, last_doc, document_marker)


def mix_rows(
    query_features, key_feat, value_heads, running_state, carry_norm, same_doc, leading_document
):
    scores = (
        jnp.einsum("rihm,rjhm->rhij", query_features, key_feat, precision=highest_precision)
        * same_doc[:, None]
    )
    attention_numerator = jnp.einsum(
        "rhij,rjhd->rihd", scores, value_heads, precision=highest_precision
    )
    attention_numerator = attention_numerator + leading_document[:, :, None, None] * jnp.einsum(
        "rihm,rhmd->rihd", query_features, running_state, precision=highest_precision
    )
    denominator = jnp.transpose(jnp.sum(scores, axis=-1), (0, 2, 1))
    denominator = denominator + leading_document[:, :, None] * jnp.einsum(
        "rihm,rhm->rih", query_features, carry_norm, precision=highest_precision
    )
    return attention_numerator / denominator[..., None]


def stretch_totals(key_feat, value_heads, last_doc):
    key_masked_rows = key_feat * last_doc[:, :, None, None]
    state_sum = jnp.einsum(
        "rchm,rchd->rhmd", key_masked_rows, value_heads, precision=highest_precision
    )
    return (state_sum, jnp.sum(key_masked_rows, axis=1))


def carry_on(earlier, later):
    state_sum, norm_sum, document_marker = later
    pass_on = 1.0 - document_marker
    return (
        state_sum + pass_on[:, None, None, None] * earlier[0],
        norm_sum + pass_on[:, None, None] * earlier[1],
        jnp.maximum(earlier[2], document_marker),
    )


def local(
    tokens,
    doc_start,
    norm1_gain,
    qkv_weight,
    out_weight,
    norm2_gain,
    up_weight,
    down_weight,
    omega,
    cotangent,
):
    row_count, stretch_len, model_width = tokens.shape
    head_count = omega.shape[0]
    head_dim = omega.shape[1]
    token_count = row_count * stretch_len
    stream = tokens.astype(jnp.float32).reshape(token_count, model_width)
    same_doc, leading_document, last_doc, document_marker = row_masks(doc_start)
    normed_one, norm1_back = jax.vjp(layer_norm, stream, norm1_gain)
    normed_one_low = normed_one.astype(jnp.bfloat16)
    projected = jnp.dot(normed_one_low, qkv_weight, preferred_element_type=jnp.float32)
    head_split = projected.reshape(row_count, stretch_len, 3, head_count, head_dim)
    query_heads = head_split[:, :, 0]
    key_heads = head_split[:, :, 1]
    value_heads = head_split[:, :, 2]

    def both_features(query_part, key_part):
        return (features(query_part, omega), features(key_part, omega))

    (query_features, key_feat), feature_back = jax.vjp(both_features, query_heads, key_heads)

    def local_totals(key_part, value_part):
        return stretch_totals(key_part, value_part, last_doc)

    (state_sum, norm_sum), totals_back = jax.vjp(local_totals, key_feat, value_heads)
    empty_state = jnp.zeros_like(state_sum)
    empty_norm = jnp.zeros_like(norm_sum)
    empty_flag = jnp.zeros_like(document_marker)
    running_state, carry_norm, unused_flag = entering(
        (state_sum, norm_sum, document_marker),
        "seq",
        carry_on,
        (empty_state, empty_norm, empty_flag),
        False,
    )

    def local_mix(query_part, key_part, value_part, state_part, norm_part):
        return mix_rows(
            query_part, key_part, value_part, state_part, norm_part, same_doc, leading_document
        )

    mixed, mix_back = jax.vjp(
        local_mix, query_features, key_feat, value_heads, running_state, carry_norm
    )
    mixed_low = mixed.reshape(token_count, model_width).astype(jnp.bfloat16)
    branch = jnp.dot(mixed_low, out_weight, preferred_element_type=jnp.float32)
    middle = stream + branch
    normed_two, norm2_back = jax.vjp(layer_norm, middle, norm2_gain)
    normed_two_low = normed_two.astype(jnp.bfloat16)
    up_values = jnp.dot(normed_two_low, up_weight, preferred_element_type=jnp.float32)
    gelu_out, gelu_back = jax.vjp(exact_gelu, up_values)
    hidden = gelu_out.astype(jnp.bfloat16)
    ffn_out = jnp.dot(hidden, down_weight, preferred_element_type=jnp.float32)
    output = (middle + ffn_out).astype(jnp.bfloat16).reshape(row_count, stretch_len, model_width)
    incoming = cotangent.reshape(token_count, model_width)
    down_grad = jnp.einsum("tf,td->fd", hidden, incoming, preferred_element_type=jnp.float32)
    hidden_grad = jnp.einsum("td,fd->tf", incoming, down_weight, preferred_element_type=jnp.float32)
    (up_full,) = gelu_back(hidden_grad)
    up_grad_low = up_full.astype(jnp.bfloat16)
    up_grad = jnp.einsum(
        "td,tf->df", normed_two_low, up_grad_low, preferred_element_type=jnp.float32
    )
    normed_two_grad = jnp.einsum(
        "tf,df->td", up_grad_low, up_weight, preferred_element_type=jnp.float32
    )
    middle_part, norm2_grad = norm2_back(normed_two_grad)
    middle_grad = incoming.astype(jnp.float32) + middle_part
    middle_low = middle_grad.astype(jnp.bfloat16)
    out_grad = jnp.einsum("td,te->de", mixed_low, middle_low, preferred_element_type=jnp.float32)
    mixed_grad = jnp.einsum("te,de->td", middle_low, out_weight, preferred_element_type=jnp.float32)
    mixed_grad = mixed_grad.reshape(row_count, stretch_len, head_count, head_dim)
    query_feat_grad, key_feat_mix, value_mix, carry_state_grad, carry_norm_grad = mix_back(
        mixed_grad
    )
    later_state, later_norm, unused_later = entering(
        (carry_state_grad, carry_norm_grad, document_marker),
        "seq",
        carry_on,
        (empty_state, empty_norm, empty_flag),
        True,
    )
    key_feat_tot, value_tot = totals_back((later_state, later_norm))
    query_grad, key_grad = feature_back((query_feat_grad, key_feat_mix + key_feat_tot))
    value_grad = value_mix + value_tot
    projected_grad = jnp.stack((query_grad, key_grad, value_grad), axis=2)
    projected_grad = projected_grad.reshape(token_count, 3 * model_width).astype(jnp.bfloat16)
    qkv_grad = jnp.einsum(
        "td,te->de", normed_one_low, projected_grad, preferred_element_type=jnp.float32
    )
    normed_one_grad = jnp.einsum(
        "te,de->td", projected_grad, qkv_weight, preferred_element_type=jnp.float32
    )
    stream_part, norm1_grad = norm1_back(normed_one_grad)
    tokens_grad = (middle_grad + stream_part).reshape(row_count, stretch_len, model_width)
    device_count = lax.axis_size("dp") * lax.axis_size("seq")
    qkv_sum, out_sum, up_sum, down_sum, norm1_sum, norm2_sum = lax.psum(
        (qkv_grad, out_grad, up_grad, down_grad, norm1_grad, norm2_grad), ("dp", "seq")
    )
    return (
        output,
        tokens_grad,
        norm1_sum / device_count,
        qkv_sum / device_count,
        out_sum / device_count,
        norm2_sum / device_count,
        up_sum / device_count,
        down_sum / device_count,
    )


eps = 1e-05
f32 = jnp.float32
bf16 = jnp.bfloat16
AXES = ("dp", "seq")
GRID_DP, GRID_SEQ = 4, 8
ROOM = 56 * 2**20


def place(y, x, z, c):
    return (y * 2 + x) * GRID_SEQ + z * 2 + c


def pairs(move):
    return [
        (place(y, x, z, c), place(*move(y, x, z, c)))
        for y in range(2)
        for x in range(2)
        for z in range(4)
        for c in range(2)
    ]


ALONG_Z = {k: pairs(lambda y, x, z, c, k=k: (y, x, z ^ k, c)) for k in (1, 2, 3)}
CORES = pairs(lambda y, x, z, c: (y, x, z, 1 - c))
FIRST = pairs(lambda y, x, z, c: (y, 1 - x, z, c) if c == 0 else (1 - y, x, z, c))
SECOND = pairs(lambda y, x, z, c: (1 - y, x, z, c) if c == 0 else (y, 1 - x, z, c))


def send(value, perm):
    return lax.ppermute(value, AXES, perm)


def nn(a, b, precision=None):
    return lax.dot_general(
        a, b, (((1,), (0,)), ((), ())), precision=precision, preferred_element_type=f32
    )


def nt(a, b, precision=None):
    return lax.dot_general(
        a, b, (((1,), (1,)), ((), ())), precision=precision, preferred_element_type=f32
    )


def work(micros):
    return pl.CostEstimate(flops=int(micros * 1e9), bytes_accessed=0, transcendentals=0)


def kernel_call(body, outs, ids, args, scratch=(), name=None, micros=2):
    vmem = pl.BlockSpec(memory_space=pltpu.VMEM)
    return pl.pallas_call(
        body,
        out_shape=[jax.ShapeDtypeStruct(s, d) for s, d in outs],
        in_specs=[pl.BlockSpec(memory_space=pltpu.SMEM)] + [vmem] * len(args),
        out_specs=[vmem] * len(outs),
        scratch_shapes=list(scratch),
        compiler_params=pltpu.CompilerParams(vmem_limit_bytes=ROOM),
        name=name,
        cost_estimate=work(micros),
    )(ids, *args)


def normalise(v):
    mean = jnp.mean(v, axis=-1, keepdims=True)
    centred = v - mean
    inv = lax.rsqrt(jnp.mean(centred * centred, axis=-1, keepdims=True) + eps)
    return centred * inv, inv


def normalise_back(e, n, inv):
    return (e - jnp.mean(e, axis=-1, keepdims=True) - n * jnp.mean(e * n, axis=-1, keepdims=True)) * inv


def doc_numbers(doc):
    at = lax.broadcasted_iota(jnp.int32, (128, 128), 0)
    to = lax.broadcasted_iota(jnp.int32, (128, 128), 1)
    upper = (at <= to).astype(f32)
    a8 = lax.broadcasted_iota(jnp.int32, (8, 8), 0)
    t8 = lax.broadcasted_iota(jnp.int32, (8, 8), 1)
    before = (t8 < a8).astype(f32)
    spread = jnp.broadcast_to(jnp.sum(doc, axis=1, keepdims=True), (8, 128))
    high = lax.Precision.HIGHEST
    rows = nn(doc, upper, high) + nn(before, spread, high)
    eye = (at == to).astype(f32)
    cols = nt(eye, rows, high)
    return rows, cols


def row_of(rows, lo, hi):
    return jnp.concatenate([rows[j : j + 1, :] for j in range(lo, hi)], axis=1)


def col_of(cols, lo, hi):
    return jnp.concatenate([cols[:, j : j + 1] for j in range(lo, hi)], axis=0)


def gelu_parts(u):
    e = jnp.exp(-0.5 * u * u)
    base = 1.0 + (0.3275911 * 0.7071067811865476) * jnp.abs(u)
    t = pl.reciprocal(base, approx=True)
    t = t * (2.0 - base * t)
    tail = t * (
        0.5 * 0.254829592
        + t * (-0.5 * 0.284496736 + t * (0.5 * 1.421413741 + t * (-0.5 * 1.453152027 + t * (0.5 * 1.061405429))))
    ) * e
    return jnp.where(u < 0, tail, 1.0 - tail), e * 0.3989422804014327


def head_forward(ids, t0, t1, t2, t3, p0, p1, p2, p3, gain, wh, omega,
                 keep, give, phq_o, phk_o, qk_o, v_o, mxd_o, doc_o, nt_o, low):
    z, c = ids[0], ids[1]
    g = gain[...]
    for k, (mine, theirs) in enumerate(((t0, p0), (t1, p1), (t2, p2), (t3, p3))):
        for ref, core in ((mine, c), (theirs, 1 - c)):
            chunk = 2 * jnp.bitwise_xor(z, k) + core
            n, _ = normalise(ref[0:128, :])
            low[pl.ds(pl.multiple_of(chunk * 128, 128), 128), :] = (n * g).astype(bf16)
            doc_o[pl.ds(chunk, 1), :] = ref[128:129, 0:128]
    rows, cols = doc_numbers(doc_o[...])
    nt_o[...] = jnp.transpose(low[:, pl.ds(pl.multiple_of(c * 256, 256), 256)])
    s = 64 ** -0.25
    om = omega[...]
    oh = om.astype(bf16)
    ol = (om - oh.astype(f32)).astype(bf16)
    stack = jnp.concatenate([oh, oh, ol], axis=0)

    def feature(v):
        v = v * s
        hi = v.astype(bf16)
        lo = (v - hi.astype(f32)).astype(bf16)
        proj = nn(jnp.concatenate([hi, lo, hi], axis=1), stack)
        return jnp.exp(proj - 0.5 * jnp.sum(v * v, axis=-1, keepdims=True))

    for b in range(4):
        at = pl.ds(256 * b, 256)
        pr = nn(low[at, :], wh[...])
        qk_o[at, :] = pr[:, 0:128]
        v_o[at, :] = pr[:, 128:192].astype(bf16)
        phq_o[at, :] = feature(pr[:, 0:64]).astype(bf16)
        phk_o[at, :] = feature(pr[:, 64:128]).astype(bf16)
    for b in range(4):
        at = pl.ds(256 * b, 256)
        n = 256 * (b + 1)
        scores = nt(phq_o[at, :], phk_o[0:n, :])
        i = lax.broadcasted_iota(jnp.int32, (256, n), 0) + 256 * b
        j = lax.broadcasted_iota(jnp.int32, (256, n), 1)
        same = (col_of(cols, 2 * b, 2 * b + 2) == row_of(rows, 0, 2 * b + 2)) & (i >= j)
        scores = jnp.where(same, scores, 0.0)
        inv = 1.0 / jnp.sum(scores, axis=-1, keepdims=True)
        mixed = nn(scores.astype(bf16), v_o[0:n, :]) * inv
        mxd_o[at, :] = jnp.concatenate([mixed, jnp.broadcast_to(inv, (256, 64))], axis=1)
        top, bottom = mixed[0:128, :], mixed[128:256, :]
        keep[b] = jnp.where(c == 0, top, bottom)
        give[b] = jnp.where(c == 0, bottom, top)


def pack_pairs(ids, keep, got, b0, b1, b2, b3):
    z, c = ids[0], ids[1]
    for k, out in enumerate((b0, b1, b2, b3)):
        j = jnp.bitwise_xor(z, k)
        a, b = keep[j], got[j]
        out[...] = jnp.where(c == 0, jnp.concatenate([a, b], axis=1), jnp.concatenate([b, a], axis=1))


def unpack_pairs(ids, b0, b1, b2, b3, keep, give):
    z, c = ids[0], ids[1]
    for k, ref in enumerate((b0, b1, b2, b3)):
        j = jnp.bitwise_xor(z, k)
        a, b = ref[:, 0:64], ref[:, 64:128]
        keep[j] = jnp.where(c == 0, a, b)
        give[j] = jnp.where(c == 0, b, a)


def middle_part(ids, b0, b1, b2, b3, tokens, wo, gain, mixed_o, middle_o, normed_o):
    z = ids[0]
    for k, ref in enumerate((b0, b1, b2, b3)):
        j = jnp.bitwise_xor(z, k)
        mixed_o[:, pl.ds(pl.multiple_of(j * 128, 128), 128)] = ref[...].astype(bf16)
    middle = tokens[...].astype(f32) + nn(mixed_o[...], wo[...])
    middle_o[...] = middle
    n, _ = normalise(middle)
    normed_o[...] = (n * gain[...]).astype(bf16).astype(f32)


def feed_forward(ids, mixed, middle, normed, cot, wu, wd, wo, gain,
                 out_o, mg_o, ml_o, ex_o, b0, b1, b2, b3, scr):
    z, c = ids[0], ids[1]
    x = normed[...].astype(bf16)
    inc = cot[...]
    total = middle[...]
    back = jnp.zeros((128, 512), f32)
    for u in range(4):
        at = pl.ds(512 * u, 512)
        wub, wdb = wu[:, at], wd[at, :]
        up = nn(x, wub)
        cdf, pdf = gelu_parts(up)
        total = total + nn((up * cdf).astype(bf16), wdb)
        ug = ((cdf + up * pdf) * nt(inc, wdb)).astype(bf16)
        back = back + nt(ug, wub)
    out_o[...] = total.astype(bf16)
    n, inv = normalise(middle[...])
    mg = inc.astype(f32) + normalise_back(gain[...] * back, n, inv)
    mg_o[...] = mg
    low = mg.astype(bf16)
    ml_o[...] = low
    ex_o[:, 0:256] = mixed[:, pl.ds(pl.multiple_of((1 - c) * 256, 256), 256)].astype(f32)
    ex_o[:, 256:768] = low.astype(f32)
    scr[...] = nt(low, wo[...])
    for k, ref in enumerate((b0, b1, b2, b3)):
        j = jnp.bitwise_xor(z, k)
        ref[...] = scr[:, pl.ds(pl.multiple_of(j * 128, 128), 128)]


def out_part(ids, mixed, mlow, got, keep, give, scr):
    c, first = ids[1], ids[2]
    mine = mixed[:, pl.ds(pl.multiple_of(c * 256, 256), 256)].astype(f32)
    left = jnp.transpose(jnp.concatenate([mine, got[:, 0:256]], axis=0)).astype(bf16)
    right = jnp.concatenate([mlow[...], got[:, 256:768].astype(bf16)], axis=0)
    scr[...] = nn(left, right)
    keep[...] = scr[pl.ds(pl.multiple_of(first * 128, 128), 128), :]
    give[...] = scr[pl.ds(pl.multiple_of((1 - first) * 128, 128), 128), :]


def add_spread(ids, mine, got, o0, o1, o2, o3, scr):
    scr[...] = mine[...] + got[...]
    for k, ref in enumerate((o0, o1, o2, o3)):
        j = jnp.bitwise_xor(ids[0], k)
        ref[...] = scr[:, pl.ds(pl.multiple_of(j * 128, 128), 128)]


def add_last(ids, mine, got, o0, o1, o2, o3, out):
    out[:, 0:384] = (mine[...] + got[...]) * (1.0 / 32)
    out[:, 384:512] = ((o0[...] + o1[...]) + (o2[...] + o3[...])) * (1.0 / 32)


def head_backward(ids, keep, got, phq, phk, qk, v, mxd, doc, omega, pg_o, r_scr, m_scr):
    c = ids[1]
    for b in range(4):
        a, g = keep[b], got[b]
        at = pl.ds(256 * b, 256)
        dm = jnp.concatenate([jnp.where(c == 0, a, g), jnp.where(c == 0, g, a)], axis=0)
        r = dm * mxd[at, 64:128]
        r_scr[at, :] = r.astype(bf16)
        m_scr[at, :] = r * mxd[at, 0:64]
    rows, cols = doc_numbers(doc[...])
    ones = jnp.ones((8, 64), f32)
    s = 64 ** -0.25
    om = omega[...].astype(bf16)

    def feature_back(ph, grad, base):
        a = ph.astype(f32) * grad
        return s * nt(a.astype(bf16), om) - (s * s) * base * jnp.sum(a, axis=-1, keepdims=True)

    for b in range(4):
        at = pl.ds(256 * b, 256)
        n = 256 * (b + 1)
        i = lax.broadcasted_iota(jnp.int32, (256, n), 0) + 256 * b
        j = lax.broadcasted_iota(jnp.int32, (256, n), 1)
        same = (col_of(cols, 2 * b, 2 * b + 2) == row_of(rows, 0, 2 * b + 2)) & (i >= j)
        ds = nt(r_scr[at, :], v[0:n, :]) - jnp.sum(m_scr[at, :], axis=-1, keepdims=True)
        ds = jnp.where(same, ds, 0.0).astype(bf16)
        qg = feature_back(phq[at, :], nn(ds, phk[0:n, :]), qk[at, 0:64])
        m = 1024 - 256 * b
        later = pl.ds(256 * b, m)
        j2 = lax.broadcasted_iota(jnp.int32, (256, m), 0)
        i2 = lax.broadcasted_iota(jnp.int32, (256, m), 1)
        same2 = (col_of(cols, 2 * b, 2 * b + 2) == row_of(rows, 2 * b, 8)) & (i2 >= j2)
        scores = jnp.where(same2, nt(phk[at, :], phq[later, :]), 0.0).astype(bf16)
        vg = nn(scores, r_scr[later, :])
        mr = nt(ones, m_scr[later, :], lax.Precision.HIGHEST)[0:1, :]
        ds2 = jnp.where(same2, nt(v[at, :], r_scr[later, :]) - mr, 0.0).astype(bf16)
        kg = feature_back(phk[at, :], nn(ds2, phq[later, :]), qk[at, 64:128])
        rnd = lambda t: t.astype(bf16).astype(f32)
        pg_o[at, :] = rnd(jnp.concatenate([qg, kg], axis=1))
        pg_o[pl.ds(1024 + 256 * (b % 2), 256), 64 * (b // 2) : 64 * (b // 2) + 64] = rnd(vg)


def weight_part(ids, mine, theirs, nt_low, q0, q1, q2, q3, keep, give, scr, g_scr):
    z, c, first = ids[0], ids[1], ids[2]
    for b in range(4):
        at = pl.ds(256 * b, 256)
        va = pl.ds(1024 + 256 * (b % 2), 256)
        lanes = slice(64 * (b // 2), 64 * (b // 2) + 64)
        a, t = mine[at, :], theirs[at, :]
        av, tv = mine[va, lanes], theirs[va, lanes]
        h0 = jnp.where(c == 0, a, t)
        h1 = jnp.where(c == 0, t, a)
        scr[at, 0:128] = jnp.concatenate([h0[:, 0:64], h1[:, 0:64]], axis=1)
        scr[at, 128:256] = jnp.concatenate([h0[:, 64:128], h1[:, 64:128]], axis=1)
        scr[at, 256:384] = jnp.concatenate([jnp.where(c == 0, av, tv), jnp.where(c == 0, tv, av)], axis=1)
    for k, ref in enumerate((q0, q1, q2, q3)):
        chunk = 2 * jnp.bitwise_xor(z, k) + c
        ref[...] = scr[pl.ds(pl.multiple_of(chunk * 128, 128), 128), :]
    g_scr[...] = nn(nt_low[...], scr[...].astype(bf16))
    keep[...] = g_scr[pl.ds(pl.multiple_of(first * 128, 128), 128), :]
    give[...] = g_scr[pl.ds(pl.multiple_of((1 - first) * 128, 128), 128), :]


def tokens_part(ids, q0, q1, q2, q3, mg, tokens, w, gain, out_o, scr):
    z = ids[0]
    for k, ref in enumerate((q0, q1, q2, q3)):
        j = jnp.bitwise_xor(z, k)
        for part in range(3):
            scr[:, pl.ds(pl.multiple_of(part * 512 + j * 128, 128), 128)] = ref[:, 128 * part : 128 * part + 128].astype(bf16)
    n, inv = normalise(tokens[...].astype(f32))
    e = gain[...] * nt(scr[...], w[...])
    out_o[...] = mg[...] + normalise_back(e, n, inv)


def add_split(ids, mine, got, keep, give):
    second = ids[3]
    a = pl.ds(pl.multiple_of(second * 64, 64), 64)
    b = pl.ds(pl.multiple_of((1 - second) * 64, 64), 64)
    keep[...] = mine[a, :] + got[a, :]
    give[...] = mine[b, :] + got[b, :]


def ffn_weights(count, first, last, ids, *refs):
    xs, cs = refs[:count], refs[count : 2 * count]
    wut, wd = refs[2 * count : 2 * count + 2]
    rest = refs[2 * count + 2 :]
    if not first:
        up_in, down_in, rest = rest[0], rest[1], rest[2:]
    if last:
        up_o, down_o, gain_o, xb, cb = rest
    else:
        up_o, down_o, xb, cb = rest
    step = pl.program_id(0)

    @pl.when(step == 0)
    def _():
        at = 0
        for x, cc in zip(xs, cs):
            for i in range(x.shape[0]):
                xb[pl.ds(at, 128), :] = x[i].astype(bf16)
                cb[pl.ds(at, 128), :] = cc[i].astype(bf16)
                at += 128

    total_up = None
    size = 512
    for blk in range(xb.shape[0] // size):
        at = pl.ds(blk * size, size)
        x, inc = xb[at, :], cb[at, :]
        up = nt(wut[...], x)
        hg = nt(wd[...], inc)
        cdf, pdf = gelu_parts(up)
        du = nn(((cdf + up * pdf) * hg).astype(bf16), x)
        dd = nn((up * cdf).astype(bf16), inc)
        total_up = du if total_up is None else total_up + du
        total_down = dd if blk == 0 else total_down + dd
    if not first:
        total_up = total_up + up_in[...]
        total_down = total_down + down_in[...]
    if last:
        total_up = total_up * (1.0 / 32)
        up_o[...] = jnp.transpose(total_up)
        down_o[...] = total_down * (1.0 / 32)
        part = jnp.sum(total_up * wut[...].astype(f32), axis=0, keepdims=True)

        @pl.when(step == 0)
        def _():
            gain_o[...] = jnp.zeros((8, 512), f32)

        gain_o[0:1, :] = gain_o[0:1, :] + part
    else:
        up_o[...] = total_up
        down_o[...] = total_down


def ffn_call(ids, xs, cs, wut, wd, carried, last):
    count, first = len(xs), carried is None
    tokens = count * 256
    pair = lambda v: pl.BlockSpec((2, 128, 512), lambda i, ids, at=v[1]: (at, 0, 0))
    block = pl.BlockSpec((256, 512), lambda i, ids: (i, 0))
    in_specs = [pair(v) for v in xs] + [pair(v) for v in cs] + [block, block]
    args = [v[0] for v in xs] + [v[0] for v in cs] + [wut, wd]
    if not first:
        in_specs += [block, block]
        args += list(carried)
    out_specs, out_shapes = [block, block], [(1024, 512), (1024, 512)]
    if last:
        out_specs = [
            pl.BlockSpec((512, 256), lambda i, ids: (0, i + 4 * ids[1])),
            pl.BlockSpec((256, 512), lambda i, ids: (i + 4 * ids[1], 0)),
            pl.BlockSpec((8, 512), lambda i, ids: (0, 0)),
        ]
        out_shapes = [(512, 2048), (2048, 512), (8, 512)]
    return pl.pallas_call(
        functools.partial(ffn_weights, count, first, last),
        grid_spec=pltpu.PrefetchScalarGridSpec(
            num_scalar_prefetch=1,
            grid=(4,),
            in_specs=in_specs,
            out_specs=out_specs,
            scratch_shapes=[pltpu.VMEM((tokens, 512), bf16), pltpu.VMEM((tokens, 512), bf16)],
        ),
        out_shape=[jax.ShapeDtypeStruct(shape, f32) for shape in out_shapes],
        compiler_params=pltpu.CompilerParams(vmem_limit_bytes=ROOM),
        name="ffn_weights",
        cost_estimate=work(tokens / 100),
    )(ids, *args)


def put_half(ids, up_in, down_in, up_any, down_any, up_o, down_o):
    up_o[...] = up_in[...]
    down_o[...] = down_in[...]


def put_halves(ids, up, down, up_full, down_full):
    up_spec = pl.BlockSpec((512, 256), lambda i, ids: (0, i + 4 - 4 * ids[1]))
    down_spec = pl.BlockSpec((256, 512), lambda i, ids: (i + 4 - 4 * ids[1], 0))
    whole = pl.BlockSpec(memory_space=pl.ANY)
    return pl.pallas_call(
        put_half,
        grid_spec=pltpu.PrefetchScalarGridSpec(
            num_scalar_prefetch=1,
            grid=(4,),
            in_specs=[pl.BlockSpec((512, 256), lambda i, ids: (0, i)), pl.BlockSpec((256, 512), lambda i, ids: (i, 0)), whole, whole],
            out_specs=[up_spec, down_spec],
        ),
        out_shape=[jax.ShapeDtypeStruct((512, 2048), f32), jax.ShapeDtypeStruct((2048, 512), f32)],
        input_output_aliases={3: 0, 4: 1},
        compiler_params=pltpu.CompilerParams(vmem_limit_bytes=ROOM),
        name="put_halves",
        cost_estimate=work(3),
    )(ids, up, down, up_full, down_full)


def gather_all(own, split):
    z1, z2, z3 = (send(own, ALONG_Z[k]) for k in (1, 2, 3))
    groups = []
    for members in ([own, z1], [z2, z3]) if split else ([own, z1, z2, z3],):
        base = jnp.stack(members)
        two = jnp.concatenate([base, send(base, FIRST)])
        other = send(two, SECOND)
        groups.append([two, other, send(two, CORES), send(other, CORES)])
    return groups


def finish(ids, a, f, ca, cf, w, gain, qkv_o, out_o, gain_o, total):
    z, c, first, second = ids[0], ids[1], ids[2], ids[3]
    for core, ref, r1, r2, flip in ((c, a, first, second, 0), (c, f, first, second, 1), (1 - c, ca, second, first, 0), (1 - c, cf, second, first, 1)):
        for n in range(2):
            row = core * 256 + jnp.bitwise_xor(r1, flip) * 128 + jnp.bitwise_xor(r2, n) * 64
            rows = pl.ds(pl.multiple_of(row, 64), 64)
            for k in range(4):
                j = jnp.bitwise_xor(z, k)
                for part in range(3):
                    at = pl.ds(pl.multiple_of(part * 512 + j * 128, 128), 128)
                    qkv_o[rows, at] = ref[4 * n + k, :, 128 * part : 128 * part + 128]
                out_o[rows, pl.ds(pl.multiple_of(j * 128, 128), 128)] = ref[4 * n + k, :, 384:512]
    for r in range(4):
        rows = pl.ds(128 * r, 128)
        acc = jnp.zeros((128, 128), f32)
        for j in range(12):
            lanes = pl.ds(128 * j, 128)
            acc = acc + w[rows, lanes].astype(f32) * qkv_o[rows, lanes]
        lanes = pl.ds(128 * r, 128)
        gain_o[0:1, lanes] = jnp.sum(jnp.transpose(acc), axis=0, keepdims=True) / gain[0:1, lanes]


def local_fast(tokens, doc_start, norm1_gain, qkv_weight, out_weight, norm2_gain, up_weight, down_weight, omega, cotangent):
    dp, seq = lax.axis_index("dp"), lax.axis_index("seq")
    y, x, z, c = dp // 2, dp % 2, seq // 2, seq % 2
    first = jnp.where(c == 0, x, y)
    second = jnp.where(c == 0, y, x)
    ids = jnp.stack([z, c, first, second]).astype(jnp.int32)
    g1, g2 = norm1_gain.reshape(1, 512), norm2_gain.reshape(1, 512)
    tok, cot = tokens[0], cotangent[0]
    marks = jnp.pad(doc_start.astype(f32), ((0, 7), (0, 384)))
    message = jnp.concatenate([tok.astype(f32), marks], axis=0)
    t = [message] + [send(message, ALONG_Z[k]) for k in (1, 2, 3)]
    p = [send(v, CORES) for v in t]
    head = seq
    wh = lax.dynamic_index_in_dim(qkv_weight.reshape(512, 3, 8, 64), head, 2, keepdims=False).reshape(512, 192)
    om = lax.dynamic_index_in_dim(omega, head, 0, keepdims=False)
    wut = jnp.transpose(lax.dynamic_slice_in_dim(up_weight, c * 1024, 1024, 1))
    wdh = lax.dynamic_slice_in_dim(down_weight, c * 1024, 1024, 0)
    keep, give, phq, phk, qk, v, mxd, doc, nt_low = kernel_call(
        head_forward,
        [((4, 128, 64), f32), ((4, 128, 64), f32), ((1024, 256), bf16), ((1024, 256), bf16), ((1024, 128), f32),
         ((1024, 64), bf16), ((1024, 128), f32), ((8, 128), f32), ((256, 1024), bf16)],
        ids, [*t, *p, g1, wh, om], [pltpu.VMEM((1024, 512), bf16)], "head_forward", 7,
    )
    block = ((128, 128), f32)
    b = kernel_call(pack_pairs, [block] * 4, ids, [keep, send(give, CORES)], name="pack_pairs")
    b = [b[0]] + [send(b[k], ALONG_Z[k]) for k in (1, 2, 3)]
    mixed, middle, normed = kernel_call(
        middle_part, [((128, 512), bf16), ((128, 512), f32), ((128, 512), f32)], ids, [*b, tok, out_weight, g2],
        name="middle_part",
    )
    (cot_group,) = gather_all(cot.astype(f32), False)
    x_groups = gather_all(normed, True)
    output, mg, mlow, ex, *b = kernel_call(
        feed_forward,
        [((128, 512), bf16), ((128, 512), f32), ((128, 512), bf16), ((128, 768), f32)] + [block] * 4,
        ids, [mixed, middle, normed, cot, up_weight, down_weight, out_weight, g2], [pltpu.VMEM((128, 512), f32)],
        "feed_forward", 7,
    )
    b = [b[0]] + [send(b[k], ALONG_Z[k]) for k in (1, 2, 3)]
    keep, give = kernel_call(unpack_pairs, [((4, 128, 64), f32)] * 2, ids, b, name="unpack_pairs")
    got = send(give, CORES)
    okeep, ogive = kernel_call(out_part, [((128, 512), f32)] * 2, ids, [mixed, mlow, send(ex, CORES)],
                             [pltpu.VMEM((256, 512), f32)], "out_part")
    okeep, ogive = kernel_call(add_split, [((64, 512), f32)] * 2, ids, [okeep, send(ogive, FIRST)], name="add_split")
    o = kernel_call(add_spread, [((64, 128), f32)] * 4, ids, [okeep, send(ogive, SECOND)],
                    [pltpu.VMEM((64, 512), f32)], "add_spread")
    o = [o[0]] + [send(o[k], ALONG_Z[k]) for k in (1, 2, 3)]
    (pg,) = kernel_call(
        head_backward, [((1536, 128), f32)], ids, [keep, got, phq, phk, qk, v, mxd, doc, om],
        [pltpu.VMEM((1024, 64), bf16), pltpu.VMEM((1024, 64), f32)], "head_backward", 9,
    )
    *q, keep, give = kernel_call(
        weight_part, [((128, 384), f32)] * 4 + [((128, 384), f32)] * 2, ids, [pg, send(pg, CORES), nt_low],
        [pltpu.VMEM((1024, 384), f32), pltpu.VMEM((256, 384), f32)], "weight_part",
    )
    keep, give = kernel_call(add_split, [((64, 384), f32)] * 2, ids, [keep, send(give, FIRST)], name="add_split")
    (piece,) = kernel_call(add_last, [((64, 512), f32)], ids, [keep, send(give, SECOND), *o], name="add_last")
    pieces = jnp.stack([piece] + [send(piece, ALONG_Z[k]) for k in (1, 2, 3)])
    q = [q[0]] + [send(q[k], ALONG_Z[k]) for k in (1, 2, 3)]
    (tokens_grad,) = kernel_call(
        tokens_part, [((128, 512), f32)], ids, [*q, mg, tok, qkv_weight, g1], [pltpu.VMEM((128, 1536), bf16)],
        "tokens_part",
    )
    carried = None
    for i, xg in enumerate(x_groups):
        xs = [(v, at) for v in xg for at in (0, 1)]
        cs = [(v, at) for v in cot_group for at in (i, 2 + i)]
        carried = ffn_call(ids, xs, cs, wut, wdh, carried, i == len(x_groups) - 1)
    up_grad, down_grad, part2 = carried
    up_half = lax.dynamic_slice_in_dim(up_grad, c * 1024, 1024, 1)
    down_half = lax.dynamic_slice_in_dim(down_grad, c * 1024, 1024, 0)
    up_grad, down_grad = put_halves(ids, send(up_half, CORES), send(down_half, CORES), up_grad, down_grad)
    norm2_grad = (part2 + send(part2, CORES))[0] / norm2_gain
    mine = jnp.concatenate([pieces, send(pieces, SECOND)])
    theirs = send(mine, FIRST)
    qkv_grad, out_grad, norm1_grad = kernel_call(
        finish, [((512, 1536), f32), ((512, 512), f32), ((1, 512), f32)], ids,
        [mine, theirs, send(mine, CORES), send(theirs, CORES), qkv_weight, g1], [pltpu.VMEM((8, 128), f32)], "finish", 5,
    )
    norm1_grad = norm1_grad[0]
    return (output[None], tokens_grad[None], norm1_grad, qkv_grad, out_grad, norm2_grad, up_grad, down_grad)


def solution(mesh):
    placed = (
        P("dp", "seq", None),
        P("dp", "seq"),
        P(),
        P(),
        P(),
        P(),
        P(),
        P(),
        P(),
        P("dp", "seq", None),
    )
    fits = mesh.shape["dp"] == GRID_DP and mesh.shape["seq"] == GRID_SEQ
    return jax.shard_map(
        local_fast if fits else local,
        mesh=mesh,
        in_specs=placed,
        out_specs=(P("dp", "seq", None), P("dp", "seq", None), P(), P(), P(), P(), P(), P()),
        check_vma=False,
    )
```

```python
import functools

import jax
import jax.numpy as jnp
from jax import lax
from jax.experimental import pallas as pl
from jax.experimental.pallas import tpu as pltpu
from jax.sharding import PartitionSpec as P

norm_eps = 1e-05
highest_precision = lax.Precision.HIGHEST


def entering(value, axis, join, neutral, backward):
    count, mine = (lax.axis_size(axis), lax.axis_index(axis))
    pieces = jax.tree.map(lambda part: lax.all_gather(part, axis), value)
    if backward:
        pieces = jax.tree.map(lambda part: part[::-1], pieces)
        mine = count - 1 - mine
    running = jax.tree.map(
        lambda part, zero: jnp.full_like(part, 0) + jnp.asarray(zero, part.dtype), value, neutral
    )

    def hop(position, running):
        longer = join(running, jax.tree.map(lambda part: part[position], pieces))
        return jax.tree.map(lambda new, old: jnp.where(position < mine, new, old), longer, running)

    return lax.fori_loop(0, count - 1, hop, running)


def layer_norm(values, gain):
    average = jnp.mean(values, axis=-1, keepdims=True)
    centred = values - average
    spread_sq = jnp.mean(centred * centred, axis=-1, keepdims=True)
    return centred * lax.rsqrt(spread_sq + norm_eps) * gain


def features(head_values, omega):
    width_dim = head_values.shape[-1]
    scaled = head_values * width_dim ** (-0.25)
    projection = jnp.einsum("...hd,hdm->...hm", scaled, omega, precision=highest_precision)
    half_square = 0.5 * jnp.sum(scaled * scaled, axis=-1, keepdims=True)
    return jnp.exp(projection - half_square)


def exact_gelu(values):
    return jax.nn.gelu(values, approximate=False)


def row_masks(doc_start):
    stretch_len = doc_start.shape[1]
    doc_index = jnp.cumsum(doc_start, axis=1)
    position = jnp.arange(stretch_len, dtype=jnp.int32)
    same_doc = (doc_index[:, :, None] == doc_index[:, None, :]) & (
        position[None, :, None] >= position[None, None, :]
    )
    leading_document = (doc_index == 0).astype(jnp.float32)
    last_doc = (doc_index == doc_index[:, -1:]).astype(jnp.float32)
    document_marker = (doc_index[:, -1] > 0).astype(jnp.float32)
    return (same_doc.astype(jnp.float32), leading_document, last_doc, document_marker)


def mix_rows(
    query_features, key_feat, value_heads, running_state, carry_norm, same_doc, leading_document
):
    scores = (
        jnp.einsum("rihm,rjhm->rhij", query_features, key_feat, precision=highest_precision)
        * same_doc[:, None]
    )
    attention_numerator = jnp.einsum(
        "rhij,rjhd->rihd", scores, value_heads, precision=highest_precision
    )
    attention_numerator = attention_numerator + leading_document[:, :, None, None] * jnp.einsum(
        "rihm,rhmd->rihd", query_features, running_state, precision=highest_precision
    )
    denominator = jnp.transpose(jnp.sum(scores, axis=-1), (0, 2, 1))
    denominator = denominator + leading_document[:, :, None] * jnp.einsum(
        "rihm,rhm->rih", query_features, carry_norm, precision=highest_precision
    )
    return attention_numerator / denominator[..., None]


def stretch_totals(key_feat, value_heads, last_doc):
    key_masked_rows = key_feat * last_doc[:, :, None, None]
    state_sum = jnp.einsum(
        "rchm,rchd->rhmd", key_masked_rows, value_heads, precision=highest_precision
    )
    return (state_sum, jnp.sum(key_masked_rows, axis=1))


def carry_on(earlier, later):
    state_sum, norm_sum, document_marker = later
    pass_on = 1.0 - document_marker
    return (
        state_sum + pass_on[:, None, None, None] * earlier[0],
        norm_sum + pass_on[:, None, None] * earlier[1],
        jnp.maximum(earlier[2], document_marker),
    )


def local(
    tokens,
    doc_start,
    norm1_gain,
    qkv_weight,
    out_weight,
    norm2_gain,
    up_weight,
    down_weight,
    omega,
    cotangent,
):
    row_count, stretch_len, model_width = tokens.shape
    head_count = omega.shape[0]
    head_dim = omega.shape[1]
    token_count = row_count * stretch_len
    stream = tokens.astype(jnp.float32).reshape(token_count, model_width)
    same_doc, leading_document, last_doc, document_marker = row_masks(doc_start)
    normed_one, norm1_back = jax.vjp(layer_norm, stream, norm1_gain)
    normed_one_low = normed_one.astype(jnp.bfloat16)
    projected = jnp.dot(normed_one_low, qkv_weight, preferred_element_type=jnp.float32)
    head_split = projected.reshape(row_count, stretch_len, 3, head_count, head_dim)
    query_heads = head_split[:, :, 0]
    key_heads = head_split[:, :, 1]
    value_heads = head_split[:, :, 2]

    def both_features(query_part, key_part):
        return (features(query_part, omega), features(key_part, omega))

    (query_features, key_feat), feature_back = jax.vjp(both_features, query_heads, key_heads)

    def local_totals(key_part, value_part):
        return stretch_totals(key_part, value_part, last_doc)

    (state_sum, norm_sum), totals_back = jax.vjp(local_totals, key_feat, value_heads)
    empty_state = jnp.zeros_like(state_sum)
    empty_norm = jnp.zeros_like(norm_sum)
    empty_flag = jnp.zeros_like(document_marker)
    running_state, carry_norm, unused_flag = entering(
        (state_sum, norm_sum, document_marker),
        "seq",
        carry_on,
        (empty_state, empty_norm, empty_flag),
        False,
    )

    def local_mix(query_part, key_part, value_part, state_part, norm_part):
        return mix_rows(
            query_part, key_part, value_part, state_part, norm_part, same_doc, leading_document
        )

    mixed, mix_back = jax.vjp(
        local_mix, query_features, key_feat, value_heads, running_state, carry_norm
    )
    mixed_low = mixed.reshape(token_count, model_width).astype(jnp.bfloat16)
    branch = jnp.dot(mixed_low, out_weight, preferred_element_type=jnp.float32)
    middle = stream + branch
    normed_two, norm2_back = jax.vjp(layer_norm, middle, norm2_gain)
    normed_two_low = normed_two.astype(jnp.bfloat16)
    up_values = jnp.dot(normed_two_low, up_weight, preferred_element_type=jnp.float32)
    gelu_out, gelu_back = jax.vjp(exact_gelu, up_values)
    hidden = gelu_out.astype(jnp.bfloat16)
    ffn_out = jnp.dot(hidden, down_weight, preferred_element_type=jnp.float32)
    output = (middle + ffn_out).astype(jnp.bfloat16).reshape(row_count, stretch_len, model_width)
    incoming = cotangent.reshape(token_count, model_width)
    down_grad = jnp.einsum("tf,td->fd", hidden, incoming, preferred_element_type=jnp.float32)
    hidden_grad = jnp.einsum("td,fd->tf", incoming, down_weight, preferred_element_type=jnp.float32)
    (up_full,) = gelu_back(hidden_grad)
    up_grad_low = up_full.astype(jnp.bfloat16)
    up_grad = jnp.einsum(
        "td,tf->df", normed_two_low, up_grad_low, preferred_element_type=jnp.float32
    )
    normed_two_grad = jnp.einsum(
        "tf,df->td", up_grad_low, up_weight, preferred_element_type=jnp.float32
    )
    middle_part, norm2_grad = norm2_back(normed_two_grad)
    middle_grad = incoming.astype(jnp.float32) + middle_part
    middle_low = middle_grad.astype(jnp.bfloat16)
    out_grad = jnp.einsum("td,te->de", mixed_low, middle_low, preferred_element_type=jnp.float32)
    mixed_grad = jnp.einsum("te,de->td", middle_low, out_weight, preferred_element_type=jnp.float32)
    mixed_grad = mixed_grad.reshape(row_count, stretch_len, head_count, head_dim)
    query_feat_grad, key_feat_mix, value_mix, carry_state_grad, carry_norm_grad = mix_back(
        mixed_grad
    )
    later_state, later_norm, unused_later = entering(
        (carry_state_grad, carry_norm_grad, document_marker),
        "seq",
        carry_on,
        (empty_state, empty_norm, empty_flag),
        True,
    )
    key_feat_tot, value_tot = totals_back((later_state, later_norm))
    query_grad, key_grad = feature_back((query_feat_grad, key_feat_mix + key_feat_tot))
    value_grad = value_mix + value_tot
    projected_grad = jnp.stack((query_grad, key_grad, value_grad), axis=2)
    projected_grad = projected_grad.reshape(token_count, 3 * model_width).astype(jnp.bfloat16)
    qkv_grad = jnp.einsum(
        "td,te->de", normed_one_low, projected_grad, preferred_element_type=jnp.float32
    )
    normed_one_grad = jnp.einsum(
        "te,de->td", projected_grad, qkv_weight, preferred_element_type=jnp.float32
    )
    stream_part, norm1_grad = norm1_back(normed_one_grad)
    tokens_grad = (middle_grad + stream_part).reshape(row_count, stretch_len, model_width)
    device_count = lax.axis_size("dp") * lax.axis_size("seq")
    qkv_sum, out_sum, up_sum, down_sum, norm1_sum, norm2_sum = lax.psum(
        (qkv_grad, out_grad, up_grad, down_grad, norm1_grad, norm2_grad), ("dp", "seq")
    )
    return (
        output,
        tokens_grad,
        norm1_sum / device_count,
        qkv_sum / device_count,
        out_sum / device_count,
        norm2_sum / device_count,
        up_sum / device_count,
        down_sum / device_count,
    )


eps = 1e-05
f32 = jnp.float32
bf16 = jnp.bfloat16
AXES = ("dp", "seq")
GRID_DP, GRID_SEQ = 4, 8
ROOM = 56 * 2**20


def place(y, x, z, c):
    return (y * 2 + x) * GRID_SEQ + z * 2 + c


def pairs(move):
    return [
        (place(y, x, z, c), place(*move(y, x, z, c)))
        for y in range(2)
        for x in range(2)
        for z in range(4)
        for c in range(2)
    ]


INNER = pairs(lambda y, x, z, c: (y, x, 3 - z, c))
INNER = [(a, b) for a, b in INNER if (a % GRID_SEQ) // 2 in (1, 2)]
OUTWARD = pairs(lambda y, x, z, c: (y, x, z ^ 1, c))
OUTWARD = [(a, b) for a, b in OUTWARD if (a % GRID_SEQ) // 2 in (1, 2)]
ALONG_Z = {k: pairs(lambda y, x, z, c, k=k: (y, x, z ^ k, c)) for k in (1, 2, 3)}
CORES = pairs(lambda y, x, z, c: (y, x, z, 1 - c))
FIRST = pairs(lambda y, x, z, c: (y, 1 - x, z, c) if c == 0 else (1 - y, x, z, c))
SECOND = pairs(lambda y, x, z, c: (1 - y, x, z, c) if c == 0 else (y, 1 - x, z, c))


def send(value, perm, tag="send"):
    with jax.named_scope("t_" + tag):
        return lax.ppermute(value, AXES, perm)


def nn(a, b, precision=None):
    return lax.dot_general(
        a, b, (((1,), (0,)), ((), ())), precision=precision, preferred_element_type=f32
    )


def nt(a, b, precision=None):
    return lax.dot_general(
        a, b, (((1,), (1,)), ((), ())), precision=precision, preferred_element_type=f32
    )


def work(micros):
    return pl.CostEstimate(flops=int(micros * 1e9), bytes_accessed=0, transcendentals=0)


def here():
    dp, seq = lax.axis_index("dp"), lax.axis_index("seq")
    y, x, z, c = dp // 2, dp % 2, seq // 2, seq % 2
    return z, c, jnp.where(c == 0, x, y), jnp.where(c == 0, y, x)


def kernel_call(body, outs, args, scratch=(), name=None, micros=2, room=16, far=(), out=(), order=None, early=(), onto=()):
    vmem = pl.BlockSpec(memory_space=pltpu.VMEM)
    args = list(args)
    staged = len(args)
    args += list(onto)
    held = len(args)
    args += list(early) + list(order or ())
    ignored = len(args) - held
    outs = [*outs, ((8, 128), f32)]
    shapes = [
        jax.ShapeDtypeStruct(s, d) if n in far or n in out else pltpu.VMEM(s, d) for n, (s, d) in enumerate(outs)
    ]
    specs = [pl.BlockSpec(memory_space=pl.ANY) if n in far else vmem for n in range(len(outs))]
    results = len(outs) - 1

    def whole(*refs):
        refs, mark, rest = refs[: held + ignored + results], refs[held + ignored + results], refs[held + ignored + results + 1 :]
        mark[...] = jnp.zeros((8, 128), f32)
        body(*refs[:held], *refs[held + ignored :], *rest)

    *values, mark = pl.pallas_call(
        whole,
        out_shape=shapes,
        in_specs=[pl.BlockSpec(memory_space=pl.ANY) if staged <= n < held else vmem for n in range(len(args))],
        out_specs=specs,
        scratch_shapes=list(scratch),
        input_output_aliases={staged + n: n for n in range(len(onto))},
        compiler_params=pltpu.CompilerParams(vmem_limit_bytes=room * 2**20),
        name=name,
        cost_estimate=work(micros),
    )(*[a if staged <= n < held else pltpu.with_memory_space_constraint(a, pltpu.VMEM) for n, a in enumerate(args)])
    if order is not None:
        order[:] = [mark]
    return values


def pick(v, bit):
    return jnp.where(bit == 0, v[:, 0:64], v[:, 64:128])


def normalise(v):
    mean = jnp.mean(v, axis=-1, keepdims=True)
    centred = v - mean
    inv = lax.rsqrt(jnp.mean(centred * centred, axis=-1, keepdims=True) + eps)
    return centred * inv, inv


def normalise_back(e, n, inv):
    return (e - jnp.mean(e, axis=-1, keepdims=True) - n * jnp.mean(e * n, axis=-1, keepdims=True)) * inv


def doc_numbers(doc):
    at = lax.broadcasted_iota(jnp.int32, (128, 128), 0)
    to = lax.broadcasted_iota(jnp.int32, (128, 128), 1)
    upper = (at <= to).astype(f32)
    a8 = lax.broadcasted_iota(jnp.int32, (8, 8), 0)
    t8 = lax.broadcasted_iota(jnp.int32, (8, 8), 1)
    before = (t8 < a8).astype(f32)
    spread = jnp.broadcast_to(jnp.sum(doc, axis=1, keepdims=True), (8, 128))
    high = lax.Precision.HIGHEST
    rows = nn(doc, upper, high) + nn(before, spread, high)
    eye = (at == to).astype(f32)
    cols = nt(eye, rows, high)
    return rows, cols


def row_of(rows, lo, hi):
    return jnp.concatenate([rows[j : j + 1, :] for j in range(lo, hi)], axis=1)


def col_of(cols, lo, hi):
    return jnp.concatenate([cols[:, j : j + 1] for j in range(lo, hi)], axis=0)


def gelu_parts(u):
    return 0.5 + 0.5 * lax.erf(u * 0.7071067811865476), jnp.exp(-0.5 * u * u) * 0.3989422804014327


def prepare(tokens, doc, cot, message, cot_o):
    message[0:128, :] = tokens[...].astype(f32)
    message[128:136, :] = jnp.zeros((8, 512), f32)
    message[128:129, 0:128] = doc[...].astype(f32)
    cot_o[...] = cot[...].astype(f32)


def join(*refs):
    at = 0
    out = refs[-1]
    for ref in refs[:-1]:
        out[at : at + ref.shape[0]] = ref[...]
        at += ref.shape[0]


def joined(order, *values, early=()):
    values = [v[None] if v.ndim == 2 else v for v in values]
    shape = (sum(v.shape[0] for v in values),) + values[0].shape[1:]
    return kernel_call(join, [(shape, f32)], values, name="join", micros=0, order=order, early=early)[0]


def gate(*refs):
    half = len(refs) // 2
    for ref, out in zip(refs[:half], refs[half:]):
        out[...] = ref[...]


def choose_far(near, far, out):
    z, _, _, _ = here()
    inner = (z == 1) | (z == 2)
    for n in range(2):
        out[n] = jnp.where(inner, near[1 - n], far[n])


def head_forward(t0, t1, t2, t3, p0, p1, p2, p3, gain, w, omega,
                 keep, give, phq_o, phk_o, qk_o, v_o, mxd_o, doc_o, nt_o, low):
    z, c, _, _ = here()
    wh = jnp.concatenate([pick(w[:, pl.ds(pl.multiple_of(part * 512 + z * 128, 128), 128)], c) for part in range(3)], axis=1)
    g = gain[...]
    for k, (mine, theirs) in enumerate(((t0, p0), (t1, p1), (t2, p2), (t3, p3))):
        for ref, core in ((mine, c), (theirs, 1 - c)):
            chunk = 2 * jnp.bitwise_xor(z, k) + core
            n, _ = normalise(ref[0:128, :])
            low[pl.ds(pl.multiple_of(chunk * 128, 128), 128), :] = (n * g).astype(bf16)
            doc_o[pl.ds(chunk, 1), :] = ref[128:129, 0:128]
    rows, cols = doc_numbers(doc_o[...])
    nt_o[...] = jnp.transpose(low[:, pl.ds(pl.multiple_of(c * 256, 256), 256)])
    s = 64 ** -0.25
    om = omega[2 * z + c]
    oh = om.astype(bf16)
    ol = (om - oh.astype(f32)).astype(bf16)
    stack = jnp.concatenate([oh, oh, ol], axis=0)

    def feature(v):
        v = v * s
        hi = v.astype(bf16)
        lo = (v - hi.astype(f32)).astype(bf16)
        proj = nn(jnp.concatenate([hi, lo, hi], axis=1), stack)
        return jnp.exp(proj - 0.5 * jnp.sum(v * v, axis=-1, keepdims=True))

    for b in range(4):
        at = pl.ds(256 * b, 256)
        pr = nn(low[at, :], wh)
        qk_o[at, :] = pr[:, 0:128]
        v_o[at, :] = pr[:, 128:192].astype(bf16)
        phq_o[at, :] = feature(pr[:, 0:64]).astype(bf16)
        phk_o[at, :] = feature(pr[:, 64:128]).astype(bf16)
    for b in range(4):
        at = pl.ds(256 * b, 256)
        n = 256 * (b + 1)
        scores = nt(phq_o[at, :], phk_o[0:n, :])
        i = lax.broadcasted_iota(jnp.int32, (256, n), 0) + 256 * b
        j = lax.broadcasted_iota(jnp.int32, (256, n), 1)
        same = (col_of(cols, 2 * b, 2 * b + 2) == row_of(rows, 0, 2 * b + 2)) & (i >= j)
        scores = jnp.where(same, scores, 0.0)
        inv = 1.0 / jnp.sum(scores, axis=-1, keepdims=True)
        mixed = nn(scores.astype(bf16), v_o[0:n, :]) * inv
        mxd_o[at, :] = jnp.concatenate([mixed, jnp.broadcast_to(inv, (256, 64))], axis=1)
        top, bottom = mixed[0:128, :], mixed[128:256, :]
        keep[b] = jnp.where(c == 0, top, bottom)
        give[b] = jnp.where(c == 0, bottom, top)


def pack_pairs(keep, got, b0, b1, b2, b3):
    z, c, _, _ = here()
    for k, out in enumerate((b0, b1, b2, b3)):
        j = jnp.bitwise_xor(z, k)
        a, b = keep[j], got[j]
        out[...] = jnp.where(c == 0, jnp.concatenate([a, b], axis=1), jnp.concatenate([b, a], axis=1))


def unpack_pairs(b0, b1, b2, b3, keep, give):
    z, c, _, _ = here()
    for k, ref in enumerate((b0, b1, b2, b3)):
        j = jnp.bitwise_xor(z, k)
        a, b = ref[:, 0:64], ref[:, 64:128]
        keep[j] = jnp.where(c == 0, a, b)
        give[j] = jnp.where(c == 0, b, a)


def middle_part(b0, b1, b2, b3, tokens, wo, gain, mixed_o, middle_o, normed_o):
    z, _, _, _ = here()
    for k, ref in enumerate((b0, b1, b2, b3)):
        j = jnp.bitwise_xor(z, k)
        mixed_o[:, pl.ds(pl.multiple_of(j * 128, 128), 128)] = ref[...].astype(bf16)
    middle = tokens[...].astype(f32) + nn(mixed_o[...], wo[...])
    middle_o[...] = middle
    n, _ = normalise(middle)
    normed_o[...] = (n * gain[...]).astype(bf16).astype(f32)


def feed_forward(mixed, middle, normed, cot, wu, wd, wo, gain,
                 out_o, mg_o, ml_o, ex0, ex1, ex2, b0, b1, b2, b3, scr):
    z, c, _, _ = here()
    x = normed[...].astype(bf16)
    inc = cot[...]
    total = middle[...]
    back = jnp.zeros((128, 512), f32)
    for u in range(4):
        at = pl.ds(512 * u, 512)
        wub, wdb = wu[:, at], wd[at, :]
        up = nn(x, wub)
        cdf, pdf = gelu_parts(up)
        total = total + nn((up * cdf).astype(bf16), wdb)
        ug = ((cdf + up * pdf) * nt(inc, wdb)).astype(bf16)
        back = back + nt(ug, wub)
    out_o[...] = total.astype(bf16)
    n, inv = normalise(middle[...])
    mg = inc.astype(f32) + normalise_back(gain[...] * back, n, inv)
    mg_o[...] = mg
    low = mg.astype(bf16)
    ml_o[...] = low
    ex0[...] = mixed[:, pl.ds(pl.multiple_of((1 - c) * 256, 256), 256)].astype(f32)
    ex1[...] = low[:, 0:256].astype(f32)
    ex2[...] = low[:, 256:512].astype(f32)
    scr[...] = nt(low, wo[...])
    for k, ref in enumerate((b0, b1, b2, b3)):
        j = jnp.bitwise_xor(z, k)
        ref[...] = scr[:, pl.ds(pl.multiple_of(j * 128, 128), 128)]


def out_part(mixed, mlow, got0, got1, got2, keep, give, scr):
    _, c, first, _ = here()
    mine = mixed[:, pl.ds(pl.multiple_of(c * 256, 256), 256)].astype(f32)
    left = jnp.transpose(jnp.concatenate([mine, got0[...]], axis=0)).astype(bf16)
    theirs = jnp.concatenate([got1[...], got2[...]], axis=1).astype(bf16)
    right = jnp.concatenate([mlow[...], theirs], axis=0)
    scr[...] = nn(left, right)
    keep[...] = scr[pl.ds(pl.multiple_of(first * 128, 128), 128), :]
    give[...] = scr[pl.ds(pl.multiple_of((1 - first) * 128, 128), 128), :]


def add_spread(mine, got, o0, o1, o2, o3, scr):
    z, _, _, _ = here()
    scr[...] = mine[...] + got[...]
    for k, ref in enumerate((o0, o1, o2, o3)):
        j = jnp.bitwise_xor(z, k)
        ref[...] = scr[:, pl.ds(pl.multiple_of(j * 128, 128), 128)]


def add_last(mine, got, o0, o1, o2, o3, out):
    out[:, 0:384] = (mine[...] + got[...]) * (1.0 / 32)
    out[:, 384:512] = ((o0[...] + o1[...]) + (o2[...] + o3[...])) * (1.0 / 32)


def head_backward(keep, got, phq, phk, qk, v, mxd, doc, omega, pg0, pg1, pg2, r_scr, m_scr, pg_o):
    z, c, _, _ = here()
    for b in range(4):
        a, g = keep[b], got[b]
        at = pl.ds(256 * b, 256)
        dm = jnp.concatenate([jnp.where(c == 0, a, g), jnp.where(c == 0, g, a)], axis=0)
        r = dm * mxd[at, 64:128]
        r_scr[at, :] = r.astype(bf16)
        m_scr[at, :] = r * mxd[at, 0:64]
    rows, cols = doc_numbers(doc[...])
    ones = jnp.ones((8, 64), f32)
    s = 64 ** -0.25
    om = omega[2 * z + c].astype(bf16)

    def feature_back(ph, grad, base):
        a = ph.astype(f32) * grad
        return s * nt(a.astype(bf16), om) - (s * s) * base * jnp.sum(a, axis=-1, keepdims=True)

    for b in range(4):
        at = pl.ds(256 * b, 256)
        n = 256 * (b + 1)
        i = lax.broadcasted_iota(jnp.int32, (256, n), 0) + 256 * b
        j = lax.broadcasted_iota(jnp.int32, (256, n), 1)
        same = (col_of(cols, 2 * b, 2 * b + 2) == row_of(rows, 0, 2 * b + 2)) & (i >= j)
        ds = nt(r_scr[at, :], v[0:n, :]) - jnp.sum(m_scr[at, :], axis=-1, keepdims=True)
        ds = jnp.where(same, ds, 0.0).astype(bf16)
        qg = feature_back(phq[at, :], nn(ds, phk[0:n, :]), qk[at, 0:64])
        m = 1024 - 256 * b
        later = pl.ds(256 * b, m)
        j2 = lax.broadcasted_iota(jnp.int32, (256, m), 0)
        i2 = lax.broadcasted_iota(jnp.int32, (256, m), 1)
        same2 = (col_of(cols, 2 * b, 2 * b + 2) == row_of(rows, 2 * b, 8)) & (i2 >= j2)
        scores = jnp.where(same2, nt(phk[at, :], phq[later, :]), 0.0).astype(bf16)
        vg = nn(scores, r_scr[later, :])
        mr = nt(ones, m_scr[later, :], lax.Precision.HIGHEST)[0:1, :]
        ds2 = jnp.where(same2, nt(v[at, :], r_scr[later, :]) - mr, 0.0).astype(bf16)
        kg = feature_back(phk[at, :], nn(ds2, phq[later, :]), qk[at, 64:128])
        rnd = lambda t: t.astype(bf16).astype(f32)
        pg_o[at, :] = rnd(jnp.concatenate([qg, kg], axis=1))
        pg_o[pl.ds(1024 + 256 * (b % 2), 256), 64 * (b // 2) : 64 * (b // 2) + 64] = rnd(vg)
    for n, out in enumerate((pg0, pg1, pg2)):
        out[...] = pg_o[512 * n : 512 * n + 512, :]


def weight_part(m0, m1, m2, t0, t1, t2, nt_low, q0, q1, q2, q3, keep, give, scr, g_scr):
    z, c, first, _ = here()
    for b in range(4):
        at = pl.ds(256 * b, 256)
        half = pl.ds(256 * (b % 2), 256)
        lanes = slice(64 * (b // 2), 64 * (b // 2) + 64)
        a, t = ((m0, t0), (m1, t1))[b // 2]
        a, t = a[half, :], t[half, :]
        av, tv = m2[half, lanes], t2[half, lanes]
        h0 = jnp.where(c == 0, a, t)
        h1 = jnp.where(c == 0, t, a)
        scr[at, 0:128] = jnp.concatenate([h0[:, 0:64], h1[:, 0:64]], axis=1)
        scr[at, 128:256] = jnp.concatenate([h0[:, 64:128], h1[:, 64:128]], axis=1)
        scr[at, 256:384] = jnp.concatenate([jnp.where(c == 0, av, tv), jnp.where(c == 0, tv, av)], axis=1)
    for k, ref in enumerate((q0, q1, q2, q3)):
        chunk = 2 * jnp.bitwise_xor(z, k) + c
        ref[...] = scr[pl.ds(pl.multiple_of(chunk * 128, 128), 128), :]
    g_scr[...] = nn(nt_low[...], scr[...].astype(bf16))
    keep[...] = g_scr[pl.ds(pl.multiple_of(first * 128, 128), 128), :]
    give[...] = g_scr[pl.ds(pl.multiple_of((1 - first) * 128, 128), 128), :]


def tokens_part(q0, q1, q2, q3, mg, tokens, w, gain, out_o, scr):
    z, _, _, _ = here()
    for k, ref in enumerate((q0, q1, q2, q3)):
        j = jnp.bitwise_xor(z, k)
        for part in range(3):
            scr[:, pl.ds(pl.multiple_of(part * 512 + j * 128, 128), 128)] = ref[:, 128 * part : 128 * part + 128].astype(bf16)
    n, inv = normalise(tokens[...].astype(f32))
    e = gain[...] * nt(scr[...], w[...])
    out_o[...] = mg[...] + normalise_back(e, n, inv)


def add_split(mine, got, keep, give):
    _, _, _, second = here()
    a = pl.ds(pl.multiple_of(second * 64, 64), 64)
    b = pl.ds(pl.multiple_of((1 - second) * 64, 64), 64)
    keep[...] = mine[a, :] + got[a, :]
    give[...] = mine[b, :] + got[b, :]


def ffn_narrow(count, *refs):
    xs, cs, (xb, cb) = refs[:count], refs[count : 2 * count], refs[2 * count :]
    at = 0
    for x, cc in zip(xs, cs):
        for i in range(x.shape[0]):
            xb[pl.ds(at, 128), :] = x[i].astype(bf16)
            cb[pl.ds(at, 128), :] = cc[i].astype(bf16)
            at += 128


def ffn_weights(unit, mine, first, last, xb, cb, wu, wd, *refs):
    if not first:
        before, *refs = refs
    if last:
        theirs, out, up_o, gain_o = refs
    else:
        (out,) = refs
    _, c, _, _ = here()
    core = c if mine else 1 - c
    place = pl.ds(pl.multiple_of(core * 1024 + 256 * unit, 256), 256)
    wut, wdu = jnp.transpose(wu[:, place]), wd[place, :]
    x, inc = xb[...], cb[...]
    up = nt(wut, x)
    hg = nt(wdu, inc)
    cdf, pdf = gelu_parts(up)
    total_up = nn(((cdf + up * pdf) * hg).astype(bf16), x)
    total_down = nn((up * cdf).astype(bf16), inc)
    if not first:
        total_up = total_up + before[0:256, :]
        total_down = total_down + before[256:512, :]
    if last:
        total_up = (total_up + theirs[0:256, :]) * (1.0 / 32)
        total_down = (total_down + theirs[256:512, :]) * (1.0 / 32)
        up_o[...] = jnp.transpose(total_up)
        part = jnp.sum(total_up * wut.astype(f32), axis=0, keepdims=True)
        gain_o[...] = jnp.broadcast_to(part, (8, 512))
    out[0:256, :] = total_up
    out[256:512, :] = total_down


def place_mine(*refs):
    ups, both = refs[0:4], refs[4:8]
    up_o, down_o, sems = refs[8:]
    _, c, _, _ = here()
    copies = []
    for n in range(4):
        at = pl.ds(pl.multiple_of(c * 1024 + 256 * n, 256), 256)
        copies.append(pltpu.make_async_copy(ups[n], up_o.at[:, at], sems.at[2 * n]))
        copies.append(pltpu.make_async_copy(both[n].at[256:512, :], down_o.at[at, :], sems.at[2 * n + 1]))
    for copy in copies:
        copy.start()
    for copy in copies:
        copy.wait()


def place_theirs(b0, b1, b2, b3, up_in, down_in, up_o, down_o, ups, sems):
    _, c, _, _ = here()
    copies = []
    for n, both in enumerate((b0, b1, b2, b3)):
        at = pl.ds(pl.multiple_of((1 - c) * 1024 + 256 * n, 256), 256)
        copies.append(pltpu.make_async_copy(both.at[256:512, :], down_o.at[at, :], sems.at[2 * n]))
        copies[-1].start()
    for n, both in enumerate((b0, b1, b2, b3)):
        at = pl.ds(pl.multiple_of((1 - c) * 1024 + 256 * n, 256), 256)
        ups[n] = jnp.transpose(both[0:256, :])
        copies.append(pltpu.make_async_copy(ups.at[n], up_o.at[:, at], sems.at[2 * n + 1]))
        copies[-1].start()
    for copy in copies:
        copy.wait()


def add_gains(g0, g1, g2, g3, other, gain2, out):
    total = (g0[...] + g1[...]) + (g2[...] + g3[...])
    out[...] = (total[0:1, :] + other[0:1, :]) / gain2[...]


def sum_gains(g0, g1, g2, g3, out):
    out[...] = (g0[...] + g1[...]) + (g2[...] + g3[...])


def finish(a, b, ca, cb, w, gain, qkv_o, out_o, gain_o):
    z, c, first, second = here()
    for n in range(4):
        for core, ref, r1, r2 in ((c, (a, b)[n // 2], first, second), (1 - c, (ca, cb)[n // 2], second, first)):
            row = core * 256 + jnp.bitwise_xor(r1, n % 2) * 128 + jnp.bitwise_xor(r2, n // 2) * 64
            rows = pl.ds(pl.multiple_of(row, 64), 64)
            for k in range(4):
                j = jnp.bitwise_xor(z, k)
                piece = ref.at[4 * (n % 2) + k]
                for part in range(3):
                    at = pl.ds(pl.multiple_of(part * 512 + j * 128, 128), 128)
                    qkv_o[rows, at] = piece[:, 128 * part : 128 * part + 128]
                out_o[rows, pl.ds(pl.multiple_of(j * 128, 128), 128)] = piece[:, 384:512]
    for r in range(4):
        rows = pl.ds(128 * r, 128)
        acc = jnp.zeros((128, 128), f32)
        for j in range(12):
            lanes = pl.ds(128 * j, 128)
            acc = acc + w[rows, lanes].astype(f32) * qkv_o[rows, lanes]
        lanes = pl.ds(128 * r, 128)
        gain_o[0:1, lanes] = jnp.sum(jnp.transpose(acc), axis=0, keepdims=True) / gain[0:1, lanes]


def across(values):
    return [send(v, CORES) for v in values]


def local_fast(tokens, doc_start, norm1_gain, qkv_weight, out_weight, norm2_gain, up_weight, down_weight, omega, cotangent):
    g1, g2 = norm1_gain.reshape(1, 512), norm2_gain.reshape(1, 512)
    tok, cot = tokens[0], cotangent[0]
    order = []
    call = functools.partial(kernel_call, order=order)
    join = functools.partial(joined, order)
    block = ((128, 128), f32)

    def later(*values):
        return call(gate, [(v.shape, v.dtype) for v in values], values, name="gate", micros=0)

    def wait(*values):
        call(gate, [], [], name="gate", micros=0, early=values)

    def pause(micros):
        call(gate, [], [], name="pause", micros=micros)

    def narrow(xs, cs):
        rows = 128 * sum(v.shape[0] for v in xs)
        return call(functools.partial(ffn_narrow, len(xs)), [((rows, 512), bf16)] * 2, [*xs, *cs], name="ffn_narrow", micros=0)

    def ffn(unit, mine, xc, before=None, theirs=None, micros=0):
        first, last = before is None, theirs is not None
        outs = [((512, 512), f32)] + ([((512, 256), f32), ((8, 512), f32)] if last else [])
        more = ([] if first else [before]) + ([theirs] if last else [])
        got = call(
            functools.partial(ffn_weights, unit, mine, first, last), outs, [*xc, up_weight, down_weight, *more],
            (), "ffn_weights", micros, 24,
        )
        return got if last else got[0]

    message, cot_wide = call(prepare, [((136, 512), f32), ((128, 512), f32)], [tok, doc_start, cot], name="prepare")
    t = [message] + [send(message, ALONG_Z[k], "tok") for k in (1, 2, 3)]
    ca = join(cot_wide, send(cot_wide, ALONG_Z[1], "c1"), early=t)
    p = [send(v, CORES, "tok") for v in t]
    ca_first = send(ca, FIRST, "ca")
    c_inner = send(ca, INNER, "c")
    keep, give, phq, phk, qk, v, mxd, doc, nt_low = call(
        head_forward,
        [((4, 128, 64), f32), ((4, 128, 64), f32), ((1024, 256), bf16), ((1024, 256), bf16), ((1024, 128), f32),
         ((1024, 64), bf16), ((1024, 128), f32), ((8, 128), f32), ((256, 1024), bf16)],
        [*t, *p, g1, qkv_weight, omega], [pltpu.VMEM((1024, 512), bf16)], "head_forward", 2,
    )
    b = call(pack_pairs, [block] * 4, [keep, send(give, CORES, "give")], name="pack_pairs", micros=0)
    b = [b[0]] + [send(b[k], ALONG_Z[k], "mixed") for k in (1, 2, 3)]
    pause(0.8)
    ca_two = join(ca, ca_first)
    ca_other = send(ca_two, SECOND, "ca")
    (c_inner,) = later(c_inner)
    mixed, middle, normed = call(
        middle_part, [((128, 512), bf16), ((128, 512), f32), ((128, 512), f32)], [*b, tok, out_weight, g2],
        name="middle_part", micros=0.2,
    )
    x1 = send(normed, ALONG_Z[1], "x1")
    output, mg, mlow, ex0, ex1, ex2, *b = call(
        feed_forward,
        [((128, 512), bf16), ((128, 512), f32), ((128, 512), bf16)] + [((128, 256), f32)] * 3 + [block] * 4,
        [mixed, middle, normed, cot, up_weight, down_weight, out_weight, g2], [pltpu.VMEM((128, 512), f32)],
        "feed_forward", 1.4, out=(0,),
    )
    b = [b[0]] + [send(b[k], ALONG_Z[k], "mg") for k in (1, 2, 3)]
    ex_other = [send(w, CORES, "ex") for w in (ex0, ex1, ex2)]
    pause(1.5)
    okeep, ogive = call(out_part, [((128, 512), f32)] * 2, [mixed, mlow, *ex_other],
                        [pltpu.VMEM((256, 512), f32)], "out_part", micros=0)
    ogot = send(ogive, FIRST, "o")
    xa = join(normed, x1)
    xa_first = send(xa, FIRST, "xa")
    keep, give = call(unpack_pairs, [((4, 128, 64), f32)] * 2, b, name="unpack_pairs", micros=0)
    got = send(give, CORES, "give")
    c_outer = send(later(c_inner)[0], OUTWARD, "c")
    x_inner = send(later(xa)[0], INNER, "x")
    pg = call(
        head_backward, [((512, 128), f32)] * 3, [keep, got, phq, phk, qk, v, mxd, doc, omega],
        [pltpu.VMEM((1024, 64), bf16), pltpu.VMEM((1024, 64), f32), pltpu.VMEM((1536, 128), f32)], "head_backward", 2.9,
    )
    pg_other = [send(w, CORES, "pg") for w in pg]
    okeep, ogive = call(add_split, [((64, 512), f32)] * 2, [okeep, ogot], name="add_split", micros=0)
    ogot = send(ogive, SECOND, "o")
    xa_two = join(xa, xa_first)
    xa_other = send(xa_two, SECOND, "xa")
    *q, keep, give = call(
        weight_part, [((128, 384), f32)] * 4 + [((128, 384), f32)] * 2, [*pg, *pg_other, nt_low],
        [pltpu.VMEM((1024, 384), f32), pltpu.VMEM((256, 384), f32)], "weight_part", micros=0,
    )
    got = send(give, FIRST, "rs")
    pause(2.2)
    c_a = later(ca_two, ca_other)
    (cb,) = call(choose_far, [((2, 128, 512), f32)], [c_inner, c_outer], name="choose_far", micros=0)
    (x_inner,) = later(x_inner)
    o = call(add_spread, [((64, 128), f32)] * 4, [okeep, ogot], [pltpu.VMEM((64, 512), f32)], "add_spread", micros=0)
    o = [o[0]] + [send(o[k], ALONG_Z[k], "o") for k in (1, 2, 3)]
    keep, give = call(add_split, [((64, 384), f32)] * 2, [keep, got], name="add_split", micros=0)
    got = send(give, SECOND, "rs")
    pause(1.2)
    cb_first = send(later(cb)[0], FIRST, "cb")
    (x_inner,) = later(x_inner)
    x_outer = send(x_inner, OUTWARD, "x")
    (piece,) = call(add_last, [((64, 512), f32)], [keep, got, *o], name="add_last", micros=0)
    piece_line = [send(piece, ALONG_Z[k], "piece") for k in (1, 2, 3)]
    pause(3)
    pause(5)
    x_a = later(xa_two, xa_other)
    cb_two = join(cb, cb_first)
    cb_other = send(cb_two, SECOND, "cb")
    (xb,) = call(choose_far, [((2, 128, 512), f32)], [x_inner, x_outer], name="choose_far", micros=0)
    xb_first = send(xb, FIRST, "xb")
    x_now = narrow(x_a, c_a)
    order_of = [(u, mine) for mine in (False, True) for u in range(4)]
    total = {}
    for n, (u, mine) in enumerate(order_of):
        total[u, mine] = ffn(u, mine, x_now, micros=1)
        if n == 0:
            pieces = join(piece, *piece_line)
            pieces_first = send(pieces, FIRST, "piece")
        if n == 5:
            xb_two = join(xb, xb_first)
            xb_other = send(xb_two, SECOND, "xb")
    pause(3.5)
    c_b = later(cb_two, cb_other)
    pieces = [join(pieces, pieces_first)]
    pieces.append(send(pieces[0], SECOND, "piece"))
    q = [q[0]] + [send(w, ALONG_Z[k], "q") for k, w in zip((1, 2, 3), later(*q[1:]))]
    pause(6)
    (tokens_grad,) = call(
        tokens_part, [((128, 512), f32)], [*q, mg, tok, qkv_weight, g1], [pltpu.VMEM((128, 1536), bf16)],
        "tokens_part", micros=1, out=(0,),
    )
    x_b = later(xb_two, xb_other)
    x_now = narrow(x_b, c_b)
    others = [send(ffn(u, False, x_now, total[u, False], micros=2.8), CORES, "part") for u in range(4)]
    both, ups, gains = zip(*[ffn(u, True, x_now, total[u, True], others[u], micros=2.8) for u in range(4)])
    both_other = [send(w, CORES, "both") for w in both]
    (gain,) = call(sum_gains, [((8, 512), f32)], gains, name="sum_gains", micros=0)
    gain_other = send(gain, CORES, "gain")
    dma = [pltpu.SemaphoreType.DMA((8,))]
    up_grad, down_grad = call(
        place_mine, [((512, 2048), f32), ((2048, 512), f32)], [*ups, *both], dma, "place_mine", 2, far=(0, 1),
    )
    qkv_grad, out_grad, norm1_grad = call(
        finish, [((512, 1536), f32), ((512, 512), f32), ((1, 512), f32)],
        [*pieces, *[send(w, CORES, "piece") for w in pieces], qkv_weight, g1], (), "finish", 3, out=(0, 1),
    )
    (norm2_grad,) = call(add_gains, [((1, 512), f32)], [*gains, gain_other, g2], name="add_gains", micros=0)
    up_grad, down_grad = call(
        place_theirs, [((512, 2048), f32), ((2048, 512), f32)], both_other, [pltpu.VMEM((4, 512, 256), f32), *dma],
        "place_theirs", 2, far=(0, 1), onto=(up_grad, down_grad),
    )
    return (output[None], tokens_grad[None], norm1_grad[0], qkv_grad, out_grad, norm2_grad[0], up_grad, down_grad)


def solution(mesh):
    placed = (
        P("dp", "seq", None),
        P("dp", "seq"),
        P(),
        P(),
        P(),
        P(),
        P(),
        P(),
        P(),
        P("dp", "seq", None),
    )
    fits = mesh.shape["dp"] == GRID_DP and mesh.shape["seq"] == GRID_SEQ
    return jax.shard_map(
        local_fast if fits else local,
        mesh=mesh,
        in_specs=placed,
        out_specs=(P("dp", "seq", None), P("dp", "seq", None), P(), P(), P(), P(), P(), P()),
        check_vma=False,
    )
```

```python
import functools

import jax
import jax.numpy as jnp
from jax import lax
from jax.experimental import pallas as pl
from jax.experimental.pallas import tpu as pltpu
from jax.sharding import PartitionSpec as P

norm_eps = 1e-05
highest_precision = lax.Precision.HIGHEST


def entering(value, axis, join, neutral, backward):
    count, mine = (lax.axis_size(axis), lax.axis_index(axis))
    pieces = jax.tree.map(lambda part: lax.all_gather(part, axis), value)
    if backward:
        pieces = jax.tree.map(lambda part: part[::-1], pieces)
        mine = count - 1 - mine
    running = jax.tree.map(
        lambda part, zero: jnp.full_like(part, 0) + jnp.asarray(zero, part.dtype), value, neutral
    )

    def hop(position, running):
        longer = join(running, jax.tree.map(lambda part: part[position], pieces))
        return jax.tree.map(lambda new, old: jnp.where(position < mine, new, old), longer, running)

    return lax.fori_loop(0, count - 1, hop, running)


def layer_norm(values, gain):
    average = jnp.mean(values, axis=-1, keepdims=True)
    centred = values - average
    spread_sq = jnp.mean(centred * centred, axis=-1, keepdims=True)
    return centred * lax.rsqrt(spread_sq + norm_eps) * gain


def features(head_values, omega):
    width_dim = head_values.shape[-1]
    scaled = head_values * width_dim ** (-0.25)
    projection = jnp.einsum("...hd,hdm->...hm", scaled, omega, precision=highest_precision)
    half_square = 0.5 * jnp.sum(scaled * scaled, axis=-1, keepdims=True)
    return jnp.exp(projection - half_square)


def exact_gelu(values):
    return jax.nn.gelu(values, approximate=False)


def row_masks(doc_start):
    stretch_len = doc_start.shape[1]
    doc_index = jnp.cumsum(doc_start, axis=1)
    position = jnp.arange(stretch_len, dtype=jnp.int32)
    same_doc = (doc_index[:, :, None] == doc_index[:, None, :]) & (
        position[None, :, None] >= position[None, None, :]
    )
    leading_document = (doc_index == 0).astype(jnp.float32)
    last_doc = (doc_index == doc_index[:, -1:]).astype(jnp.float32)
    document_marker = (doc_index[:, -1] > 0).astype(jnp.float32)
    return (same_doc.astype(jnp.float32), leading_document, last_doc, document_marker)


def mix_rows(
    query_features, key_feat, value_heads, running_state, carry_norm, same_doc, leading_document
):
    scores = (
        jnp.einsum("rihm,rjhm->rhij", query_features, key_feat, precision=highest_precision)
        * same_doc[:, None]
    )
    attention_numerator = jnp.einsum(
        "rhij,rjhd->rihd", scores, value_heads, precision=highest_precision
    )
    attention_numerator = attention_numerator + leading_document[:, :, None, None] * jnp.einsum(
        "rihm,rhmd->rihd", query_features, running_state, precision=highest_precision
    )
    denominator = jnp.transpose(jnp.sum(scores, axis=-1), (0, 2, 1))
    denominator = denominator + leading_document[:, :, None] * jnp.einsum(
        "rihm,rhm->rih", query_features, carry_norm, precision=highest_precision
    )
    return attention_numerator / denominator[..., None]


def stretch_totals(key_feat, value_heads, last_doc):
    key_masked_rows = key_feat * last_doc[:, :, None, None]
    state_sum = jnp.einsum(
        "rchm,rchd->rhmd", key_masked_rows, value_heads, precision=highest_precision
    )
    return (state_sum, jnp.sum(key_masked_rows, axis=1))


def carry_on(earlier, later):
    state_sum, norm_sum, document_marker = later
    pass_on = 1.0 - document_marker
    return (
        state_sum + pass_on[:, None, None, None] * earlier[0],
        norm_sum + pass_on[:, None, None] * earlier[1],
        jnp.maximum(earlier[2], document_marker),
    )


def local(
    tokens,
    doc_start,
    norm1_gain,
    qkv_weight,
    out_weight,
    norm2_gain,
    up_weight,
    down_weight,
    omega,
    cotangent,
):
    row_count, stretch_len, model_width = tokens.shape
    head_count = omega.shape[0]
    head_dim = omega.shape[1]
    token_count = row_count * stretch_len
    stream = tokens.astype(jnp.float32).reshape(token_count, model_width)
    same_doc, leading_document, last_doc, document_marker = row_masks(doc_start)
    normed_one, norm1_back = jax.vjp(layer_norm, stream, norm1_gain)
    normed_one_low = normed_one.astype(jnp.bfloat16)
    projected = jnp.dot(normed_one_low, qkv_weight, preferred_element_type=jnp.float32)
    head_split = projected.reshape(row_count, stretch_len, 3, head_count, head_dim)
    query_heads = head_split[:, :, 0]
    key_heads = head_split[:, :, 1]
    value_heads = head_split[:, :, 2]

    def both_features(query_part, key_part):
        return (features(query_part, omega), features(key_part, omega))

    (query_features, key_feat), feature_back = jax.vjp(both_features, query_heads, key_heads)

    def local_totals(key_part, value_part):
        return stretch_totals(key_part, value_part, last_doc)

    (state_sum, norm_sum), totals_back = jax.vjp(local_totals, key_feat, value_heads)
    empty_state = jnp.zeros_like(state_sum)
    empty_norm = jnp.zeros_like(norm_sum)
    empty_flag = jnp.zeros_like(document_marker)
    running_state, carry_norm, unused_flag = entering(
        (state_sum, norm_sum, document_marker),
        "seq",
        carry_on,
        (empty_state, empty_norm, empty_flag),
        False,
    )

    def local_mix(query_part, key_part, value_part, state_part, norm_part):
        return mix_rows(
            query_part, key_part, value_part, state_part, norm_part, same_doc, leading_document
        )

    mixed, mix_back = jax.vjp(
        local_mix, query_features, key_feat, value_heads, running_state, carry_norm
    )
    mixed_low = mixed.reshape(token_count, model_width).astype(jnp.bfloat16)
    branch = jnp.dot(mixed_low, out_weight, preferred_element_type=jnp.float32)
    middle = stream + branch
    normed_two, norm2_back = jax.vjp(layer_norm, middle, norm2_gain)
    normed_two_low = normed_two.astype(jnp.bfloat16)
    up_values = jnp.dot(normed_two_low, up_weight, preferred_element_type=jnp.float32)
    gelu_out, gelu_back = jax.vjp(exact_gelu, up_values)
    hidden = gelu_out.astype(jnp.bfloat16)
    ffn_out = jnp.dot(hidden, down_weight, preferred_element_type=jnp.float32)
    output = (middle + ffn_out).astype(jnp.bfloat16).reshape(row_count, stretch_len, model_width)
    incoming = cotangent.reshape(token_count, model_width)
    down_grad = jnp.einsum("tf,td->fd", hidden, incoming, preferred_element_type=jnp.float32)
    hidden_grad = jnp.einsum("td,fd->tf", incoming, down_weight, preferred_element_type=jnp.float32)
    (up_full,) = gelu_back(hidden_grad)
    up_grad_low = up_full.astype(jnp.bfloat16)
    up_grad = jnp.einsum(
        "td,tf->df", normed_two_low, up_grad_low, preferred_element_type=jnp.float32
    )
    normed_two_grad = jnp.einsum(
        "tf,df->td", up_grad_low, up_weight, preferred_element_type=jnp.float32
    )
    middle_part, norm2_grad = norm2_back(normed_two_grad)
    middle_grad = incoming.astype(jnp.float32) + middle_part
    middle_low = middle_grad.astype(jnp.bfloat16)
    out_grad = jnp.einsum("td,te->de", mixed_low, middle_low, preferred_element_type=jnp.float32)
    mixed_grad = jnp.einsum("te,de->td", middle_low, out_weight, preferred_element_type=jnp.float32)
    mixed_grad = mixed_grad.reshape(row_count, stretch_len, head_count, head_dim)
    query_feat_grad, key_feat_mix, value_mix, carry_state_grad, carry_norm_grad = mix_back(
        mixed_grad
    )
    later_state, later_norm, unused_later = entering(
        (carry_state_grad, carry_norm_grad, document_marker),
        "seq",
        carry_on,
        (empty_state, empty_norm, empty_flag),
        True,
    )
    key_feat_tot, value_tot = totals_back((later_state, later_norm))
    query_grad, key_grad = feature_back((query_feat_grad, key_feat_mix + key_feat_tot))
    value_grad = value_mix + value_tot
    projected_grad = jnp.stack((query_grad, key_grad, value_grad), axis=2)
    projected_grad = projected_grad.reshape(token_count, 3 * model_width).astype(jnp.bfloat16)
    qkv_grad = jnp.einsum(
        "td,te->de", normed_one_low, projected_grad, preferred_element_type=jnp.float32
    )
    normed_one_grad = jnp.einsum(
        "te,de->td", projected_grad, qkv_weight, preferred_element_type=jnp.float32
    )
    stream_part, norm1_grad = norm1_back(normed_one_grad)
    tokens_grad = (middle_grad + stream_part).reshape(row_count, stretch_len, model_width)
    device_count = lax.axis_size("dp") * lax.axis_size("seq")
    qkv_sum, out_sum, up_sum, down_sum, norm1_sum, norm2_sum = lax.psum(
        (qkv_grad, out_grad, up_grad, down_grad, norm1_grad, norm2_grad), ("dp", "seq")
    )
    return (
        output,
        tokens_grad,
        norm1_sum / device_count,
        qkv_sum / device_count,
        out_sum / device_count,
        norm2_sum / device_count,
        up_sum / device_count,
        down_sum / device_count,
    )


eps = 1e-05
f32 = jnp.float32
bf16 = jnp.bfloat16
AXES = ("dp", "seq")
GRID_DP, GRID_SEQ = 4, 8
ROOM = 56 * 2**20


def place(y, x, z, c):
    return (y * 2 + x) * GRID_SEQ + z * 2 + c


def pairs(move):
    return [
        (place(y, x, z, c), place(*move(y, x, z, c)))
        for y in range(2)
        for x in range(2)
        for z in range(4)
        for c in range(2)
    ]


INNER = pairs(lambda y, x, z, c: (y, x, 3 - z, c))
INNER = [(a, b) for a, b in INNER if (a % GRID_SEQ) // 2 in (1, 2)]
OUTWARD = pairs(lambda y, x, z, c: (y, x, z ^ 1, c))
OUTWARD = [(a, b) for a, b in OUTWARD if (a % GRID_SEQ) // 2 in (1, 2)]
ALONG_Z = {k: pairs(lambda y, x, z, c, k=k: (y, x, z ^ k, c)) for k in (1, 2, 3)}
CORES = pairs(lambda y, x, z, c: (y, x, z, 1 - c))
FIRST = pairs(lambda y, x, z, c: (y, 1 - x, z, c) if c == 0 else (1 - y, x, z, c))
SECOND = pairs(lambda y, x, z, c: (1 - y, x, z, c) if c == 0 else (y, 1 - x, z, c))


def send(value, perm, tag="send"):
    with jax.named_scope("t_" + tag):
        return lax.ppermute(value, AXES, perm)


def nn(a, b, precision=None):
    return lax.dot_general(
        a, b, (((1,), (0,)), ((), ())), precision=precision, preferred_element_type=f32
    )


def nt(a, b, precision=None):
    return lax.dot_general(
        a, b, (((1,), (1,)), ((), ())), precision=precision, preferred_element_type=f32
    )


def work(micros):
    return pl.CostEstimate(flops=int(micros * 1e9), bytes_accessed=0, transcendentals=0)


def here():
    dp, seq = lax.axis_index("dp"), lax.axis_index("seq")
    y, x, z, c = dp // 2, dp % 2, seq // 2, seq % 2
    return z, c, jnp.where(c == 0, x, y), jnp.where(c == 0, y, x)


def kernel_call(body, outs, args, scratch=(), name=None, micros=2, room=16, far=(), out=(), order=None, early=(), onto=()):
    vmem = pl.BlockSpec(memory_space=pltpu.VMEM)
    args = list(args)
    staged = len(args)
    args += list(onto)
    held = len(args)
    args += list(early) + list(order or ())
    ignored = len(args) - held
    outs = [*outs, ((8, 128), f32)]
    shapes = [
        jax.ShapeDtypeStruct(s, d) if n in far or n in out else pltpu.VMEM(s, d) for n, (s, d) in enumerate(outs)
    ]
    specs = [pl.BlockSpec(memory_space=pl.ANY) if n in far else vmem for n in range(len(outs))]
    results = len(outs) - 1

    def whole(*refs):
        refs, mark, rest = refs[: held + ignored + results], refs[held + ignored + results], refs[held + ignored + results + 1 :]
        mark[...] = jnp.zeros((8, 128), f32)
        body(*refs[:held], *refs[held + ignored :], *rest)

    *values, mark = pl.pallas_call(
        whole,
        out_shape=shapes,
        in_specs=[pl.BlockSpec(memory_space=pl.ANY) if staged <= n < held else vmem for n in range(len(args))],
        out_specs=specs,
        scratch_shapes=list(scratch),
        input_output_aliases={staged + n: n for n in range(len(onto))},
        compiler_params=pltpu.CompilerParams(vmem_limit_bytes=room * 2**20),
        name=name,
        cost_estimate=work(micros),
    )(*[a if staged <= n < held else pltpu.with_memory_space_constraint(a, pltpu.VMEM) for n, a in enumerate(args)])
    if order is not None:
        order[:] = [mark]
    return values


def pick(v, bit):
    return jnp.where(bit == 0, v[:, 0:64], v[:, 64:128])


def normalise(v):
    mean = jnp.mean(v, axis=-1, keepdims=True)
    centred = v - mean
    inv = lax.rsqrt(jnp.mean(centred * centred, axis=-1, keepdims=True) + eps)
    return centred * inv, inv


def normalise_back(e, n, inv):
    return (e - jnp.mean(e, axis=-1, keepdims=True) - n * jnp.mean(e * n, axis=-1, keepdims=True)) * inv


def doc_numbers(doc):
    at = lax.broadcasted_iota(jnp.int32, (128, 128), 0)
    to = lax.broadcasted_iota(jnp.int32, (128, 128), 1)
    upper = (at <= to).astype(f32)
    a8 = lax.broadcasted_iota(jnp.int32, (8, 8), 0)
    t8 = lax.broadcasted_iota(jnp.int32, (8, 8), 1)
    before = (t8 < a8).astype(f32)
    spread = jnp.broadcast_to(jnp.sum(doc, axis=1, keepdims=True), (8, 128))
    high = lax.Precision.HIGHEST
    rows = nn(doc, upper, high) + nn(before, spread, high)
    eye = (at == to).astype(f32)
    cols = nt(eye, rows, high)
    return rows, cols


def row_of(rows, lo, hi):
    return jnp.concatenate([rows[j : j + 1, :] for j in range(lo, hi)], axis=1)


def col_of(cols, lo, hi):
    return jnp.concatenate([cols[:, j : j + 1] for j in range(lo, hi)], axis=0)


def gelu_parts(u):
    return 0.5 + 0.5 * lax.erf(u * 0.7071067811865476), jnp.exp(-0.5 * u * u) * 0.3989422804014327


def prepare(tokens, doc, cot, message, cot_o):
    message[0:128, :] = tokens[...].astype(f32)
    message[128:136, :] = jnp.zeros((8, 512), f32)
    message[128:129, 0:128] = doc[...].astype(f32)
    cot_o[...] = cot[...].astype(f32)


def join(*refs):
    at = 0
    out = refs[-1]
    for ref in refs[:-1]:
        out[at : at + ref.shape[0]] = ref[...]
        at += ref.shape[0]


def joined(order, *values, early=()):
    values = [v[None] if v.ndim == 2 else v for v in values]
    shape = (sum(v.shape[0] for v in values),) + values[0].shape[1:]
    return kernel_call(join, [(shape, f32)], values, name="join", micros=0, order=order, early=early)[0]


def gate(*refs):
    half = len(refs) // 2
    for ref, out in zip(refs[:half], refs[half:]):
        out[...] = ref[...]


def choose_far(near, far, out):
    z, _, _, _ = here()
    inner = (z == 1) | (z == 2)
    for n in range(2):
        out[n] = jnp.where(inner, near[1 - n], far[n])


def head_forward(t0, t1, t2, t3, p0, p1, p2, p3, gain, w, omega,
                 keep, give, phq_o, phk_o, qk_o, v_o, mxd_o, doc_o, nt_o, low):
    z, c, _, _ = here()
    wh = jnp.concatenate([pick(w[:, pl.ds(pl.multiple_of(part * 512 + z * 128, 128), 128)], c) for part in range(3)], axis=1)
    g = gain[...]
    for k, (mine, theirs) in enumerate(((t0, p0), (t1, p1), (t2, p2), (t3, p3))):
        for ref, core in ((mine, c), (theirs, 1 - c)):
            chunk = 2 * jnp.bitwise_xor(z, k) + core
            n, _ = normalise(ref[0:128, :])
            low[pl.ds(pl.multiple_of(chunk * 128, 128), 128), :] = (n * g).astype(bf16)
            doc_o[pl.ds(chunk, 1), :] = ref[128:129, 0:128]
    rows, cols = doc_numbers(doc_o[...])
    nt_o[...] = jnp.transpose(low[:, pl.ds(pl.multiple_of(c * 256, 256), 256)])
    s = 64 ** -0.25
    om = omega[2 * z + c]
    oh = om.astype(bf16)
    ol = (om - oh.astype(f32)).astype(bf16)
    stack = jnp.concatenate([oh, oh, ol], axis=0)

    def feature(v):
        v = v * s
        hi = v.astype(bf16)
        lo = (v - hi.astype(f32)).astype(bf16)
        proj = nn(jnp.concatenate([hi, lo, hi], axis=1), stack)
        return jnp.exp(proj - 0.5 * jnp.sum(v * v, axis=-1, keepdims=True))

    for b in range(4):
        at = pl.ds(256 * b, 256)
        pr = nn(low[at, :], wh)
        qk_o[at, :] = pr[:, 0:128]
        v_o[at, :] = pr[:, 128:192].astype(bf16)
        phq_o[at, :] = feature(pr[:, 0:64]).astype(bf16)
        phk_o[at, :] = feature(pr[:, 64:128]).astype(bf16)
    for b in range(4):
        at = pl.ds(256 * b, 256)
        n = 256 * (b + 1)
        scores = nt(phq_o[at, :], phk_o[0:n, :])
        i = lax.broadcasted_iota(jnp.int32, (256, n), 0) + 256 * b
        j = lax.broadcasted_iota(jnp.int32, (256, n), 1)
        same = (col_of(cols, 2 * b, 2 * b + 2) == row_of(rows, 0, 2 * b + 2)) & (i >= j)
        scores = jnp.where(same, scores, 0.0)
        inv = 1.0 / jnp.sum(scores, axis=-1, keepdims=True)
        mixed = nn(scores.astype(bf16), v_o[0:n, :]) * inv
        mxd_o[at, :] = jnp.concatenate([mixed, jnp.broadcast_to(inv, (256, 64))], axis=1)
        top, bottom = mixed[0:128, :], mixed[128:256, :]
        keep[b] = jnp.where(c == 0, top, bottom)
        give[b] = jnp.where(c == 0, bottom, top)


def pack_pairs(keep, got, b0, b1, b2, b3):
    z, c, _, _ = here()
    for k, out in enumerate((b0, b1, b2, b3)):
        j = jnp.bitwise_xor(z, k)
        a, b = keep[j], got[j]
        out[...] = jnp.where(c == 0, jnp.concatenate([a, b], axis=1), jnp.concatenate([b, a], axis=1))


def unpack_pairs(b0, b1, b2, b3, keep, give):
    z, c, _, _ = here()
    for k, ref in enumerate((b0, b1, b2, b3)):
        j = jnp.bitwise_xor(z, k)
        a, b = ref[:, 0:64], ref[:, 64:128]
        keep[j] = jnp.where(c == 0, a, b)
        give[j] = jnp.where(c == 0, b, a)


def middle_part(b0, b1, b2, b3, tokens, wo, gain, mixed_o, middle_o, normed_o):
    z, _, _, _ = here()
    for k, ref in enumerate((b0, b1, b2, b3)):
        j = jnp.bitwise_xor(z, k)
        mixed_o[:, pl.ds(pl.multiple_of(j * 128, 128), 128)] = ref[...].astype(bf16)
    middle = tokens[...].astype(f32) + nn(mixed_o[...], wo[...])
    middle_o[...] = middle
    n, _ = normalise(middle)
    normed_o[...] = (n * gain[...]).astype(bf16).astype(f32)


def feed_forward(mixed, middle, normed, cot, wu, wd, wo, gain,
                 out_o, mg_o, ml_o, ex0, ex1, ex2, b0, b1, b2, b3, scr):
    z, c, _, _ = here()
    x = normed[...].astype(bf16)
    inc = cot[...]
    total = middle[...]
    back = jnp.zeros((128, 512), f32)
    for u in range(4):
        at = pl.ds(512 * u, 512)
        wub, wdb = wu[:, at], wd[at, :]
        up = nn(x, wub)
        cdf, pdf = gelu_parts(up)
        total = total + nn((up * cdf).astype(bf16), wdb)
        ug = ((cdf + up * pdf) * nt(inc, wdb)).astype(bf16)
        back = back + nt(ug, wub)
    out_o[...] = total.astype(bf16)
    n, inv = normalise(middle[...])
    mg = inc.astype(f32) + normalise_back(gain[...] * back, n, inv)
    mg_o[...] = mg
    low = mg.astype(bf16)
    ml_o[...] = low
    ex0[...] = mixed[:, pl.ds(pl.multiple_of((1 - c) * 256, 256), 256)].astype(f32)
    ex1[...] = low[:, 0:256].astype(f32)
    ex2[...] = low[:, 256:512].astype(f32)
    scr[...] = nt(low, wo[...])
    for k, ref in enumerate((b0, b1, b2, b3)):
        j = jnp.bitwise_xor(z, k)
        ref[...] = scr[:, pl.ds(pl.multiple_of(j * 128, 128), 128)]


def out_part(mixed, mlow, got0, got1, got2, keep, give, scr):
    _, c, first, _ = here()
    mine = mixed[:, pl.ds(pl.multiple_of(c * 256, 256), 256)].astype(f32)
    left = jnp.transpose(jnp.concatenate([mine, got0[...]], axis=0)).astype(bf16)
    theirs = jnp.concatenate([got1[...], got2[...]], axis=1).astype(bf16)
    right = jnp.concatenate([mlow[...], theirs], axis=0)
    scr[...] = nn(left, right)
    keep[...] = scr[pl.ds(pl.multiple_of(first * 128, 128), 128), :]
    give[...] = scr[pl.ds(pl.multiple_of((1 - first) * 128, 128), 128), :]


def add_last(mine, got, out):
    out[...] = (mine[...] + got[...]) * (1.0 / 32)


def join_pieces(p0, p1, p2, p3, out):
    z, _, _, _ = here()
    parts = (p0, p1, p2, p3)
    total = (p0[:, 384:896] + p1[:, 384:896]) + (p2[:, 384:896] + p3[:, 384:896])
    for k, ref in enumerate(parts):
        j = jnp.bitwise_xor(z, k)
        out[k, :, 0:384] = ref[:, 0:384]
        block = total[:, 0:128]
        for n in range(1, 4):
            block = jnp.where(j == n, total[:, 128 * n : 128 * n + 128], block)
        out[k, :, 384:512] = block


def head_backward(keep, got, phq, phk, qk, v, mxd, doc, omega, pg0, pg1, pg2, r_scr, m_scr, pg_o):
    z, c, _, _ = here()
    for b in range(4):
        a, g = keep[b], got[b]
        at = pl.ds(256 * b, 256)
        dm = jnp.concatenate([jnp.where(c == 0, a, g), jnp.where(c == 0, g, a)], axis=0)
        r = dm * mxd[at, 64:128]
        r_scr[at, :] = r.astype(bf16)
        m_scr[at, :] = r * mxd[at, 0:64]
    rows, cols = doc_numbers(doc[...])
    ones = jnp.ones((8, 64), f32)
    s = 64 ** -0.25
    om = omega[2 * z + c].astype(bf16)

    def feature_back(ph, grad, base):
        a = ph.astype(f32) * grad
        return s * nt(a.astype(bf16), om) - (s * s) * base * jnp.sum(a, axis=-1, keepdims=True)

    for b in range(4):
        at = pl.ds(256 * b, 256)
        n = 256 * (b + 1)
        i = lax.broadcasted_iota(jnp.int32, (256, n), 0) + 256 * b
        j = lax.broadcasted_iota(jnp.int32, (256, n), 1)
        same = (col_of(cols, 2 * b, 2 * b + 2) == row_of(rows, 0, 2 * b + 2)) & (i >= j)
        ds = nt(r_scr[at, :], v[0:n, :]) - jnp.sum(m_scr[at, :], axis=-1, keepdims=True)
        ds = jnp.where(same, ds, 0.0).astype(bf16)
        qg = feature_back(phq[at, :], nn(ds, phk[0:n, :]), qk[at, 0:64])
        m = 1024 - 256 * b
        later = pl.ds(256 * b, m)
        j2 = lax.broadcasted_iota(jnp.int32, (256, m), 0)
        i2 = lax.broadcasted_iota(jnp.int32, (256, m), 1)
        same2 = (col_of(cols, 2 * b, 2 * b + 2) == row_of(rows, 2 * b, 8)) & (i2 >= j2)
        scores = jnp.where(same2, nt(phk[at, :], phq[later, :]), 0.0).astype(bf16)
        vg = nn(scores, r_scr[later, :])
        mr = nt(ones, m_scr[later, :], lax.Precision.HIGHEST)[0:1, :]
        ds2 = jnp.where(same2, nt(v[at, :], r_scr[later, :]) - mr, 0.0).astype(bf16)
        kg = feature_back(phk[at, :], nn(ds2, phq[later, :]), qk[at, 64:128])
        rnd = lambda t: t.astype(bf16).astype(f32)
        pg_o[at, :] = rnd(jnp.concatenate([qg, kg], axis=1))
        pg_o[pl.ds(1024 + 256 * (b % 2), 256), 64 * (b // 2) : 64 * (b // 2) + 64] = rnd(vg)
    for n, out in enumerate((pg0, pg1, pg2)):
        out[...] = pg_o[512 * n : 512 * n + 512, :]


def weight_part(m0, m1, m2, t0, t1, t2, nt_low, okeep, ogive, q0, q1, q2, q3, keep, give, scr, g_scr):
    z, c, first, _ = here()
    for b in range(4):
        at = pl.ds(256 * b, 256)
        half = pl.ds(256 * (b % 2), 256)
        lanes = slice(64 * (b // 2), 64 * (b // 2) + 64)
        a, t = ((m0, t0), (m1, t1))[b // 2]
        a, t = a[half, :], t[half, :]
        av, tv = m2[half, lanes], t2[half, lanes]
        h0 = jnp.where(c == 0, a, t)
        h1 = jnp.where(c == 0, t, a)
        scr[at, 0:128] = jnp.concatenate([h0[:, 0:64], h1[:, 0:64]], axis=1)
        scr[at, 128:256] = jnp.concatenate([h0[:, 64:128], h1[:, 64:128]], axis=1)
        scr[at, 256:384] = jnp.concatenate([jnp.where(c == 0, av, tv), jnp.where(c == 0, tv, av)], axis=1)
    for k, ref in enumerate((q0, q1, q2, q3)):
        chunk = 2 * jnp.bitwise_xor(z, k) + c
        ref[...] = scr[pl.ds(pl.multiple_of(chunk * 128, 128), 128), :]
    g_scr[...] = nn(nt_low[...], scr[...].astype(bf16))
    keep[:, 0:384] = g_scr[pl.ds(pl.multiple_of(first * 128, 128), 128), :]
    give[:, 0:384] = g_scr[pl.ds(pl.multiple_of((1 - first) * 128, 128), 128), :]
    keep[:, 384:896] = okeep[...]
    give[:, 384:896] = ogive[...]


def tokens_part(q0, q1, q2, q3, mg, tokens, w, gain, out_o, scr):
    z, _, _, _ = here()
    for k, ref in enumerate((q0, q1, q2, q3)):
        j = jnp.bitwise_xor(z, k)
        for part in range(3):
            scr[:, pl.ds(pl.multiple_of(part * 512 + j * 128, 128), 128)] = ref[:, 128 * part : 128 * part + 128].astype(bf16)
    n, inv = normalise(tokens[...].astype(f32))
    e = gain[...] * nt(scr[...], w[...])
    out_o[...] = mg[...] + normalise_back(e, n, inv)


def add_split(mine, got, keep, give):
    _, _, _, second = here()
    a = pl.ds(pl.multiple_of(second * 64, 64), 64)
    b = pl.ds(pl.multiple_of((1 - second) * 64, 64), 64)
    keep[...] = mine[a, :] + got[a, :]
    give[...] = mine[b, :] + got[b, :]


def ffn_narrow(count, *refs):
    xs, cs, (xb, cb) = refs[:count], refs[count : 2 * count], refs[2 * count :]
    at = 0
    for x, cc in zip(xs, cs):
        for i in range(x.shape[0]):
            xb[pl.ds(at, 128), :] = x[i].astype(bf16)
            cb[pl.ds(at, 128), :] = cc[i].astype(bf16)
            at += 128


def ffn_weights(unit, mine, first, last, xb, cb, wu, wd, *refs):
    if not first:
        before, *refs = refs
    if last:
        theirs, out, up_o, gain_o = refs
    else:
        (out,) = refs
    _, c, _, _ = here()
    core = c if mine else 1 - c
    place = pl.ds(pl.multiple_of(core * 1024 + 256 * unit, 256), 256)
    wut, wdu = jnp.transpose(wu[:, place]), wd[place, :]
    x, inc = xb[...], cb[...]
    up = nt(wut, x)
    hg = nt(wdu, inc)
    cdf, pdf = gelu_parts(up)
    total_up = nn(((cdf + up * pdf) * hg).astype(bf16), x)
    total_down = nn((up * cdf).astype(bf16), inc)
    if not first:
        total_up = total_up + before[0:256, :]
        total_down = total_down + before[256:512, :]
    if last:
        total_up = (total_up + theirs[0:256, :]) * (1.0 / 32)
        total_down = (total_down + theirs[256:512, :]) * (1.0 / 32)
        up_o[...] = jnp.transpose(total_up)
        part = jnp.sum(total_up * wut.astype(f32), axis=0, keepdims=True)
        gain_o[...] = jnp.broadcast_to(part, (8, 512))
    out[0:256, :] = total_up
    out[256:512, :] = total_down


def place_mine(*refs):
    ups, both = refs[0:4], refs[4:8]
    up_o, down_o, sems = refs[8:]
    _, c, _, _ = here()
    copies = []
    for n in range(4):
        at = pl.ds(pl.multiple_of(c * 1024 + 256 * n, 256), 256)
        copies.append(pltpu.make_async_copy(ups[n], up_o.at[:, at], sems.at[2 * n]))
        copies.append(pltpu.make_async_copy(both[n].at[256:512, :], down_o.at[at, :], sems.at[2 * n + 1]))
    for copy in copies:
        copy.start()
    for copy in copies:
        copy.wait()


def place_theirs(b0, b1, b2, b3, up_in, down_in, up_o, down_o, ups, sems):
    _, c, _, _ = here()
    copies = []
    for n, both in enumerate((b0, b1, b2, b3)):
        at = pl.ds(pl.multiple_of((1 - c) * 1024 + 256 * n, 256), 256)
        copies.append(pltpu.make_async_copy(both.at[256:512, :], down_o.at[at, :], sems.at[2 * n]))
        copies[-1].start()
    for n, both in enumerate((b0, b1, b2, b3)):
        at = pl.ds(pl.multiple_of((1 - c) * 1024 + 256 * n, 256), 256)
        ups[n] = jnp.transpose(both[0:256, :])
        copies.append(pltpu.make_async_copy(ups.at[n], up_o.at[:, at], sems.at[2 * n + 1]))
        copies[-1].start()
    for copy in copies:
        copy.wait()


def add_gains(g0, g1, g2, g3, other, gain2, out):
    total = (g0[...] + g1[...]) + (g2[...] + g3[...])
    out[...] = (total[0:1, :] + other[0:1, :]) / gain2[...]


def sum_gains(g0, g1, g2, g3, out):
    out[...] = (g0[...] + g1[...]) + (g2[...] + g3[...])


def finish(a, b, ca, cb, w, gain, qkv_o, out_o, gain_o):
    z, c, first, second = here()
    for n in range(4):
        for core, ref, r1, r2 in ((c, (a, b)[n // 2], first, second), (1 - c, (ca, cb)[n // 2], second, first)):
            row = core * 256 + jnp.bitwise_xor(r1, n % 2) * 128 + jnp.bitwise_xor(r2, n // 2) * 64
            rows = pl.ds(pl.multiple_of(row, 64), 64)
            for k in range(4):
                j = jnp.bitwise_xor(z, k)
                piece = ref.at[4 * (n % 2) + k]
                for part in range(3):
                    at = pl.ds(pl.multiple_of(part * 512 + j * 128, 128), 128)
                    qkv_o[rows, at] = piece[:, 128 * part : 128 * part + 128]
                out_o[rows, pl.ds(pl.multiple_of(j * 128, 128), 128)] = piece[:, 384:512]
    for r in range(4):
        rows = pl.ds(128 * r, 128)
        acc = jnp.zeros((128, 128), f32)
        for j in range(12):
            lanes = pl.ds(128 * j, 128)
            acc = acc + w[rows, lanes].astype(f32) * qkv_o[rows, lanes]
        lanes = pl.ds(128 * r, 128)
        gain_o[0:1, lanes] = jnp.sum(jnp.transpose(acc), axis=0, keepdims=True) / gain[0:1, lanes]


def across(values):
    return [send(v, CORES) for v in values]


def local_fast(tokens, doc_start, norm1_gain, qkv_weight, out_weight, norm2_gain, up_weight, down_weight, omega, cotangent):
    g1, g2 = norm1_gain.reshape(1, 512), norm2_gain.reshape(1, 512)
    tok, cot = tokens[0], cotangent[0]
    order = []
    call = functools.partial(kernel_call, order=order)
    join = functools.partial(joined, order)
    block = ((128, 128), f32)

    def later(*values):
        return call(gate, [(v.shape, v.dtype) for v in values], values, name="gate", micros=0)

    def wait(*values):
        call(gate, [], [], name="gate", micros=0, early=values)

    def pause(micros):
        call(gate, [], [], name="pause", micros=micros)

    def narrow(xs, cs):
        rows = 128 * sum(v.shape[0] for v in xs)
        return call(functools.partial(ffn_narrow, len(xs)), [((rows, 512), bf16)] * 2, [*xs, *cs], name="ffn_narrow", micros=0)

    def ffn(unit, mine, xc, before=None, theirs=None, micros=0):
        first, last = before is None, theirs is not None
        outs = [((512, 512), f32)] + ([((512, 256), f32), ((8, 512), f32)] if last else [])
        more = ([] if first else [before]) + ([theirs] if last else [])
        got = call(
            functools.partial(ffn_weights, unit, mine, first, last), outs, [*xc, up_weight, down_weight, *more],
            (), "ffn_weights", micros, 24,
        )
        return got if last else got[0]

    message, cot_wide = call(prepare, [((136, 512), f32), ((128, 512), f32)], [tok, doc_start, cot], name="prepare")
    t = [message] + [send(message, ALONG_Z[k], "tok") for k in (1, 2, 3)]
    ca = join(cot_wide, send(cot_wide, ALONG_Z[1], "c1"), early=t)
    p = [send(v, CORES, "tok") for v in t]
    ca_first = send(ca, FIRST, "ca")
    keep, give, phq, phk, qk, v, mxd, doc, nt_low = call(
        head_forward,
        [((4, 128, 64), f32), ((4, 128, 64), f32), ((1024, 256), bf16), ((1024, 256), bf16), ((1024, 128), f32),
         ((1024, 64), bf16), ((1024, 128), f32), ((8, 128), f32), ((256, 1024), bf16)],
        [*t, *p, g1, qkv_weight, omega], [pltpu.VMEM((1024, 512), bf16)], "head_forward", 2,
    )
    b = call(pack_pairs, [block] * 4, [keep, send(give, CORES, "give")], name="pack_pairs", micros=0)
    b = [b[0]] + [send(b[k], ALONG_Z[k], "mixed") for k in (1, 2, 3)]
    pause(0.8)
    ca_two = join(ca, ca_first)
    ca_other = send(ca_two, SECOND, "ca")
    mixed, middle, normed = call(
        middle_part, [((128, 512), bf16), ((128, 512), f32), ((128, 512), f32)], [*b, tok, out_weight, g2],
        name="middle_part", micros=2.5,
    )
    x1 = send(normed, ALONG_Z[1], "x1")
    output, mg, mlow, ex0, ex1, ex2, *b = call(
        feed_forward,
        [((128, 512), bf16), ((128, 512), f32), ((128, 512), bf16)] + [((128, 256), f32)] * 3 + [block] * 4,
        [mixed, middle, normed, cot, up_weight, down_weight, out_weight, g2], [pltpu.VMEM((128, 512), f32)],
        "feed_forward", 1.2, out=(0,),
    )
    b = [b[0]] + [send(b[k], ALONG_Z[k], "mg") for k in (1, 2, 3)]
    ex_other = [send(w, CORES, "ex") for w in (ex0, ex1, ex2)]
    pause(1.5)
    okeep, ogive = call(out_part, [((128, 512), f32)] * 2, [mixed, mlow, *ex_other],
                        [pltpu.VMEM((256, 512), f32)], "out_part", micros=0)
    xa = join(normed, x1)
    xa_first = send(xa, FIRST, "xa")
    c_inner = send(later(ca)[0], INNER, "c")
    keep, give = call(unpack_pairs, [((4, 128, 64), f32)] * 2, b, name="unpack_pairs", micros=0)
    got = send(give, CORES, "give")
    pg = call(
        head_backward, [((512, 128), f32)] * 3, [keep, got, phq, phk, qk, v, mxd, doc, omega],
        [pltpu.VMEM((1024, 64), bf16), pltpu.VMEM((1024, 64), f32), pltpu.VMEM((1536, 128), f32)], "head_backward", 4,
    )
    pg_other = [send(w, CORES, "pg") for w in pg]
    c_a = later(ca_two, ca_other)
    c_inner, xa_late = later(c_inner, xa)
    c_outer = send(c_inner, OUTWARD, "c")
    x_inner = send(xa_late, INNER, "x")
    xa_two = join(xa, xa_first)
    xa_other = send(xa_two, SECOND, "xa")
    *q, keep, give = call(
        weight_part, [((128, 384), f32)] * 4 + [((128, 896), f32)] * 2, [*pg, *pg_other, nt_low, okeep, ogive],
        [pltpu.VMEM((1024, 384), f32), pltpu.VMEM((256, 384), f32)], "weight_part", micros=0,
    )
    got = send(give, FIRST, "rs")
    pause(4.7)
    (cb,) = call(choose_far, [((2, 128, 512), f32)], [c_inner, c_outer], name="choose_far", micros=0)
    cb_first = send(cb, FIRST, "cb")
    (x_inner,) = later(x_inner)
    x_outer = send(x_inner, OUTWARD, "x")
    keep, give = call(add_split, [((64, 896), f32)] * 2, [keep, got], name="add_split", micros=0)
    got = send(give, SECOND, "rs")
    pause(5.5)
    x_a = later(xa_two, xa_other)
    x_now = narrow(x_a, c_a)
    total = {}
    for u in range(4):
        total[u, False] = ffn(u, False, x_now, micros=0.7)
    cb_two = join(cb, cb_first)
    cb_other = send(cb_two, SECOND, "cb")
    for u in range(4):
        total[u, True] = ffn(u, True, x_now, micros=1.3)
    (piece,) = call(add_last, [((64, 896), f32)], [keep, got], name="add_last", micros=0)
    piece_line = [send(piece, ALONG_Z[k], "piece") for k in (1, 2, 3)]
    (xb,) = call(choose_far, [((2, 128, 512), f32)], [x_inner, x_outer], name="choose_far", micros=0)
    xb_first = send(xb, FIRST, "xb")
    pause(5.3)
    xb_two = join(xb, xb_first)
    xb_other = send(xb_two, SECOND, "xb")
    (pieces,) = call(join_pieces, [((4, 64, 512), f32)], [piece, *piece_line], name="join_pieces", micros=0)
    pieces_first = send(pieces, FIRST, "piece")
    c_b = later(cb_two, cb_other)
    q = [q[0]] + [send(w, ALONG_Z[k], "q") for k, w in zip((1, 2, 3), later(*q[1:]))]
    pause(5.3)
    pieces = [join(pieces, pieces_first)]
    pieces.append(send(pieces[0], SECOND, "piece"))
    pause(5.2)
    (tokens_grad,) = call(
        tokens_part, [((128, 512), f32)], [*q, mg, tok, qkv_weight, g1], [pltpu.VMEM((128, 1536), bf16)],
        "tokens_part", micros=0, out=(0,),
    )
    x_b = later(xb_two, xb_other)
    x_now = narrow(x_b, c_b)
    others = [send(ffn(u, False, x_now, total[u, False], micros=2.8), CORES, "part") for u in range(4)]
    both, ups, gains = zip(*[ffn(u, True, x_now, total[u, True], others[u], micros=2.8) for u in range(4)])
    both_other = [send(w, CORES, "both") for w in both]
    (gain,) = call(sum_gains, [((8, 512), f32)], gains, name="sum_gains", micros=0)
    gain_other = send(gain, CORES, "gain")
    dma = [pltpu.SemaphoreType.DMA((8,))]
    up_grad, down_grad = call(
        place_mine, [((512, 2048), f32), ((2048, 512), f32)], [*ups, *both], dma, "place_mine", 2, far=(0, 1),
    )
    qkv_grad, out_grad, norm1_grad = call(
        finish, [((512, 1536), f32), ((512, 512), f32), ((1, 512), f32)],
        [*pieces, *[send(w, CORES, "piece") for w in pieces], qkv_weight, g1], (), "finish", 3, out=(0, 1),
    )
    (norm2_grad,) = call(add_gains, [((1, 512), f32)], [*gains, gain_other, g2], name="add_gains", micros=0)
    up_grad, down_grad = call(
        place_theirs, [((512, 2048), f32), ((2048, 512), f32)], both_other, [pltpu.VMEM((4, 512, 256), f32), *dma],
        "place_theirs", 2, far=(0, 1), onto=(up_grad, down_grad),
    )
    return (output[None], tokens_grad[None], norm1_grad[0], qkv_grad, out_grad, norm2_grad[0], up_grad, down_grad)


def solution(mesh):
    placed = (
        P("dp", "seq", None),
        P("dp", "seq"),
        P(),
        P(),
        P(),
        P(),
        P(),
        P(),
        P(),
        P("dp", "seq", None),
    )
    fits = mesh.shape["dp"] == GRID_DP and mesh.shape["seq"] == GRID_SEQ
    return jax.shard_map(
        local_fast if fits else local,
        mesh=mesh,
        in_specs=placed,
        out_specs=(P("dp", "seq", None), P("dp", "seq", None), P(), P(), P(), P(), P(), P()),
        check_vma=False,
    )
```

```python
import functools

import jax
import jax.numpy as jnp
from jax import lax
from jax.experimental import pallas as pl
from jax.experimental.pallas import tpu as pltpu
from jax.sharding import PartitionSpec as P

norm_eps = 1e-05
highest_precision = lax.Precision.HIGHEST


def entering(value, axis, join, neutral, backward):
    count, mine = (lax.axis_size(axis), lax.axis_index(axis))
    pieces = jax.tree.map(lambda part: lax.all_gather(part, axis), value)
    if backward:
        pieces = jax.tree.map(lambda part: part[::-1], pieces)
        mine = count - 1 - mine
    running = jax.tree.map(
        lambda part, zero: jnp.full_like(part, 0) + jnp.asarray(zero, part.dtype), value, neutral
    )

    def hop(position, running):
        longer = join(running, jax.tree.map(lambda part: part[position], pieces))
        return jax.tree.map(lambda new, old: jnp.where(position < mine, new, old), longer, running)

    return lax.fori_loop(0, count - 1, hop, running)


def layer_norm(values, gain):
    average = jnp.mean(values, axis=-1, keepdims=True)
    centred = values - average
    spread_sq = jnp.mean(centred * centred, axis=-1, keepdims=True)
    return centred * lax.rsqrt(spread_sq + norm_eps) * gain


def features(head_values, omega):
    width_dim = head_values.shape[-1]
    scaled = head_values * width_dim ** (-0.25)
    projection = jnp.einsum("...hd,hdm->...hm", scaled, omega, precision=highest_precision)
    half_square = 0.5 * jnp.sum(scaled * scaled, axis=-1, keepdims=True)
    return jnp.exp(projection - half_square)


def exact_gelu(values):
    return jax.nn.gelu(values, approximate=False)


def row_masks(doc_start):
    stretch_len = doc_start.shape[1]
    doc_index = jnp.cumsum(doc_start, axis=1)
    position = jnp.arange(stretch_len, dtype=jnp.int32)
    same_doc = (doc_index[:, :, None] == doc_index[:, None, :]) & (
        position[None, :, None] >= position[None, None, :]
    )
    leading_document = (doc_index == 0).astype(jnp.float32)
    last_doc = (doc_index == doc_index[:, -1:]).astype(jnp.float32)
    document_marker = (doc_index[:, -1] > 0).astype(jnp.float32)
    return (same_doc.astype(jnp.float32), leading_document, last_doc, document_marker)


def mix_rows(
    query_features, key_feat, value_heads, running_state, carry_norm, same_doc, leading_document
):
    scores = (
        jnp.einsum("rihm,rjhm->rhij", query_features, key_feat, precision=highest_precision)
        * same_doc[:, None]
    )
    attention_numerator = jnp.einsum(
        "rhij,rjhd->rihd", scores, value_heads, precision=highest_precision
    )
    attention_numerator = attention_numerator + leading_document[:, :, None, None] * jnp.einsum(
        "rihm,rhmd->rihd", query_features, running_state, precision=highest_precision
    )
    denominator = jnp.transpose(jnp.sum(scores, axis=-1), (0, 2, 1))
    denominator = denominator + leading_document[:, :, None] * jnp.einsum(
        "rihm,rhm->rih", query_features, carry_norm, precision=highest_precision
    )
    return attention_numerator / denominator[..., None]


def stretch_totals(key_feat, value_heads, last_doc):
    key_masked_rows = key_feat * last_doc[:, :, None, None]
    state_sum = jnp.einsum(
        "rchm,rchd->rhmd", key_masked_rows, value_heads, precision=highest_precision
    )
    return (state_sum, jnp.sum(key_masked_rows, axis=1))


def carry_on(earlier, later):
    state_sum, norm_sum, document_marker = later
    pass_on = 1.0 - document_marker
    return (
        state_sum + pass_on[:, None, None, None] * earlier[0],
        norm_sum + pass_on[:, None, None] * earlier[1],
        jnp.maximum(earlier[2], document_marker),
    )


def local(
    tokens,
    doc_start,
    norm1_gain,
    qkv_weight,
    out_weight,
    norm2_gain,
    up_weight,
    down_weight,
    omega,
    cotangent,
):
    row_count, stretch_len, model_width = tokens.shape
    head_count = omega.shape[0]
    head_dim = omega.shape[1]
    token_count = row_count * stretch_len
    stream = tokens.astype(jnp.float32).reshape(token_count, model_width)
    same_doc, leading_document, last_doc, document_marker = row_masks(doc_start)
    normed_one, norm1_back = jax.vjp(layer_norm, stream, norm1_gain)
    normed_one_low = normed_one.astype(jnp.bfloat16)
    projected = jnp.dot(normed_one_low, qkv_weight, preferred_element_type=jnp.float32)
    head_split = projected.reshape(row_count, stretch_len, 3, head_count, head_dim)
    query_heads = head_split[:, :, 0]
    key_heads = head_split[:, :, 1]
    value_heads = head_split[:, :, 2]

    def both_features(query_part, key_part):
        return (features(query_part, omega), features(key_part, omega))

    (query_features, key_feat), feature_back = jax.vjp(both_features, query_heads, key_heads)

    def local_totals(key_part, value_part):
        return stretch_totals(key_part, value_part, last_doc)

    (state_sum, norm_sum), totals_back = jax.vjp(local_totals, key_feat, value_heads)
    empty_state = jnp.zeros_like(state_sum)
    empty_norm = jnp.zeros_like(norm_sum)
    empty_flag = jnp.zeros_like(document_marker)
    running_state, carry_norm, unused_flag = entering(
        (state_sum, norm_sum, document_marker),
        "seq",
        carry_on,
        (empty_state, empty_norm, empty_flag),
        False,
    )

    def local_mix(query_part, key_part, value_part, state_part, norm_part):
        return mix_rows(
            query_part, key_part, value_part, state_part, norm_part, same_doc, leading_document
        )

    mixed, mix_back = jax.vjp(
        local_mix, query_features, key_feat, value_heads, running_state, carry_norm
    )
    mixed_low = mixed.reshape(token_count, model_width).astype(jnp.bfloat16)
    branch = jnp.dot(mixed_low, out_weight, preferred_element_type=jnp.float32)
    middle = stream + branch
    normed_two, norm2_back = jax.vjp(layer_norm, middle, norm2_gain)
    normed_two_low = normed_two.astype(jnp.bfloat16)
    up_values = jnp.dot(normed_two_low, up_weight, preferred_element_type=jnp.float32)
    gelu_out, gelu_back = jax.vjp(exact_gelu, up_values)
    hidden = gelu_out.astype(jnp.bfloat16)
    ffn_out = jnp.dot(hidden, down_weight, preferred_element_type=jnp.float32)
    output = (middle + ffn_out).astype(jnp.bfloat16).reshape(row_count, stretch_len, model_width)
    incoming = cotangent.reshape(token_count, model_width)
    down_grad = jnp.einsum("tf,td->fd", hidden, incoming, preferred_element_type=jnp.float32)
    hidden_grad = jnp.einsum("td,fd->tf", incoming, down_weight, preferred_element_type=jnp.float32)
    (up_full,) = gelu_back(hidden_grad)
    up_grad_low = up_full.astype(jnp.bfloat16)
    up_grad = jnp.einsum(
        "td,tf->df", normed_two_low, up_grad_low, preferred_element_type=jnp.float32
    )
    normed_two_grad = jnp.einsum(
        "tf,df->td", up_grad_low, up_weight, preferred_element_type=jnp.float32
    )
    middle_part, norm2_grad = norm2_back(normed_two_grad)
    middle_grad = incoming.astype(jnp.float32) + middle_part
    middle_low = middle_grad.astype(jnp.bfloat16)
    out_grad = jnp.einsum("td,te->de", mixed_low, middle_low, preferred_element_type=jnp.float32)
    mixed_grad = jnp.einsum("te,de->td", middle_low, out_weight, preferred_element_type=jnp.float32)
    mixed_grad = mixed_grad.reshape(row_count, stretch_len, head_count, head_dim)
    query_feat_grad, key_feat_mix, value_mix, carry_state_grad, carry_norm_grad = mix_back(
        mixed_grad
    )
    later_state, later_norm, unused_later = entering(
        (carry_state_grad, carry_norm_grad, document_marker),
        "seq",
        carry_on,
        (empty_state, empty_norm, empty_flag),
        True,
    )
    key_feat_tot, value_tot = totals_back((later_state, later_norm))
    query_grad, key_grad = feature_back((query_feat_grad, key_feat_mix + key_feat_tot))
    value_grad = value_mix + value_tot
    projected_grad = jnp.stack((query_grad, key_grad, value_grad), axis=2)
    projected_grad = projected_grad.reshape(token_count, 3 * model_width).astype(jnp.bfloat16)
    qkv_grad = jnp.einsum(
        "td,te->de", normed_one_low, projected_grad, preferred_element_type=jnp.float32
    )
    normed_one_grad = jnp.einsum(
        "te,de->td", projected_grad, qkv_weight, preferred_element_type=jnp.float32
    )
    stream_part, norm1_grad = norm1_back(normed_one_grad)
    tokens_grad = (middle_grad + stream_part).reshape(row_count, stretch_len, model_width)
    device_count = lax.axis_size("dp") * lax.axis_size("seq")
    qkv_sum, out_sum, up_sum, down_sum, norm1_sum, norm2_sum = lax.psum(
        (qkv_grad, out_grad, up_grad, down_grad, norm1_grad, norm2_grad), ("dp", "seq")
    )
    return (
        output,
        tokens_grad,
        norm1_sum / device_count,
        qkv_sum / device_count,
        out_sum / device_count,
        norm2_sum / device_count,
        up_sum / device_count,
        down_sum / device_count,
    )


eps = 1e-05
f32 = jnp.float32
bf16 = jnp.bfloat16
AXES = ("dp", "seq")
GRID_DP, GRID_SEQ = 4, 8
ROOM = 56 * 2**20


def place(y, x, z, c):
    return (y * 2 + x) * GRID_SEQ + z * 2 + c


def pairs(move):
    return [
        (place(y, x, z, c), place(*move(y, x, z, c)))
        for y in range(2)
        for x in range(2)
        for z in range(4)
        for c in range(2)
    ]


INNER = pairs(lambda y, x, z, c: (y, x, 3 - z, c))
INNER = [(a, b) for a, b in INNER if (a % GRID_SEQ) // 2 in (1, 2)]
OUTWARD = pairs(lambda y, x, z, c: (y, x, z ^ 1, c))
OUTWARD = [(a, b) for a, b in OUTWARD if (a % GRID_SEQ) // 2 in (1, 2)]
ALONG_Z = {k: pairs(lambda y, x, z, c, k=k: (y, x, z ^ k, c)) for k in (1, 2, 3)}
CORES = pairs(lambda y, x, z, c: (y, x, z, 1 - c))
FIRST = pairs(lambda y, x, z, c: (y, 1 - x, z, c) if c == 0 else (1 - y, x, z, c))
SECOND = pairs(lambda y, x, z, c: (1 - y, x, z, c) if c == 0 else (y, 1 - x, z, c))


def send(value, perm, tag="send"):
    with jax.named_scope("t_" + tag):
        return lax.ppermute(value, AXES, perm)


def nn(a, b, precision=None):
    return lax.dot_general(
        a, b, (((1,), (0,)), ((), ())), precision=precision, preferred_element_type=f32
    )


def nt(a, b, precision=None):
    return lax.dot_general(
        a, b, (((1,), (1,)), ((), ())), precision=precision, preferred_element_type=f32
    )


def work(micros):
    return pl.CostEstimate(flops=int(micros * 1.16e9), bytes_accessed=0, transcendentals=0)


def here():
    dp, seq = lax.axis_index("dp"), lax.axis_index("seq")
    y, x, z, c = dp // 2, dp % 2, seq // 2, seq % 2
    return z, c, jnp.where(c == 0, x, y), jnp.where(c == 0, y, x)


def kernel_call(body, outs, args, scratch=(), name=None, micros=2, room=16, far=(), out=(), order=None, early=(), onto=()):
    vmem = pl.BlockSpec(memory_space=pltpu.VMEM)
    args = list(args)
    staged = len(args)
    args += list(onto)
    held = len(args)
    args += list(early) + list(order or ())
    ignored = len(args) - held
    outs = [*outs, ((8, 128), f32)]
    shapes = [
        jax.ShapeDtypeStruct(s, d) if n in far or n in out else pltpu.VMEM(s, d) for n, (s, d) in enumerate(outs)
    ]
    specs = [pl.BlockSpec(memory_space=pl.ANY) if n in far else vmem for n in range(len(outs))]
    results = len(outs) - 1

    def whole(*refs):
        refs, mark, rest = refs[: held + ignored + results], refs[held + ignored + results], refs[held + ignored + results + 1 :]
        mark[...] = jnp.zeros((8, 128), f32)
        body(*refs[:held], *refs[held + ignored :], *rest)

    *values, mark = pl.pallas_call(
        whole,
        out_shape=shapes,
        in_specs=[pl.BlockSpec(memory_space=pl.ANY) if staged <= n < held else vmem for n in range(len(args))],
        out_specs=specs,
        scratch_shapes=list(scratch),
        input_output_aliases={staged + n: n for n in range(len(onto))},
        compiler_params=pltpu.CompilerParams(vmem_limit_bytes=room * 2**20),
        name=name,
        cost_estimate=work(micros),
    )(*[a if staged <= n < held else pltpu.with_memory_space_constraint(a, pltpu.VMEM) for n, a in enumerate(args)])
    if order is not None:
        order[:] = [mark]
    return values


def pick(v, bit):
    return jnp.where(bit == 0, v[:, 0:64], v[:, 64:128])


def normalise(v):
    mean = jnp.mean(v, axis=-1, keepdims=True)
    centred = v - mean
    inv = lax.rsqrt(jnp.mean(centred * centred, axis=-1, keepdims=True) + eps)
    return centred * inv, inv


def normalise_back(e, n, inv):
    return (e - jnp.mean(e, axis=-1, keepdims=True) - n * jnp.mean(e * n, axis=-1, keepdims=True)) * inv


def doc_numbers(doc):
    at = lax.broadcasted_iota(jnp.int32, (128, 128), 0)
    to = lax.broadcasted_iota(jnp.int32, (128, 128), 1)
    upper = (at <= to).astype(f32)
    a8 = lax.broadcasted_iota(jnp.int32, (8, 8), 0)
    t8 = lax.broadcasted_iota(jnp.int32, (8, 8), 1)
    before = (t8 < a8).astype(f32)
    spread = jnp.broadcast_to(jnp.sum(doc, axis=1, keepdims=True), (8, 128))
    high = lax.Precision.HIGHEST
    rows = nn(doc, upper, high) + nn(before, spread, high)
    eye = (at == to).astype(f32)
    cols = nt(eye, rows, high)
    return rows, cols


def row_of(rows, lo, hi):
    return jnp.concatenate([rows[j : j + 1, :] for j in range(lo, hi)], axis=1)


def col_of(cols, lo, hi):
    return jnp.concatenate([cols[:, j : j + 1] for j in range(lo, hi)], axis=0)


def gelu_parts(u):
    return 0.5 + 0.5 * lax.erf(u * 0.7071067811865476), jnp.exp(-0.5 * u * u) * 0.3989422804014327


def prepare(tokens, doc, cot, message, cot_o):
    message[0:128, :] = tokens[...].astype(f32)
    message[128:136, :] = jnp.zeros((8, 512), f32)
    message[128:129, 0:128] = doc[...].astype(f32)
    cot_o[...] = cot[...].astype(f32)


def join(*refs):
    at = 0
    out = refs[-1]
    for ref in refs[:-1]:
        out[at : at + ref.shape[0]] = ref[...]
        at += ref.shape[0]


def joined(order, *values, early=()):
    values = [v[None] if v.ndim == 2 else v for v in values]
    shape = (sum(v.shape[0] for v in values),) + values[0].shape[1:]
    return kernel_call(join, [(shape, f32)], values, name="join", micros=0, order=order, early=early)[0]


def gate(*refs):
    half = len(refs) // 2
    for ref, out in zip(refs[:half], refs[half:]):
        out[...] = ref[...]


def choose_far(near, far, out):
    z, _, _, _ = here()
    inner = (z == 1) | (z == 2)
    for n in range(2):
        out[n] = jnp.where(inner, near[1 - n], far[n])


def head_forward(t0, t1, t2, t3, p0, p1, p2, p3, gain, w, omega,
                 keep, give, phq_o, phk_o, qk_o, v_o, mxd_o, doc_o, nt_o, low):
    z, c, _, _ = here()
    wh = jnp.concatenate([pick(w[:, pl.ds(pl.multiple_of(part * 512 + z * 128, 128), 128)], c) for part in range(3)], axis=1)
    g = gain[...]
    for k, (mine, theirs) in enumerate(((t0, p0), (t1, p1), (t2, p2), (t3, p3))):
        for ref, core in ((mine, c), (theirs, 1 - c)):
            chunk = 2 * jnp.bitwise_xor(z, k) + core
            n, _ = normalise(ref[0:128, :])
            low[pl.ds(pl.multiple_of(chunk * 128, 128), 128), :] = (n * g).astype(bf16)
            doc_o[pl.ds(chunk, 1), :] = ref[128:129, 0:128]
    rows, cols = doc_numbers(doc_o[...])
    nt_o[...] = jnp.transpose(low[:, pl.ds(pl.multiple_of(c * 256, 256), 256)])
    s = 64 ** -0.25
    om = omega[2 * z + c]
    oh = om.astype(bf16)
    ol = (om - oh.astype(f32)).astype(bf16)
    stack = jnp.concatenate([oh, oh, ol], axis=0)

    def feature(v):
        v = v * s
        hi = v.astype(bf16)
        lo = (v - hi.astype(f32)).astype(bf16)
        proj = nn(jnp.concatenate([hi, lo, hi], axis=1), stack)
        return jnp.exp(proj - 0.5 * jnp.sum(v * v, axis=-1, keepdims=True))

    for b in range(4):
        at = pl.ds(256 * b, 256)
        pr = nn(low[at, :], wh)
        qk_o[at, :] = pr[:, 0:128]
        v_o[at, :] = pr[:, 128:192].astype(bf16)
        phq_o[at, :] = feature(pr[:, 0:64]).astype(bf16)
        phk_o[at, :] = feature(pr[:, 64:128]).astype(bf16)
    for b in range(4):
        at = pl.ds(256 * b, 256)
        n = 256 * (b + 1)
        scores = nt(phq_o[at, :], phk_o[0:n, :])
        i = lax.broadcasted_iota(jnp.int32, (256, n), 0) + 256 * b
        j = lax.broadcasted_iota(jnp.int32, (256, n), 1)
        same = (col_of(cols, 2 * b, 2 * b + 2) == row_of(rows, 0, 2 * b + 2)) & (i >= j)
        scores = jnp.where(same, scores, 0.0)
        inv = 1.0 / jnp.sum(scores, axis=-1, keepdims=True)
        mixed = nn(scores.astype(bf16), v_o[0:n, :]) * inv
        mxd_o[at, :] = jnp.concatenate([mixed, jnp.broadcast_to(inv, (256, 64))], axis=1)
        top, bottom = mixed[0:128, :], mixed[128:256, :]
        keep[b] = jnp.where(c == 0, top, bottom)
        give[b] = jnp.where(c == 0, bottom, top)


def pack_pairs(keep, got, b0, b1, b2, b3):
    z, c, _, _ = here()
    for k, out in enumerate((b0, b1, b2, b3)):
        j = jnp.bitwise_xor(z, k)
        a, b = keep[j], got[j]
        out[...] = jnp.where(c == 0, jnp.concatenate([a, b], axis=1), jnp.concatenate([b, a], axis=1))


def unpack_pairs(b0, b1, b2, b3, keep, give):
    z, c, _, _ = here()
    for k, ref in enumerate((b0, b1, b2, b3)):
        j = jnp.bitwise_xor(z, k)
        a, b = ref[:, 0:64], ref[:, 64:128]
        keep[j] = jnp.where(c == 0, a, b)
        give[j] = jnp.where(c == 0, b, a)


def middle_part(b0, b1, b2, b3, tokens, wo, gain, mixed_o, middle_o, normed_o):
    z, _, _, _ = here()
    for k, ref in enumerate((b0, b1, b2, b3)):
        j = jnp.bitwise_xor(z, k)
        mixed_o[:, pl.ds(pl.multiple_of(j * 128, 128), 128)] = ref[...].astype(bf16)
    middle = tokens[...].astype(f32) + nn(mixed_o[...], wo[...])
    middle_o[...] = middle
    n, _ = normalise(middle)
    normed_o[...] = (n * gain[...]).astype(bf16).astype(f32)


def feed_forward(mixed, middle, normed, cot, wu, wd, wo, gain,
                 out_o, mg_o, ml_o, ex0, ex1, ex2, b0, b1, b2, b3, scr):
    z, c, _, _ = here()
    x = normed[...].astype(bf16)
    inc = cot[...]
    total = middle[...]
    back = jnp.zeros((128, 512), f32)
    for u in range(4):
        at = pl.ds(512 * u, 512)
        wub, wdb = wu[:, at], wd[at, :]
        up = nn(x, wub)
        cdf, pdf = gelu_parts(up)
        total = total + nn((up * cdf).astype(bf16), wdb)
        ug = ((cdf + up * pdf) * nt(inc, wdb)).astype(bf16)
        back = back + nt(ug, wub)
    out_o[...] = total.astype(bf16)
    n, inv = normalise(middle[...])
    mg = inc.astype(f32) + normalise_back(gain[...] * back, n, inv)
    mg_o[...] = mg
    low = mg.astype(bf16)
    ml_o[...] = low
    ex0[...] = mixed[:, pl.ds(pl.multiple_of((1 - c) * 256, 256), 256)].astype(f32)
    ex1[...] = low[:, 0:256].astype(f32)
    ex2[...] = low[:, 256:512].astype(f32)
    scr[...] = nt(low, wo[...])
    for k, ref in enumerate((b0, b1, b2, b3)):
        j = jnp.bitwise_xor(z, k)
        ref[...] = scr[:, pl.ds(pl.multiple_of(j * 128, 128), 128)]


def out_part(mixed, mlow, got0, got1, got2, keep, give, scr):
    _, c, first, _ = here()
    mine = mixed[:, pl.ds(pl.multiple_of(c * 256, 256), 256)].astype(f32)
    left = jnp.transpose(jnp.concatenate([mine, got0[...]], axis=0)).astype(bf16)
    theirs = jnp.concatenate([got1[...], got2[...]], axis=1).astype(bf16)
    right = jnp.concatenate([mlow[...], theirs], axis=0)
    scr[...] = nn(left, right)
    keep[...] = scr[pl.ds(pl.multiple_of(first * 128, 128), 128), :]
    give[...] = scr[pl.ds(pl.multiple_of((1 - first) * 128, 128), 128), :]


def add_last(mine, got, out):
    out[...] = (mine[...] + got[...]) * (1.0 / 32)


def join_pieces(p0, p1, p2, p3, out):
    z, _, _, _ = here()
    parts = (p0, p1, p2, p3)
    total = (p0[:, 384:896] + p1[:, 384:896]) + (p2[:, 384:896] + p3[:, 384:896])
    for k, ref in enumerate(parts):
        j = jnp.bitwise_xor(z, k)
        out[k, :, 0:384] = ref[:, 0:384]
        block = total[:, 0:128]
        for n in range(1, 4):
            block = jnp.where(j == n, total[:, 128 * n : 128 * n + 128], block)
        out[k, :, 384:512] = block


def head_backward(keep, got, phq, phk, qk, v, mxd, doc, omega, pg0, pg1, pg2, r_scr, m_scr, pg_o):
    z, c, _, _ = here()
    for b in range(4):
        a, g = keep[b], got[b]
        at = pl.ds(256 * b, 256)
        dm = jnp.concatenate([jnp.where(c == 0, a, g), jnp.where(c == 0, g, a)], axis=0)
        r = dm * mxd[at, 64:128]
        r_scr[at, :] = r.astype(bf16)
        m_scr[at, :] = r * mxd[at, 0:64]
    rows, cols = doc_numbers(doc[...])
    ones = jnp.ones((8, 64), f32)
    s = 64 ** -0.25
    om = omega[2 * z + c].astype(bf16)

    def feature_back(ph, grad, base):
        a = ph.astype(f32) * grad
        return s * nt(a.astype(bf16), om) - (s * s) * base * jnp.sum(a, axis=-1, keepdims=True)

    for b in range(4):
        at = pl.ds(256 * b, 256)
        n = 256 * (b + 1)
        i = lax.broadcasted_iota(jnp.int32, (256, n), 0) + 256 * b
        j = lax.broadcasted_iota(jnp.int32, (256, n), 1)
        same = (col_of(cols, 2 * b, 2 * b + 2) == row_of(rows, 0, 2 * b + 2)) & (i >= j)
        ds = nt(r_scr[at, :], v[0:n, :]) - jnp.sum(m_scr[at, :], axis=-1, keepdims=True)
        ds = jnp.where(same, ds, 0.0).astype(bf16)
        qg = feature_back(phq[at, :], nn(ds, phk[0:n, :]), qk[at, 0:64])
        m = 1024 - 256 * b
        later = pl.ds(256 * b, m)
        j2 = lax.broadcasted_iota(jnp.int32, (256, m), 0)
        i2 = lax.broadcasted_iota(jnp.int32, (256, m), 1)
        same2 = (col_of(cols, 2 * b, 2 * b + 2) == row_of(rows, 2 * b, 8)) & (i2 >= j2)
        scores = jnp.where(same2, nt(phk[at, :], phq[later, :]), 0.0).astype(bf16)
        vg = nn(scores, r_scr[later, :])
        mr = nt(ones, m_scr[later, :], lax.Precision.HIGHEST)[0:1, :]
        ds2 = jnp.where(same2, nt(v[at, :], r_scr[later, :]) - mr, 0.0).astype(bf16)
        kg = feature_back(phk[at, :], nn(ds2, phq[later, :]), qk[at, 64:128])
        rnd = lambda t: t.astype(bf16).astype(f32)
        pg_o[at, :] = rnd(jnp.concatenate([qg, kg], axis=1))
        pg_o[pl.ds(1024 + 256 * (b % 2), 256), 64 * (b // 2) : 64 * (b // 2) + 64] = rnd(vg)
    for n, out in enumerate((pg0, pg1, pg2)):
        out[...] = pg_o[512 * n : 512 * n + 512, :]


def weight_part(m0, m1, m2, t0, t1, t2, nt_low, okeep, ogive, q0, q1, q2, q3, keep, give, scr, g_scr):
    z, c, first, _ = here()
    for b in range(4):
        at = pl.ds(256 * b, 256)
        half = pl.ds(256 * (b % 2), 256)
        lanes = slice(64 * (b // 2), 64 * (b // 2) + 64)
        a, t = ((m0, t0), (m1, t1))[b // 2]
        a, t = a[half, :], t[half, :]
        av, tv = m2[half, lanes], t2[half, lanes]
        h0 = jnp.where(c == 0, a, t)
        h1 = jnp.where(c == 0, t, a)
        scr[at, 0:128] = jnp.concatenate([h0[:, 0:64], h1[:, 0:64]], axis=1)
        scr[at, 128:256] = jnp.concatenate([h0[:, 64:128], h1[:, 64:128]], axis=1)
        scr[at, 256:384] = jnp.concatenate([jnp.where(c == 0, av, tv), jnp.where(c == 0, tv, av)], axis=1)
    for k, ref in enumerate((q0, q1, q2, q3)):
        chunk = 2 * jnp.bitwise_xor(z, k) + c
        ref[...] = scr[pl.ds(pl.multiple_of(chunk * 128, 128), 128), :]
    g_scr[...] = nn(nt_low[...], scr[...].astype(bf16))
    keep[:, 0:384] = g_scr[pl.ds(pl.multiple_of(first * 128, 128), 128), :]
    give[:, 0:384] = g_scr[pl.ds(pl.multiple_of((1 - first) * 128, 128), 128), :]
    keep[:, 384:896] = okeep[...]
    give[:, 384:896] = ogive[...]


def tokens_part(q0, q1, q2, q3, mg, tokens, w, gain, out_o, scr):
    z, _, _, _ = here()
    for k, ref in enumerate((q0, q1, q2, q3)):
        j = jnp.bitwise_xor(z, k)
        for part in range(3):
            scr[:, pl.ds(pl.multiple_of(part * 512 + j * 128, 128), 128)] = ref[:, 128 * part : 128 * part + 128].astype(bf16)
    n, inv = normalise(tokens[...].astype(f32))
    e = gain[...] * nt(scr[...], w[...])
    out_o[...] = mg[...] + normalise_back(e, n, inv)


def add_split(mine, got, keep, give):
    _, _, _, second = here()
    a = pl.ds(pl.multiple_of(second * 64, 64), 64)
    b = pl.ds(pl.multiple_of((1 - second) * 64, 64), 64)
    keep[...] = mine[a, :] + got[a, :]
    give[...] = mine[b, :] + got[b, :]


def ffn_narrow(count, *refs):
    xs, cs, (xb, cb) = refs[:count], refs[count : 2 * count], refs[2 * count :]
    at = 0
    for x, cc in zip(xs, cs):
        for i in range(x.shape[0]):
            xb[pl.ds(at, 128), :] = x[i].astype(bf16)
            cb[pl.ds(at, 128), :] = cc[i].astype(bf16)
            at += 128


def ffn_weights(unit, mine, first, last, xb, cb, wu, wd, *refs):
    if not first:
        before, *refs = refs
    if last:
        theirs, out, up_o, gain_o = refs
    else:
        (out,) = refs
    _, c, _, _ = here()
    core = c if mine else 1 - c
    place = pl.ds(pl.multiple_of(core * 1024 + 256 * unit, 256), 256)
    wut, wdu = jnp.transpose(wu[:, place]), wd[place, :]
    x, inc = xb[...], cb[...]
    up = nt(wut, x)
    hg = nt(wdu, inc)
    cdf, pdf = gelu_parts(up)
    total_up = nn(((cdf + up * pdf) * hg).astype(bf16), x)
    total_down = nn((up * cdf).astype(bf16), inc)
    if not first:
        total_up = total_up + before[0:256, :]
        total_down = total_down + before[256:512, :]
    if last:
        total_up = (total_up + theirs[0:256, :]) * (1.0 / 32)
        total_down = (total_down + theirs[256:512, :]) * (1.0 / 32)
        up_o[...] = jnp.transpose(total_up)
        part = jnp.sum(total_up * wut.astype(f32), axis=0, keepdims=True)
        gain_o[...] = jnp.broadcast_to(part, (8, 512))
    out[0:256, :] = total_up
    out[256:512, :] = total_down


def place_mine(*refs):
    ups, both = refs[0:4], refs[4:8]
    up_o, down_o, sems = refs[8:]
    _, c, _, _ = here()
    copies = []
    for n in range(4):
        at = pl.ds(pl.multiple_of(c * 1024 + 256 * n, 256), 256)
        copies.append(pltpu.make_async_copy(ups[n], up_o.at[:, at], sems.at[2 * n]))
        copies.append(pltpu.make_async_copy(both[n].at[256:512, :], down_o.at[at, :], sems.at[2 * n + 1]))
    for copy in copies:
        copy.start()
    for copy in copies:
        copy.wait()


def place_theirs(b0, b1, b2, b3, up_in, down_in, up_o, down_o, ups, sems):
    _, c, _, _ = here()
    copies = []
    for n, both in enumerate((b0, b1, b2, b3)):
        at = pl.ds(pl.multiple_of((1 - c) * 1024 + 256 * n, 256), 256)
        copies.append(pltpu.make_async_copy(both.at[256:512, :], down_o.at[at, :], sems.at[2 * n]))
        copies[-1].start()
    for n, both in enumerate((b0, b1, b2, b3)):
        at = pl.ds(pl.multiple_of((1 - c) * 1024 + 256 * n, 256), 256)
        ups[n] = jnp.transpose(both[0:256, :])
        copies.append(pltpu.make_async_copy(ups.at[n], up_o.at[:, at], sems.at[2 * n + 1]))
        copies[-1].start()
    for copy in copies:
        copy.wait()


def add_gains(g0, g1, g2, g3, other, gain2, out):
    total = (g0[...] + g1[...]) + (g2[...] + g3[...])
    out[...] = (total[0:1, :] + other[0:1, :]) / gain2[...]


def sum_gains(g0, g1, g2, g3, out):
    out[...] = (g0[...] + g1[...]) + (g2[...] + g3[...])


def finish(a, b, ca, cb, w, gain, qkv_o, out_o, gain_o):
    z, c, first, second = here()
    for n in range(4):
        for core, ref, r1, r2 in ((c, (a, b)[n // 2], first, second), (1 - c, (ca, cb)[n // 2], second, first)):
            row = core * 256 + jnp.bitwise_xor(r1, n % 2) * 128 + jnp.bitwise_xor(r2, n // 2) * 64
            rows = pl.ds(pl.multiple_of(row, 64), 64)
            for k in range(4):
                j = jnp.bitwise_xor(z, k)
                piece = ref.at[4 * (n % 2) + k]
                for part in range(3):
                    at = pl.ds(pl.multiple_of(part * 512 + j * 128, 128), 128)
                    qkv_o[rows, at] = piece[:, 128 * part : 128 * part + 128]
                out_o[rows, pl.ds(pl.multiple_of(j * 128, 128), 128)] = piece[:, 384:512]
    for r in range(4):
        rows = pl.ds(128 * r, 128)
        acc = jnp.zeros((128, 128), f32)
        for j in range(12):
            lanes = pl.ds(128 * j, 128)
            acc = acc + w[rows, lanes].astype(f32) * qkv_o[rows, lanes]
        lanes = pl.ds(128 * r, 128)
        gain_o[0:1, lanes] = jnp.sum(jnp.transpose(acc), axis=0, keepdims=True) / gain[0:1, lanes]


def across(values):
    return [send(v, CORES) for v in values]


def local_fast(tokens, doc_start, norm1_gain, qkv_weight, out_weight, norm2_gain, up_weight, down_weight, omega, cotangent):
    g1, g2 = norm1_gain.reshape(1, 512), norm2_gain.reshape(1, 512)
    tok, cot = tokens[0], cotangent[0]
    order = []
    call = functools.partial(kernel_call, order=order)
    join = functools.partial(joined, order)
    block = ((128, 128), f32)

    def later(*values):
        return call(gate, [(v.shape, v.dtype) for v in values], values, name="gate", micros=0)

    def wait(*values):
        call(gate, [], [], name="gate", micros=0, early=values)

    def pause(micros):
        call(gate, [], [], name="pause", micros=micros)

    def narrow(xs, cs):
        rows = 128 * sum(v.shape[0] for v in xs)
        return call(functools.partial(ffn_narrow, len(xs)), [((rows, 512), bf16)] * 2, [*xs, *cs], name="ffn_narrow", micros=0)

    def ffn(unit, mine, xc, before=None, theirs=None, micros=0):
        first, last = before is None, theirs is not None
        outs = [((512, 512), f32)] + ([((512, 256), f32), ((8, 512), f32)] if last else [])
        more = ([] if first else [before]) + ([theirs] if last else [])
        got = call(
            functools.partial(ffn_weights, unit, mine, first, last), outs, [*xc, up_weight, down_weight, *more],
            (), "ffn_weights", micros, 24,
        )
        return got if last else got[0]

    message, cot_wide = call(prepare, [((136, 512), f32), ((128, 512), f32)], [tok, doc_start, cot], name="prepare")
    t = [message] + [send(message, ALONG_Z[k], "tok") for k in (1, 2, 3)]
    ca = join(cot_wide, send(cot_wide, ALONG_Z[1], "c1"), early=t)
    p = [send(v, CORES, "tok") for v in t]
    ca_first = send(ca, FIRST, "ca")
    keep, give, phq, phk, qk, v, mxd, doc, nt_low = call(
        head_forward,
        [((4, 128, 64), f32), ((4, 128, 64), f32), ((1024, 256), bf16), ((1024, 256), bf16), ((1024, 128), f32),
         ((1024, 64), bf16), ((1024, 128), f32), ((8, 128), f32), ((256, 1024), bf16)],
        [*t, *p, g1, qkv_weight, omega], [pltpu.VMEM((1024, 512), bf16)], "head_forward", 2,
    )
    b = call(pack_pairs, [block] * 4, [keep, send(give, CORES, "give")], name="pack_pairs", micros=0)
    b = [b[0]] + [send(b[k], ALONG_Z[k], "mixed") for k in (1, 2, 3)]
    pause(0.8)
    ca_two = join(ca, ca_first, early=[up_weight, down_weight, out_weight])
    ca_other = send(ca_two, SECOND, "ca")
    mixed, middle, normed = call(
        middle_part, [((128, 512), bf16), ((128, 512), f32), ((128, 512), f32)], [*b, tok, out_weight, g2],
        name="middle_part", micros=2.5,
    )
    output, mg, mlow, ex0, ex1, ex2, *b = call(
        feed_forward,
        [((128, 512), bf16), ((128, 512), f32), ((128, 512), bf16)] + [((128, 256), f32)] * 3 + [block] * 4,
        [mixed, middle, normed, cot, up_weight, down_weight, out_weight, g2], [pltpu.VMEM((128, 512), f32)],
        "feed_forward", 1.2, out=(0,),
    )
    b = [b[0]] + [send(b[k], ALONG_Z[k], "mg") for k in (1, 2, 3)]
    ex_other = [send(w, CORES, "ex") for w in (ex0, ex1, ex2)]
    pause(1.5)
    okeep, ogive = call(out_part, [((128, 512), f32)] * 2, [mixed, mlow, *ex_other],
                        [pltpu.VMEM((256, 512), f32)], "out_part", micros=0)
    ca_late, normed = later(ca, normed)
    keep, give = call(unpack_pairs, [((4, 128, 64), f32)] * 2, b, name="unpack_pairs", micros=0)
    got = send(give, CORES, "give")
    x1 = send(normed, ALONG_Z[1], "x1")
    c_inner = send(ca_late, INNER, "c")
    pg = call(
        head_backward, [((512, 128), f32)] * 3, [keep, got, phq, phk, qk, v, mxd, doc, omega],
        [pltpu.VMEM((1024, 64), bf16), pltpu.VMEM((1024, 64), f32), pltpu.VMEM((1536, 128), f32)], "head_backward", 4,
    )
    pg_other = [send(w, CORES, "pg") for w in pg]
    c_a = later(ca_two, ca_other)
    xa = join(normed, x1)
    xa_first = send(xa, FIRST, "xa")
    *q, keep, give = call(
        weight_part, [((128, 384), f32)] * 4 + [((128, 896), f32)] * 2, [*pg, *pg_other, nt_low, okeep, ogive],
        [pltpu.VMEM((1024, 384), f32), pltpu.VMEM((256, 384), f32)], "weight_part", micros=0,
    )
    got = send(give, FIRST, "rs")
    c_inner, xa_late = later(c_inner, xa)
    c_outer = send(c_inner, OUTWARD, "c")
    x_inner = send(xa_late, INNER, "x")
    pause(4.7)
    keep, give = call(add_split, [((64, 896), f32)] * 2, [keep, got], name="add_split", micros=0)
    got = send(give, SECOND, "rs")
    xa_two = join(xa, xa_first)
    xa_other = send(xa_two, SECOND, "xa")
    pause(2.4)
    (cb,) = call(choose_far, [((2, 128, 512), f32)], [c_inner, c_outer], name="choose_far", micros=0)
    cb_first = send(cb, FIRST, "cb")
    (x_inner,) = later(x_inner)
    x_outer = send(x_inner, OUTWARD, "x")
    (piece,) = call(add_last, [((64, 896), f32)], [keep, got], name="add_last", micros=0)
    pause(8.2)
    x_a = later(xa_two, xa_other)
    cb_two = join(cb, cb_first)
    cb_other = send(cb_two, SECOND, "cb")
    (piece,) = later(piece)
    piece_line = [send(piece, ALONG_Z[k], "piece") for k in (1, 2, 3)]
    x_now = narrow(x_a, c_a)
    total = {}
    for u in range(4):
        total[u, False] = ffn(u, False, x_now)
    (xb,) = call(choose_far, [((2, 128, 512), f32)], [x_inner, x_outer], name="choose_far", micros=0)
    xb_first = send(xb, FIRST, "xb")
    for u in range(4):
        total[u, True] = ffn(u, True, x_now)
    (pieces,) = call(join_pieces, [((4, 64, 512), f32)], [piece, *piece_line], name="join_pieces", micros=4.6)
    pieces_first = send(pieces, FIRST, "piece")
    xb_two = join(xb, xb_first)
    xb_other = send(xb_two, SECOND, "xb")
    pause(2.5)
    c_b = later(cb_two, cb_other)
    pause(6.4)
    q = [q[0]] + [send(w, ALONG_Z[k], "q") for k, w in zip((1, 2, 3), later(*q[1:]))]
    pieces = [join(pieces, pieces_first)]
    pieces.append(send(pieces[0], SECOND, "piece"))
    (tokens_grad,) = call(
        tokens_part, [((128, 512), f32)], [*q, mg, tok, qkv_weight, g1], [pltpu.VMEM((128, 1536), bf16)],
        "tokens_part", micros=0, out=(0,),
    )
    x_b = later(xb_two, xb_other)
    x_now = narrow(x_b, c_b)
    others = [send(ffn(u, False, x_now, total[u, False], micros=0.3), CORES, "part") for u in range(4)]
    both, ups, gains = zip(*[ffn(u, True, x_now, total[u, True], others[u], micros=1.2) for u in range(4)])
    both_other = [send(w, CORES, "both") for w in both]
    (gain,) = call(sum_gains, [((8, 512), f32)], gains, name="sum_gains", micros=0)
    gain_other = send(gain, CORES, "gain")
    dma = [pltpu.SemaphoreType.DMA((8,))]
    up_grad, down_grad = call(
        place_mine, [((512, 2048), f32), ((2048, 512), f32)], [*ups, *both], dma, "place_mine", 0, far=(0, 1),
    )
    up_grad, down_grad = call(
        place_theirs, [((512, 2048), f32), ((2048, 512), f32)], both_other, [pltpu.VMEM((4, 512, 256), f32), *dma],
        "place_theirs", 10, far=(0, 1), onto=(up_grad, down_grad),
    )
    qkv_grad, out_grad, norm1_grad = call(
        finish, [((512, 1536), f32), ((512, 512), f32), ((1, 512), f32)],
        [*pieces, *[send(w, CORES, "piece") for w in pieces], qkv_weight, g1], (), "finish", 3, out=(0, 1, 2),
    )
    (norm2_grad,) = call(
        add_gains, [((1, 512), f32)], [*gains, gain_other, g2], name="add_gains", micros=0, out=(0,)
    )
    return (output[None], tokens_grad[None], norm1_grad[0], qkv_grad, out_grad, norm2_grad[0], up_grad, down_grad)


def solution(mesh):
    placed = (
        P("dp", "seq", None),
        P("dp", "seq"),
        P(),
        P(),
        P(),
        P(),
        P(),
        P(),
        P(),
        P("dp", "seq", None),
    )
    fits = mesh.shape["dp"] == GRID_DP and mesh.shape["seq"] == GRID_SEQ
    return jax.shard_map(
        local_fast if fits else local,
        mesh=mesh,
        in_specs=placed,
        out_specs=(P("dp", "seq", None), P("dp", "seq", None), P(), P(), P(), P(), P(), P()),
        check_vma=False,
    )
```

```python
import functools

import jax
import jax.numpy as jnp
from jax import lax
from jax.experimental import pallas as pl
from jax.experimental.pallas import tpu as pltpu
from jax.sharding import PartitionSpec as P

norm_eps = 1e-05
highest_precision = lax.Precision.HIGHEST


def entering(value, axis, join, neutral, backward):
    count, mine = (lax.axis_size(axis), lax.axis_index(axis))
    pieces = jax.tree.map(lambda part: lax.all_gather(part, axis), value)
    if backward:
        pieces = jax.tree.map(lambda part: part[::-1], pieces)
        mine = count - 1 - mine
    running = jax.tree.map(
        lambda part, zero: jnp.full_like(part, 0) + jnp.asarray(zero, part.dtype), value, neutral
    )

    def hop(position, running):
        longer = join(running, jax.tree.map(lambda part: part[position], pieces))
        return jax.tree.map(lambda new, old: jnp.where(position < mine, new, old), longer, running)

    return lax.fori_loop(0, count - 1, hop, running)


def layer_norm(values, gain):
    average = jnp.mean(values, axis=-1, keepdims=True)
    centred = values - average
    spread_sq = jnp.mean(centred * centred, axis=-1, keepdims=True)
    return centred * lax.rsqrt(spread_sq + norm_eps) * gain


def features(head_values, omega):
    width_dim = head_values.shape[-1]
    scaled = head_values * width_dim ** (-0.25)
    projection = jnp.einsum("...hd,hdm->...hm", scaled, omega, precision=highest_precision)
    half_square = 0.5 * jnp.sum(scaled * scaled, axis=-1, keepdims=True)
    return jnp.exp(projection - half_square)


def exact_gelu(values):
    return jax.nn.gelu(values, approximate=False)


def row_masks(doc_start):
    stretch_len = doc_start.shape[1]
    doc_index = jnp.cumsum(doc_start, axis=1)
    position = jnp.arange(stretch_len, dtype=jnp.int32)
    same_doc = (doc_index[:, :, None] == doc_index[:, None, :]) & (
        position[None, :, None] >= position[None, None, :]
    )
    leading_document = (doc_index == 0).astype(jnp.float32)
    last_doc = (doc_index == doc_index[:, -1:]).astype(jnp.float32)
    document_marker = (doc_index[:, -1] > 0).astype(jnp.float32)
    return (same_doc.astype(jnp.float32), leading_document, last_doc, document_marker)


def mix_rows(
    query_features, key_feat, value_heads, running_state, carry_norm, same_doc, leading_document
):
    scores = (
        jnp.einsum("rihm,rjhm->rhij", query_features, key_feat, precision=highest_precision)
        * same_doc[:, None]
    )
    attention_numerator = jnp.einsum(
        "rhij,rjhd->rihd", scores, value_heads, precision=highest_precision
    )
    attention_numerator = attention_numerator + leading_document[:, :, None, None] * jnp.einsum(
        "rihm,rhmd->rihd", query_features, running_state, precision=highest_precision
    )
    denominator = jnp.transpose(jnp.sum(scores, axis=-1), (0, 2, 1))
    denominator = denominator + leading_document[:, :, None] * jnp.einsum(
        "rihm,rhm->rih", query_features, carry_norm, precision=highest_precision
    )
    return attention_numerator / denominator[..., None]


def stretch_totals(key_feat, value_heads, last_doc):
    key_masked_rows = key_feat * last_doc[:, :, None, None]
    state_sum = jnp.einsum(
        "rchm,rchd->rhmd", key_masked_rows, value_heads, precision=highest_precision
    )
    return (state_sum, jnp.sum(key_masked_rows, axis=1))


def carry_on(earlier, later):
    state_sum, norm_sum, document_marker = later
    pass_on = 1.0 - document_marker
    return (
        state_sum + pass_on[:, None, None, None] * earlier[0],
        norm_sum + pass_on[:, None, None] * earlier[1],
        jnp.maximum(earlier[2], document_marker),
    )


def local(
    tokens,
    doc_start,
    norm1_gain,
    qkv_weight,
    out_weight,
    norm2_gain,
    up_weight,
    down_weight,
    omega,
    cotangent,
):
    row_count, stretch_len, model_width = tokens.shape
    head_count = omega.shape[0]
    head_dim = omega.shape[1]
    token_count = row_count * stretch_len
    stream = tokens.astype(jnp.float32).reshape(token_count, model_width)
    same_doc, leading_document, last_doc, document_marker = row_masks(doc_start)
    normed_one, norm1_back = jax.vjp(layer_norm, stream, norm1_gain)
    normed_one_low = normed_one.astype(jnp.bfloat16)
    projected = jnp.dot(normed_one_low, qkv_weight, preferred_element_type=jnp.float32)
    head_split = projected.reshape(row_count, stretch_len, 3, head_count, head_dim)
    query_heads = head_split[:, :, 0]
    key_heads = head_split[:, :, 1]
    value_heads = head_split[:, :, 2]

    def both_features(query_part, key_part):
        return (features(query_part, omega), features(key_part, omega))

    (query_features, key_feat), feature_back = jax.vjp(both_features, query_heads, key_heads)

    def local_totals(key_part, value_part):
        return stretch_totals(key_part, value_part, last_doc)

    (state_sum, norm_sum), totals_back = jax.vjp(local_totals, key_feat, value_heads)
    empty_state = jnp.zeros_like(state_sum)
    empty_norm = jnp.zeros_like(norm_sum)
    empty_flag = jnp.zeros_like(document_marker)
    running_state, carry_norm, unused_flag = entering(
        (state_sum, norm_sum, document_marker),
        "seq",
        carry_on,
        (empty_state, empty_norm, empty_flag),
        False,
    )

    def local_mix(query_part, key_part, value_part, state_part, norm_part):
        return mix_rows(
            query_part, key_part, value_part, state_part, norm_part, same_doc, leading_document
        )

    mixed, mix_back = jax.vjp(
        local_mix, query_features, key_feat, value_heads, running_state, carry_norm
    )
    mixed_low = mixed.reshape(token_count, model_width).astype(jnp.bfloat16)
    branch = jnp.dot(mixed_low, out_weight, preferred_element_type=jnp.float32)
    middle = stream + branch
    normed_two, norm2_back = jax.vjp(layer_norm, middle, norm2_gain)
    normed_two_low = normed_two.astype(jnp.bfloat16)
    up_values = jnp.dot(normed_two_low, up_weight, preferred_element_type=jnp.float32)
    gelu_out, gelu_back = jax.vjp(exact_gelu, up_values)
    hidden = gelu_out.astype(jnp.bfloat16)
    ffn_out = jnp.dot(hidden, down_weight, preferred_element_type=jnp.float32)
    output = (middle + ffn_out).astype(jnp.bfloat16).reshape(row_count, stretch_len, model_width)
    incoming = cotangent.reshape(token_count, model_width)
    down_grad = jnp.einsum("tf,td->fd", hidden, incoming, preferred_element_type=jnp.float32)
    hidden_grad = jnp.einsum("td,fd->tf", incoming, down_weight, preferred_element_type=jnp.float32)
    (up_full,) = gelu_back(hidden_grad)
    up_grad_low = up_full.astype(jnp.bfloat16)
    up_grad = jnp.einsum(
        "td,tf->df", normed_two_low, up_grad_low, preferred_element_type=jnp.float32
    )
    normed_two_grad = jnp.einsum(
        "tf,df->td", up_grad_low, up_weight, preferred_element_type=jnp.float32
    )
    middle_part, norm2_grad = norm2_back(normed_two_grad)
    middle_grad = incoming.astype(jnp.float32) + middle_part
    middle_low = middle_grad.astype(jnp.bfloat16)
    out_grad = jnp.einsum("td,te->de", mixed_low, middle_low, preferred_element_type=jnp.float32)
    mixed_grad = jnp.einsum("te,de->td", middle_low, out_weight, preferred_element_type=jnp.float32)
    mixed_grad = mixed_grad.reshape(row_count, stretch_len, head_count, head_dim)
    query_feat_grad, key_feat_mix, value_mix, carry_state_grad, carry_norm_grad = mix_back(
        mixed_grad
    )
    later_state, later_norm, unused_later = entering(
        (carry_state_grad, carry_norm_grad, document_marker),
        "seq",
        carry_on,
        (empty_state, empty_norm, empty_flag),
        True,
    )
    key_feat_tot, value_tot = totals_back((later_state, later_norm))
    query_grad, key_grad = feature_back((query_feat_grad, key_feat_mix + key_feat_tot))
    value_grad = value_mix + value_tot
    projected_grad = jnp.stack((query_grad, key_grad, value_grad), axis=2)
    projected_grad = projected_grad.reshape(token_count, 3 * model_width).astype(jnp.bfloat16)
    qkv_grad = jnp.einsum(
        "td,te->de", normed_one_low, projected_grad, preferred_element_type=jnp.float32
    )
    normed_one_grad = jnp.einsum(
        "te,de->td", projected_grad, qkv_weight, preferred_element_type=jnp.float32
    )
    stream_part, norm1_grad = norm1_back(normed_one_grad)
    tokens_grad = (middle_grad + stream_part).reshape(row_count, stretch_len, model_width)
    device_count = lax.axis_size("dp") * lax.axis_size("seq")
    qkv_sum, out_sum, up_sum, down_sum, norm1_sum, norm2_sum = lax.psum(
        (qkv_grad, out_grad, up_grad, down_grad, norm1_grad, norm2_grad), ("dp", "seq")
    )
    return (
        output,
        tokens_grad,
        norm1_sum / device_count,
        qkv_sum / device_count,
        out_sum / device_count,
        norm2_sum / device_count,
        up_sum / device_count,
        down_sum / device_count,
    )


eps = 1e-05
f32 = jnp.float32
bf16 = jnp.bfloat16
AXES = ("dp", "seq")
GRID_DP, GRID_SEQ = 4, 8
ROOM = 56 * 2**20


def place(y, x, z, c):
    return (y * 2 + x) * GRID_SEQ + z * 2 + c


def pairs(move):
    return [
        (place(y, x, z, c), place(*move(y, x, z, c)))
        for y in range(2)
        for x in range(2)
        for z in range(4)
        for c in range(2)
    ]


INNER = pairs(lambda y, x, z, c: (y, x, 3 - z, c))
INNER = [(a, b) for a, b in INNER if (a % GRID_SEQ) // 2 in (1, 2)]
OUTWARD = pairs(lambda y, x, z, c: (y, x, z ^ 1, c))
OUTWARD = [(a, b) for a, b in OUTWARD if (a % GRID_SEQ) // 2 in (1, 2)]
ALONG_Z = {k: pairs(lambda y, x, z, c, k=k: (y, x, z ^ k, c)) for k in (1, 2, 3)}
CORES = pairs(lambda y, x, z, c: (y, x, z, 1 - c))
FIRST = pairs(lambda y, x, z, c: (y, 1 - x, z, c) if c == 0 else (1 - y, x, z, c))
SECOND = pairs(lambda y, x, z, c: (1 - y, x, z, c) if c == 0 else (y, 1 - x, z, c))


def send(value, perm, tag="send"):
    with jax.named_scope("t_" + tag):
        return lax.ppermute(value, AXES, perm)


def nn(a, b, precision=None):
    return lax.dot_general(
        a, b, (((1,), (0,)), ((), ())), precision=precision, preferred_element_type=f32
    )


def nt(a, b, precision=None):
    return lax.dot_general(
        a, b, (((1,), (1,)), ((), ())), precision=precision, preferred_element_type=f32
    )


def work(micros):
    return pl.CostEstimate(flops=int(micros * 1.16e9), bytes_accessed=0, transcendentals=0)


def here():
    dp, seq = lax.axis_index("dp"), lax.axis_index("seq")
    y, x, z, c = dp // 2, dp % 2, seq // 2, seq % 2
    return z, c, jnp.where(c == 0, x, y), jnp.where(c == 0, y, x)


def kernel_call(body, outs, args, scratch=(), name=None, micros=2, room=16, far=(), out=(), order=None, early=(), onto=(), where=pltpu.VMEM):
    vmem = pl.BlockSpec(memory_space=pltpu.VMEM)
    args = list(args)
    staged = len(args)
    args += list(onto)
    held = len(args)
    args += list(early) + list(order or ())
    ignored = len(args) - held
    outs = [*outs, ((8, 128), f32)]
    shapes = [
        jax.ShapeDtypeStruct(s, d) if n in far or n in out else pltpu.VMEM(s, d) for n, (s, d) in enumerate(outs)
    ]
    specs = [pl.BlockSpec(memory_space=pl.ANY) if n in far else vmem for n in range(len(outs))]
    results = len(outs) - 1

    def whole(*refs):
        refs, mark, rest = refs[: held + ignored + results], refs[held + ignored + results], refs[held + ignored + results + 1 :]
        mark[...] = jnp.zeros((8, 128), f32)
        body(*refs[:held], *refs[held + ignored :], *rest)

    *values, mark = pl.pallas_call(
        whole,
        out_shape=shapes,
        in_specs=[pl.BlockSpec(memory_space=pl.ANY) if staged <= n < held else vmem for n in range(len(args))],
        out_specs=specs,
        scratch_shapes=list(scratch),
        input_output_aliases={staged + n: n for n in range(len(onto))},
        compiler_params=pltpu.CompilerParams(vmem_limit_bytes=room * 2**20),
        name=name,
        cost_estimate=work(micros),
    )(*[a if staged <= n < held else pltpu.with_memory_space_constraint(a, where) for n, a in enumerate(args)])
    if order is not None:
        order[:] = [mark]
    return values


def pick(v, bit):
    return jnp.where(bit == 0, v[:, 0:64], v[:, 64:128])


def normalise(v):
    mean = jnp.mean(v, axis=-1, keepdims=True)
    centred = v - mean
    inv = lax.rsqrt(jnp.mean(centred * centred, axis=-1, keepdims=True) + eps)
    return centred * inv, inv


def normalise_back(e, n, inv):
    return (e - jnp.mean(e, axis=-1, keepdims=True) - n * jnp.mean(e * n, axis=-1, keepdims=True)) * inv


def doc_numbers(doc):
    at = lax.broadcasted_iota(jnp.int32, (128, 128), 0)
    to = lax.broadcasted_iota(jnp.int32, (128, 128), 1)
    upper = (at <= to).astype(f32)
    a8 = lax.broadcasted_iota(jnp.int32, (8, 8), 0)
    t8 = lax.broadcasted_iota(jnp.int32, (8, 8), 1)
    before = (t8 < a8).astype(f32)
    spread = jnp.broadcast_to(jnp.sum(doc, axis=1, keepdims=True), (8, 128))
    high = lax.Precision.HIGHEST
    rows = nn(doc, upper, high) + nn(before, spread, high)
    eye = (at == to).astype(f32)
    cols = nt(eye, rows, high)
    return rows, cols


def row_of(rows, lo, hi):
    return jnp.concatenate([rows[j : j + 1, :] for j in range(lo, hi)], axis=1)


def col_of(cols, lo, hi):
    return jnp.concatenate([cols[:, j : j + 1] for j in range(lo, hi)], axis=0)


def gelu_parts(u):
    return 0.5 + 0.5 * lax.erf(u * 0.7071067811865476), jnp.exp(-0.5 * u * u) * 0.3989422804014327


def prepare(tokens, doc, cot, message, cot_o):
    message[0:128, :] = tokens[...].astype(f32)
    message[128:136, :] = jnp.zeros((8, 512), f32)
    message[128:129, 0:128] = doc[...].astype(f32)
    cot_o[...] = cot[...].astype(f32)


def join(*refs):
    at = 0
    out = refs[-1]
    for ref in refs[:-1]:
        out[at : at + ref.shape[0]] = ref[...]
        at += ref.shape[0]


def joined(order, *values, early=()):
    values = [v[None] if v.ndim == 2 else v for v in values]
    shape = (sum(v.shape[0] for v in values),) + values[0].shape[1:]
    return kernel_call(join, [(shape, f32)], values, name="join", micros=0, order=order, early=early)[0]


def gate(*refs):
    half = len(refs) // 2
    for ref, out in zip(refs[:half], refs[half:]):
        out[...] = ref[...]


def choose_far(near, far, out):
    z, _, _, _ = here()
    inner = (z == 1) | (z == 2)
    for n in range(2):
        out[n] = jnp.where(inner, near[1 - n], far[n])


def head_forward(t0, t1, t2, t3, p0, p1, p2, p3, gain, w, omega,
                 keep, give, phq_o, phk_o, qk_o, v_o, mxd_o, doc_o, nt_o, low):
    z, c, _, _ = here()
    wh = jnp.concatenate([pick(w[:, pl.ds(pl.multiple_of(part * 512 + z * 128, 128), 128)], c) for part in range(3)], axis=1)
    g = gain[...]
    for k, (mine, theirs) in enumerate(((t0, p0), (t1, p1), (t2, p2), (t3, p3))):
        for ref, core in ((mine, c), (theirs, 1 - c)):
            chunk = 2 * jnp.bitwise_xor(z, k) + core
            n, _ = normalise(ref[0:128, :])
            low[pl.ds(pl.multiple_of(chunk * 128, 128), 128), :] = (n * g).astype(bf16)
            doc_o[pl.ds(chunk, 1), :] = ref[128:129, 0:128]
    rows, cols = doc_numbers(doc_o[...])
    nt_o[...] = jnp.transpose(low[:, pl.ds(pl.multiple_of(c * 256, 256), 256)])
    s = 64 ** -0.25
    om = omega[2 * z + c]
    oh = om.astype(bf16)
    ol = (om - oh.astype(f32)).astype(bf16)
    stack = jnp.concatenate([oh, oh, ol], axis=0)

    def feature(v):
        v = v * s
        hi = v.astype(bf16)
        lo = (v - hi.astype(f32)).astype(bf16)
        proj = nn(jnp.concatenate([hi, lo, hi], axis=1), stack)
        return jnp.exp(proj - 0.5 * jnp.sum(v * v, axis=-1, keepdims=True))

    for b in range(4):
        at = pl.ds(256 * b, 256)
        pr = nn(low[at, :], wh)
        qk_o[at, :] = pr[:, 0:128]
        v_o[at, :] = pr[:, 128:192].astype(bf16)
        phq_o[at, :] = feature(pr[:, 0:64]).astype(bf16)
        phk_o[at, :] = feature(pr[:, 64:128]).astype(bf16)
    for b in range(4):
        at = pl.ds(256 * b, 256)
        n = 256 * (b + 1)
        scores = nt(phq_o[at, :], phk_o[0:n, :])
        i = lax.broadcasted_iota(jnp.int32, (256, n), 0) + 256 * b
        j = lax.broadcasted_iota(jnp.int32, (256, n), 1)
        same = (col_of(cols, 2 * b, 2 * b + 2) == row_of(rows, 0, 2 * b + 2)) & (i >= j)
        scores = jnp.where(same, scores, 0.0)
        inv = 1.0 / jnp.sum(scores, axis=-1, keepdims=True)
        mixed = nn(scores.astype(bf16), v_o[0:n, :]) * inv
        mxd_o[at, :] = jnp.concatenate([mixed, jnp.broadcast_to(inv, (256, 64))], axis=1)
        top, bottom = mixed[0:128, :], mixed[128:256, :]
        keep[b] = jnp.where(c == 0, top, bottom)
        give[b] = jnp.where(c == 0, bottom, top)


def pack_pairs(keep, got, b0, b1, b2, b3):
    z, c, _, _ = here()
    for k, out in enumerate((b0, b1, b2, b3)):
        j = jnp.bitwise_xor(z, k)
        a, b = keep[j], got[j]
        out[...] = jnp.where(c == 0, jnp.concatenate([a, b], axis=1), jnp.concatenate([b, a], axis=1))


def unpack_pairs(b0, b1, b2, b3, keep, give):
    z, c, _, _ = here()
    for k, ref in enumerate((b0, b1, b2, b3)):
        j = jnp.bitwise_xor(z, k)
        a, b = ref[:, 0:64], ref[:, 64:128]
        keep[j] = jnp.where(c == 0, a, b)
        give[j] = jnp.where(c == 0, b, a)


def middle_part(b0, b1, b2, b3, tokens, wo, gain, mixed_o, middle_o, normed_o):
    z, _, _, _ = here()
    for k, ref in enumerate((b0, b1, b2, b3)):
        j = jnp.bitwise_xor(z, k)
        mixed_o[:, pl.ds(pl.multiple_of(j * 128, 128), 128)] = ref[...].astype(bf16)
    middle = tokens[...].astype(f32) + nn(mixed_o[...], wo[...])
    middle_o[...] = middle
    n, _ = normalise(middle)
    normed_o[...] = (n * gain[...]).astype(bf16).astype(f32)


def feed_forward(mixed, middle, normed, cot, wu, wd, wo, gain,
                 out_o, mg_o, ml_o, ex0, ex1, ex2, b0, b1, b2, b3, scr):
    z, c, _, _ = here()
    x = normed[...].astype(bf16)
    inc = cot[...]
    total = middle[...]
    back = jnp.zeros((128, 512), f32)
    for u in range(4):
        at = pl.ds(512 * u, 512)
        wub, wdb = wu[:, at], wd[at, :]
        up = nn(x, wub)
        cdf, pdf = gelu_parts(up)
        total = total + nn((up * cdf).astype(bf16), wdb)
        ug = ((cdf + up * pdf) * nt(inc, wdb)).astype(bf16)
        back = back + nt(ug, wub)
    out_o[...] = total.astype(bf16)
    n, inv = normalise(middle[...])
    mg = inc.astype(f32) + normalise_back(gain[...] * back, n, inv)
    mg_o[...] = mg
    low = mg.astype(bf16)
    ml_o[...] = low
    ex0[...] = mixed[:, pl.ds(pl.multiple_of((1 - c) * 256, 256), 256)].astype(f32)
    ex1[...] = low[:, 0:256].astype(f32)
    ex2[...] = low[:, 256:512].astype(f32)
    scr[...] = nt(low, wo[...])
    for k, ref in enumerate((b0, b1, b2, b3)):
        j = jnp.bitwise_xor(z, k)
        ref[...] = scr[:, pl.ds(pl.multiple_of(j * 128, 128), 128)]


def out_part(mixed, mlow, got0, got1, got2, keep, give, scr):
    _, c, first, _ = here()
    mine = mixed[:, pl.ds(pl.multiple_of(c * 256, 256), 256)].astype(f32)
    left = jnp.transpose(jnp.concatenate([mine, got0[...]], axis=0)).astype(bf16)
    theirs = jnp.concatenate([got1[...], got2[...]], axis=1).astype(bf16)
    right = jnp.concatenate([mlow[...], theirs], axis=0)
    scr[...] = nn(left, right)
    keep[...] = scr[pl.ds(pl.multiple_of(first * 128, 128), 128), :]
    give[...] = scr[pl.ds(pl.multiple_of((1 - first) * 128, 128), 128), :]


def add_last(mine, got, out):
    out[...] = (mine[...] + got[...]) * (1.0 / 32)


def join_pieces(p0, p1, p2, p3, out):
    z, _, _, _ = here()
    parts = (p0, p1, p2, p3)
    total = (p0[:, 384:896] + p1[:, 384:896]) + (p2[:, 384:896] + p3[:, 384:896])
    for k, ref in enumerate(parts):
        j = jnp.bitwise_xor(z, k)
        out[k, :, 0:384] = ref[:, 0:384]
        block = total[:, 0:128]
        for n in range(1, 4):
            block = jnp.where(j == n, total[:, 128 * n : 128 * n + 128], block)
        out[k, :, 384:512] = block


def head_backward(keep, got, phq, phk, qk, v, mxd, doc, omega, pg0, pg1, pg2, r_scr, m_scr, pg_o):
    z, c, _, _ = here()
    for b in range(4):
        a, g = keep[b], got[b]
        at = pl.ds(256 * b, 256)
        dm = jnp.concatenate([jnp.where(c == 0, a, g), jnp.where(c == 0, g, a)], axis=0)
        r = dm * mxd[at, 64:128]
        r_scr[at, :] = r.astype(bf16)
        m_scr[at, :] = r * mxd[at, 0:64]
    rows, cols = doc_numbers(doc[...])
    ones = jnp.ones((8, 64), f32)
    s = 64 ** -0.25
    om = omega[2 * z + c].astype(bf16)

    def feature_back(ph, grad, base):
        a = ph.astype(f32) * grad
        return s * nt(a.astype(bf16), om) - (s * s) * base * jnp.sum(a, axis=-1, keepdims=True)

    for b in range(4):
        at = pl.ds(256 * b, 256)
        n = 256 * (b + 1)
        i = lax.broadcasted_iota(jnp.int32, (256, n), 0) + 256 * b
        j = lax.broadcasted_iota(jnp.int32, (256, n), 1)
        same = (col_of(cols, 2 * b, 2 * b + 2) == row_of(rows, 0, 2 * b + 2)) & (i >= j)
        ds = nt(r_scr[at, :], v[0:n, :]) - jnp.sum(m_scr[at, :], axis=-1, keepdims=True)
        ds = jnp.where(same, ds, 0.0).astype(bf16)
        qg = feature_back(phq[at, :], nn(ds, phk[0:n, :]), qk[at, 0:64])
        m = 1024 - 256 * b
        later = pl.ds(256 * b, m)
        j2 = lax.broadcasted_iota(jnp.int32, (256, m), 0)
        i2 = lax.broadcasted_iota(jnp.int32, (256, m), 1)
        same2 = (col_of(cols, 2 * b, 2 * b + 2) == row_of(rows, 2 * b, 8)) & (i2 >= j2)
        scores = jnp.where(same2, nt(phk[at, :], phq[later, :]), 0.0).astype(bf16)
        vg = nn(scores, r_scr[later, :])
        mr = nt(ones, m_scr[later, :], lax.Precision.HIGHEST)[0:1, :]
        ds2 = jnp.where(same2, nt(v[at, :], r_scr[later, :]) - mr, 0.0).astype(bf16)
        kg = feature_back(phk[at, :], nn(ds2, phq[later, :]), qk[at, 64:128])
        rnd = lambda t: t.astype(bf16).astype(f32)
        pg_o[at, :] = rnd(jnp.concatenate([qg, kg], axis=1))
        pg_o[pl.ds(1024 + 256 * (b % 2), 256), 64 * (b // 2) : 64 * (b // 2) + 64] = rnd(vg)
    for n, out in enumerate((pg0, pg1, pg2)):
        out[...] = pg_o[512 * n : 512 * n + 512, :]


def weight_part(m0, m1, m2, t0, t1, t2, nt_low, okeep, ogive, q0, q1, q2, q3, keep, give, scr, g_scr):
    z, c, first, _ = here()
    for b in range(4):
        at = pl.ds(256 * b, 256)
        half = pl.ds(256 * (b % 2), 256)
        lanes = slice(64 * (b // 2), 64 * (b // 2) + 64)
        a, t = ((m0, t0), (m1, t1))[b // 2]
        a, t = a[half, :], t[half, :]
        av, tv = m2[half, lanes], t2[half, lanes]
        h0 = jnp.where(c == 0, a, t)
        h1 = jnp.where(c == 0, t, a)
        scr[at, 0:128] = jnp.concatenate([h0[:, 0:64], h1[:, 0:64]], axis=1)
        scr[at, 128:256] = jnp.concatenate([h0[:, 64:128], h1[:, 64:128]], axis=1)
        scr[at, 256:384] = jnp.concatenate([jnp.where(c == 0, av, tv), jnp.where(c == 0, tv, av)], axis=1)
    for k, ref in enumerate((q0, q1, q2, q3)):
        chunk = 2 * jnp.bitwise_xor(z, k) + c
        ref[...] = scr[pl.ds(pl.multiple_of(chunk * 128, 128), 128), :]
    g_scr[...] = nn(nt_low[...], scr[...].astype(bf16))
    keep[:, 0:384] = g_scr[pl.ds(pl.multiple_of(first * 128, 128), 128), :]
    give[:, 0:384] = g_scr[pl.ds(pl.multiple_of((1 - first) * 128, 128), 128), :]
    keep[:, 384:896] = okeep[...]
    give[:, 384:896] = ogive[...]


def tokens_part(q0, q1, q2, q3, mg, tokens, w, gain, out_o, scr):
    z, _, _, _ = here()
    for k, ref in enumerate((q0, q1, q2, q3)):
        j = jnp.bitwise_xor(z, k)
        for part in range(3):
            scr[:, pl.ds(pl.multiple_of(part * 512 + j * 128, 128), 128)] = ref[:, 128 * part : 128 * part + 128].astype(bf16)
    n, inv = normalise(tokens[...].astype(f32))
    e = gain[...] * nt(scr[...], w[...])
    out_o[...] = mg[...] + normalise_back(e, n, inv)


def add_split(mine, got, keep, give):
    _, _, _, second = here()
    a = pl.ds(pl.multiple_of(second * 64, 64), 64)
    b = pl.ds(pl.multiple_of((1 - second) * 64, 64), 64)
    keep[...] = mine[a, :] + got[a, :]
    give[...] = mine[b, :] + got[b, :]


def ffn_narrow(count, *refs):
    xs, cs, (xb, cb) = refs[:count], refs[count : 2 * count], refs[2 * count :]
    at = 0
    for x, cc in zip(xs, cs):
        for i in range(x.shape[0]):
            xb[pl.ds(at, 128), :] = x[i].astype(bf16)
            cb[pl.ds(at, 128), :] = cc[i].astype(bf16)
            at += 128


def ffn_weights(unit, mine, first, last, xb, cb, wu, wd, *refs):
    if not first:
        before, *refs = refs
    if last:
        theirs, out, up_o = refs
    else:
        (out,) = refs
    _, c, _, _ = here()
    core = c if mine else 1 - c
    place = pl.ds(pl.multiple_of(core * 1024 + 256 * unit, 256), 256)
    wut, wdu = jnp.transpose(wu[:, place]), wd[place, :]
    x, inc = xb[...], cb[...]
    up = nt(wut, x)
    hg = nt(wdu, inc)
    cdf, pdf = gelu_parts(up)
    total_up = nn(((cdf + up * pdf) * hg).astype(bf16), x)
    total_down = nn((up * cdf).astype(bf16), inc)
    if not first:
        total_up = total_up + before[0:256, :]
        total_down = total_down + before[256:512, :]
    if last:
        total_up = (total_up + theirs[0:256, :]) * (1.0 / 32)
        total_down = (total_down + theirs[256:512, :]) * (1.0 / 32)
        up_o[...] = jnp.transpose(total_up)
        part = jnp.sum(total_up * wut.astype(f32), axis=0, keepdims=True)
        out[512:520, :] = jnp.broadcast_to(part, (8, 512))
    out[0:256, :] = total_up
    out[256:512, :] = total_down


def place_mine(*refs):
    ups, both = refs[0:4], refs[4:8]
    up_o, down_o, sems = refs[8:]
    _, c, _, _ = here()
    copies = []
    for n in range(4):
        at = pl.ds(pl.multiple_of(c * 1024 + 256 * n, 256), 256)
        copies.append(pltpu.make_async_copy(ups[n], up_o.at[:, at], sems.at[2 * n]))
        copies.append(pltpu.make_async_copy(both[n].at[256:512, :], down_o.at[at, :], sems.at[2 * n + 1]))
    for copy in copies:
        copy.start()
    for copy in copies:
        copy.wait()


def place_theirs(m0, m1, m2, m3, b0, b1, b2, b3, gain2, up_in, down_in, up_o, down_o, gain_o, ups, sems):
    _, c, _, _ = here()
    copies = []
    for n, both in enumerate((b0, b1, b2, b3)):
        at = pl.ds(pl.multiple_of((1 - c) * 1024 + 256 * n, 256), 256)
        copies.append(pltpu.make_async_copy(both.at[256:512, :], down_o.at[at, :], sems.at[2 * n]))
        copies[-1].start()
    for n, both in enumerate((b0, b1, b2, b3)):
        at = pl.ds(pl.multiple_of((1 - c) * 1024 + 256 * n, 256), 256)
        ups[n] = jnp.transpose(both[0:256, :])
        copies.append(pltpu.make_async_copy(ups.at[n], up_o.at[:, at], sems.at[2 * n + 1]))
        copies[-1].start()
    total = jnp.zeros((1, 512), f32)
    for ref in (m0, m1, m2, m3, b0, b1, b2, b3):
        total = total + ref[512:513, :]
    gain_o[...] = total / gain2[...]
    for copy in copies:
        copy.wait()


def finish(a, b, ca, cb, w, gain, qkv_o, out_o, gain_o):
    z, c, first, second = here()
    for n in range(4):
        for core, ref, r1, r2 in ((c, (a, b)[n // 2], first, second), (1 - c, (ca, cb)[n // 2], second, first)):
            row = core * 256 + jnp.bitwise_xor(r1, n % 2) * 128 + jnp.bitwise_xor(r2, n // 2) * 64
            rows = pl.ds(pl.multiple_of(row, 64), 64)
            for k in range(4):
                j = jnp.bitwise_xor(z, k)
                piece = ref.at[4 * (n % 2) + k]
                for part in range(3):
                    at = pl.ds(pl.multiple_of(part * 512 + j * 128, 128), 128)
                    qkv_o[rows, at] = piece[:, 128 * part : 128 * part + 128]
                out_o[rows, pl.ds(pl.multiple_of(j * 128, 128), 128)] = piece[:, 384:512]
    for r in range(4):
        rows = pl.ds(128 * r, 128)
        acc = jnp.zeros((128, 128), f32)
        for j in range(12):
            lanes = pl.ds(128 * j, 128)
            acc = acc + w[rows, lanes].astype(f32) * qkv_o[rows, lanes]
        lanes = pl.ds(128 * r, 128)
        gain_o[0:1, lanes] = jnp.sum(jnp.transpose(acc), axis=0, keepdims=True) / gain[0:1, lanes]


def across(values):
    return [send(v, CORES) for v in values]


def local_fast(tokens, doc_start, norm1_gain, qkv_weight, out_weight, norm2_gain, up_weight, down_weight, omega, cotangent):
    g1, g2 = norm1_gain.reshape(1, 512), norm2_gain.reshape(1, 512)
    tok, cot = tokens[0], cotangent[0]
    order = []
    call = functools.partial(kernel_call, order=order)
    join = functools.partial(joined, order)
    block = ((128, 128), f32)

    def later(*values):
        return call(gate, [(v.shape, v.dtype) for v in values], values, name="gate", micros=0)

    def wait(*values):
        call(gate, [], [], name="gate", micros=0, early=values)

    def pause(micros):
        call(gate, [], [], name="pause", micros=micros)

    def narrow(xs, cs):
        rows = 128 * sum(v.shape[0] for v in xs)
        return call(functools.partial(ffn_narrow, len(xs)), [((rows, 512), bf16)] * 2, [*xs, *cs], name="ffn_narrow", micros=0)

    def ffn(unit, mine, xc, before=None, theirs=None, micros=0):
        first, last = before is None, theirs is not None
        outs = [((520, 512), f32), ((512, 256), f32)] if last else [((512, 512), f32)]
        more = ([] if first else [before]) + ([theirs] if last else [])
        got = call(
            functools.partial(ffn_weights, unit, mine, first, last), outs, [*xc, up_weight, down_weight, *more],
            (), "ffn_weights", micros, 24,
        )
        return got if last else got[0]

    message, cot_wide = call(prepare, [((136, 512), f32), ((128, 512), f32)], [tok, doc_start, cot], name="prepare", where=pltpu.HBM)
    t = [message] + [send(message, ALONG_Z[k], "tok") for k in (1, 2, 3)]
    ca = join(cot_wide, send(cot_wide, ALONG_Z[1], "c1"), early=t)
    p = [send(v, CORES, "tok") for v in t]
    ca_first = send(ca, FIRST, "ca")
    keep, give, phq, phk, qk, v, mxd, doc, nt_low = call(
        head_forward,
        [((4, 128, 64), f32), ((4, 128, 64), f32), ((1024, 256), bf16), ((1024, 256), bf16), ((1024, 128), f32),
         ((1024, 64), bf16), ((1024, 128), f32), ((8, 128), f32), ((256, 1024), bf16)],
        [*t, *p, g1, qkv_weight, omega], [pltpu.VMEM((1024, 512), bf16)], "head_forward", 2,
    )
    b = call(pack_pairs, [block] * 4, [keep, send(give, CORES, "give")], name="pack_pairs", micros=0)
    b = [b[0]] + [send(b[k], ALONG_Z[k], "mixed") for k in (1, 2, 3)]
    pause(0.8)
    ca_two = join(ca, ca_first, early=[up_weight, down_weight, out_weight])
    ca_other = send(ca_two, SECOND, "ca")
    mixed, middle, normed = call(
        middle_part, [((128, 512), bf16), ((128, 512), f32), ((128, 512), f32)], [*b, tok, out_weight, g2],
        name="middle_part", micros=2.5,
    )
    output, mg, mlow, ex0, ex1, ex2, *b = call(
        feed_forward,
        [((128, 512), bf16), ((128, 512), f32), ((128, 512), bf16)] + [((128, 256), f32)] * 3 + [block] * 4,
        [mixed, middle, normed, cot, up_weight, down_weight, out_weight, g2], [pltpu.VMEM((128, 512), f32)],
        "feed_forward", 1.2, out=(0,),
    )
    b = [b[0]] + [send(b[k], ALONG_Z[k], "mg") for k in (1, 2, 3)]
    ex_other = [send(w, CORES, "ex") for w in (ex0, ex1, ex2)]
    pause(1.5)
    okeep, ogive = call(out_part, [((128, 512), f32)] * 2, [mixed, mlow, *ex_other],
                        [pltpu.VMEM((256, 512), f32)], "out_part", micros=0)
    ca_late, normed = later(ca, normed)
    keep, give = call(unpack_pairs, [((4, 128, 64), f32)] * 2, b, name="unpack_pairs", micros=0)
    got = send(give, CORES, "give")
    x1 = send(normed, ALONG_Z[1], "x1")
    c_inner = send(ca_late, INNER, "c")
    pg = call(
        head_backward, [((512, 128), f32)] * 3, [keep, got, phq, phk, qk, v, mxd, doc, omega],
        [pltpu.VMEM((1024, 64), bf16), pltpu.VMEM((1024, 64), f32), pltpu.VMEM((1536, 128), f32)], "head_backward", 4,
    )
    pg_other = [send(w, CORES, "pg") for w in pg]
    c_a = later(ca_two, ca_other)
    xa = join(normed, x1)
    xa_first = send(xa, FIRST, "xa")
    *q, keep, give = call(
        weight_part, [((128, 384), f32)] * 4 + [((128, 896), f32)] * 2, [*pg, *pg_other, nt_low, okeep, ogive],
        [pltpu.VMEM((1024, 384), f32), pltpu.VMEM((256, 384), f32)], "weight_part", micros=0,
    )
    got = send(give, FIRST, "rs")
    c_inner, xa_late = later(c_inner, xa)
    c_outer = send(c_inner, OUTWARD, "c")
    x_inner = send(xa_late, INNER, "x")
    pause(4.7)
    keep, give = call(add_split, [((64, 896), f32)] * 2, [keep, got], name="add_split", micros=0)
    got = send(give, SECOND, "rs")
    xa_two = join(xa, xa_first)
    xa_other = send(xa_two, SECOND, "xa")
    pause(2.4)
    (cb,) = call(choose_far, [((2, 128, 512), f32)], [c_inner, c_outer], name="choose_far", micros=0)
    cb_first = send(cb, FIRST, "cb")
    (x_inner,) = later(x_inner)
    x_outer = send(x_inner, OUTWARD, "x")
    (piece,) = call(add_last, [((64, 896), f32)], [keep, got], name="add_last", micros=0)
    pause(8.2)
    x_a = later(xa_two, xa_other)
    cb_two = join(cb, cb_first)
    cb_other = send(cb_two, SECOND, "cb")
    (piece,) = later(piece)
    piece_line = [send(piece, ALONG_Z[k], "piece") for k in (1, 2, 3)]
    x_now = narrow(x_a, c_a)
    total = {}
    for u in range(4):
        total[u, False] = ffn(u, False, x_now)
    (xb,) = call(choose_far, [((2, 128, 512), f32)], [x_inner, x_outer], name="choose_far", micros=0)
    xb_first = send(xb, FIRST, "xb")
    for u in range(4):
        total[u, True] = ffn(u, True, x_now)
    (pieces,) = call(join_pieces, [((4, 64, 512), f32)], [piece, *piece_line], name="join_pieces", micros=4.6)
    pieces_first = send(pieces, FIRST, "piece")
    xb_two = join(xb, xb_first)
    xb_other = send(xb_two, SECOND, "xb")
    pause(2.5)
    c_b = later(cb_two, cb_other)
    pause(6.4)
    q = [q[0]] + [send(w, ALONG_Z[k], "q") for k, w in zip((1, 2, 3), later(*q[1:]))]
    pieces = [join(pieces, pieces_first)]
    pieces.append(send(pieces[0], SECOND, "piece"))
    (tokens_grad,) = call(
        tokens_part, [((128, 512), f32)], [*q, mg, tok, qkv_weight, g1], [pltpu.VMEM((128, 1536), bf16)],
        "tokens_part", micros=0, out=(0,),
    )
    pause(3.5)
    x_b = later(xb_two, xb_other)
    x_now = narrow(x_b, c_b)
    others = [send(ffn(u, False, x_now, total[u, False], micros=0.3), CORES, "part") for u in range(4)]
    wait(pieces[1])
    both, ups = zip(*[ffn(u, True, x_now, total[u, True], others[u], micros=1.2) for u in range(4)])
    both_other = [send(w, CORES, "both") for w in both]
    dma = [pltpu.SemaphoreType.DMA((8,))]
    up_grad, down_grad = call(
        place_mine, [((512, 2048), f32), ((2048, 512), f32)], [*ups, *both], dma, "place_mine", 0, far=(0, 1),
    )
    qkv_grad, out_grad, norm1_grad = call(
        finish, [((512, 1536), f32), ((512, 512), f32), ((1, 512), f32)],
        [*pieces, *[send(w, CORES, "piece") for w in pieces], qkv_weight, g1], (), "finish", 0, out=(0, 1, 2),
    )
    up_grad, down_grad, norm2_grad = call(
        place_theirs, [((512, 2048), f32), ((2048, 512), f32), ((1, 512), f32)], [*both, *both_other, g2],
        [pltpu.VMEM((4, 512, 256), f32), *dma], "place_theirs", 0, far=(0, 1), out=(2,), onto=(up_grad, down_grad),
    )
    return (output[None], tokens_grad[None], norm1_grad[0], qkv_grad, out_grad, norm2_grad[0], up_grad, down_grad)


def solution(mesh):
    placed = (
        P("dp", "seq", None),
        P("dp", "seq"),
        P(),
        P(),
        P(),
        P(),
        P(),
        P(),
        P(),
        P("dp", "seq", None),
    )
    fits = mesh.shape["dp"] == GRID_DP and mesh.shape["seq"] == GRID_SEQ
    return jax.shard_map(
        local_fast if fits else local,
        mesh=mesh,
        in_specs=placed,
        out_specs=(P("dp", "seq", None), P("dp", "seq", None), P(), P(), P(), P(), P(), P()),
        check_vma=False,
    )
```

```python
import functools

import jax
import jax.numpy as jnp
from jax import lax
from jax.experimental import pallas as pl
from jax.experimental.pallas import tpu as pltpu
from jax.sharding import PartitionSpec as P

norm_eps = 1e-05
highest_precision = lax.Precision.HIGHEST


def entering(value, axis, join, neutral, backward):
    count, mine = (lax.axis_size(axis), lax.axis_index(axis))
    pieces = jax.tree.map(lambda part: lax.all_gather(part, axis), value)
    if backward:
        pieces = jax.tree.map(lambda part: part[::-1], pieces)
        mine = count - 1 - mine
    running = jax.tree.map(
        lambda part, zero: jnp.full_like(part, 0) + jnp.asarray(zero, part.dtype), value, neutral
    )

    def hop(position, running):
        longer = join(running, jax.tree.map(lambda part: part[position], pieces))
        return jax.tree.map(lambda new, old: jnp.where(position < mine, new, old), longer, running)

    return lax.fori_loop(0, count - 1, hop, running)


def layer_norm(values, gain):
    average = jnp.mean(values, axis=-1, keepdims=True)
    centred = values - average
    spread_sq = jnp.mean(centred * centred, axis=-1, keepdims=True)
    return centred * lax.rsqrt(spread_sq + norm_eps) * gain


def features(head_values, omega):
    width_dim = head_values.shape[-1]
    scaled = head_values * width_dim ** (-0.25)
    projection = jnp.einsum("...hd,hdm->...hm", scaled, omega, precision=highest_precision)
    half_square = 0.5 * jnp.sum(scaled * scaled, axis=-1, keepdims=True)
    return jnp.exp(projection - half_square)


def exact_gelu(values):
    return jax.nn.gelu(values, approximate=False)


def row_masks(doc_start):
    stretch_len = doc_start.shape[1]
    doc_index = jnp.cumsum(doc_start, axis=1)
    position = jnp.arange(stretch_len, dtype=jnp.int32)
    same_doc = (doc_index[:, :, None] == doc_index[:, None, :]) & (
        position[None, :, None] >= position[None, None, :]
    )
    leading_document = (doc_index == 0).astype(jnp.float32)
    last_doc = (doc_index == doc_index[:, -1:]).astype(jnp.float32)
    document_marker = (doc_index[:, -1] > 0).astype(jnp.float32)
    return (same_doc.astype(jnp.float32), leading_document, last_doc, document_marker)


def mix_rows(
    query_features, key_feat, value_heads, running_state, carry_norm, same_doc, leading_document
):
    scores = (
        jnp.einsum("rihm,rjhm->rhij", query_features, key_feat, precision=highest_precision)
        * same_doc[:, None]
    )
    attention_numerator = jnp.einsum(
        "rhij,rjhd->rihd", scores, value_heads, precision=highest_precision
    )
    attention_numerator = attention_numerator + leading_document[:, :, None, None] * jnp.einsum(
        "rihm,rhmd->rihd", query_features, running_state, precision=highest_precision
    )
    denominator = jnp.transpose(jnp.sum(scores, axis=-1), (0, 2, 1))
    denominator = denominator + leading_document[:, :, None] * jnp.einsum(
        "rihm,rhm->rih", query_features, carry_norm, precision=highest_precision
    )
    return attention_numerator / denominator[..., None]


def stretch_totals(key_feat, value_heads, last_doc):
    key_masked_rows = key_feat * last_doc[:, :, None, None]
    state_sum = jnp.einsum(
        "rchm,rchd->rhmd", key_masked_rows, value_heads, precision=highest_precision
    )
    return (state_sum, jnp.sum(key_masked_rows, axis=1))


def carry_on(earlier, later):
    state_sum, norm_sum, document_marker = later
    pass_on = 1.0 - document_marker
    return (
        state_sum + pass_on[:, None, None, None] * earlier[0],
        norm_sum + pass_on[:, None, None] * earlier[1],
        jnp.maximum(earlier[2], document_marker),
    )


def local(
    tokens,
    doc_start,
    norm1_gain,
    qkv_weight,
    out_weight,
    norm2_gain,
    up_weight,
    down_weight,
    omega,
    cotangent,
):
    row_count, stretch_len, model_width = tokens.shape
    head_count = omega.shape[0]
    head_dim = omega.shape[1]
    token_count = row_count * stretch_len
    stream = tokens.astype(jnp.float32).reshape(token_count, model_width)
    same_doc, leading_document, last_doc, document_marker = row_masks(doc_start)
    normed_one, norm1_back = jax.vjp(layer_norm, stream, norm1_gain)
    normed_one_low = normed_one.astype(jnp.bfloat16)
    projected = jnp.dot(normed_one_low, qkv_weight, preferred_element_type=jnp.float32)
    head_split = projected.reshape(row_count, stretch_len, 3, head_count, head_dim)
    query_heads = head_split[:, :, 0]
    key_heads = head_split[:, :, 1]
    value_heads = head_split[:, :, 2]

    def both_features(query_part, key_part):
        return (features(query_part, omega), features(key_part, omega))

    (query_features, key_feat), feature_back = jax.vjp(both_features, query_heads, key_heads)

    def local_totals(key_part, value_part):
        return stretch_totals(key_part, value_part, last_doc)

    (state_sum, norm_sum), totals_back = jax.vjp(local_totals, key_feat, value_heads)
    empty_state = jnp.zeros_like(state_sum)
    empty_norm = jnp.zeros_like(norm_sum)
    empty_flag = jnp.zeros_like(document_marker)
    running_state, carry_norm, unused_flag = entering(
        (state_sum, norm_sum, document_marker),
        "seq",
        carry_on,
        (empty_state, empty_norm, empty_flag),
        False,
    )

    def local_mix(query_part, key_part, value_part, state_part, norm_part):
        return mix_rows(
            query_part, key_part, value_part, state_part, norm_part, same_doc, leading_document
        )

    mixed, mix_back = jax.vjp(
        local_mix, query_features, key_feat, value_heads, running_state, carry_norm
    )
    mixed_low = mixed.reshape(token_count, model_width).astype(jnp.bfloat16)
    branch = jnp.dot(mixed_low, out_weight, preferred_element_type=jnp.float32)
    middle = stream + branch
    normed_two, norm2_back = jax.vjp(layer_norm, middle, norm2_gain)
    normed_two_low = normed_two.astype(jnp.bfloat16)
    up_values = jnp.dot(normed_two_low, up_weight, preferred_element_type=jnp.float32)
    gelu_out, gelu_back = jax.vjp(exact_gelu, up_values)
    hidden = gelu_out.astype(jnp.bfloat16)
    ffn_out = jnp.dot(hidden, down_weight, preferred_element_type=jnp.float32)
    output = (middle + ffn_out).astype(jnp.bfloat16).reshape(row_count, stretch_len, model_width)
    incoming = cotangent.reshape(token_count, model_width)
    down_grad = jnp.einsum("tf,td->fd", hidden, incoming, preferred_element_type=jnp.float32)
    hidden_grad = jnp.einsum("td,fd->tf", incoming, down_weight, preferred_element_type=jnp.float32)
    (up_full,) = gelu_back(hidden_grad)
    up_grad_low = up_full.astype(jnp.bfloat16)
    up_grad = jnp.einsum(
        "td,tf->df", normed_two_low, up_grad_low, preferred_element_type=jnp.float32
    )
    normed_two_grad = jnp.einsum(
        "tf,df->td", up_grad_low, up_weight, preferred_element_type=jnp.float32
    )
    middle_part, norm2_grad = norm2_back(normed_two_grad)
    middle_grad = incoming.astype(jnp.float32) + middle_part
    middle_low = middle_grad.astype(jnp.bfloat16)
    out_grad = jnp.einsum("td,te->de", mixed_low, middle_low, preferred_element_type=jnp.float32)
    mixed_grad = jnp.einsum("te,de->td", middle_low, out_weight, preferred_element_type=jnp.float32)
    mixed_grad = mixed_grad.reshape(row_count, stretch_len, head_count, head_dim)
    query_feat_grad, key_feat_mix, value_mix, carry_state_grad, carry_norm_grad = mix_back(
        mixed_grad
    )
    later_state, later_norm, unused_later = entering(
        (carry_state_grad, carry_norm_grad, document_marker),
        "seq",
        carry_on,
        (empty_state, empty_norm, empty_flag),
        True,
    )
    key_feat_tot, value_tot = totals_back((later_state, later_norm))
    query_grad, key_grad = feature_back((query_feat_grad, key_feat_mix + key_feat_tot))
    value_grad = value_mix + value_tot
    projected_grad = jnp.stack((query_grad, key_grad, value_grad), axis=2)
    projected_grad = projected_grad.reshape(token_count, 3 * model_width).astype(jnp.bfloat16)
    qkv_grad = jnp.einsum(
        "td,te->de", normed_one_low, projected_grad, preferred_element_type=jnp.float32
    )
    normed_one_grad = jnp.einsum(
        "te,de->td", projected_grad, qkv_weight, preferred_element_type=jnp.float32
    )
    stream_part, norm1_grad = norm1_back(normed_one_grad)
    tokens_grad = (middle_grad + stream_part).reshape(row_count, stretch_len, model_width)
    device_count = lax.axis_size("dp") * lax.axis_size("seq")
    qkv_sum, out_sum, up_sum, down_sum, norm1_sum, norm2_sum = lax.psum(
        (qkv_grad, out_grad, up_grad, down_grad, norm1_grad, norm2_grad), ("dp", "seq")
    )
    return (
        output,
        tokens_grad,
        norm1_sum / device_count,
        qkv_sum / device_count,
        out_sum / device_count,
        norm2_sum / device_count,
        up_sum / device_count,
        down_sum / device_count,
    )


eps = 1e-05
f32 = jnp.float32
bf16 = jnp.bfloat16
AXES = ("dp", "seq")
GRID_DP, GRID_SEQ = 4, 8
ROOM = 56 * 2**20


def place(y, x, z, c):
    return (y * 2 + x) * GRID_SEQ + z * 2 + c


def pairs(move):
    return [
        (place(y, x, z, c), place(*move(y, x, z, c)))
        for y in range(2)
        for x in range(2)
        for z in range(4)
        for c in range(2)
    ]


INNER = pairs(lambda y, x, z, c: (y, x, 3 - z, c))
INNER = [(a, b) for a, b in INNER if (a % GRID_SEQ) // 2 in (1, 2)]
OUTWARD = pairs(lambda y, x, z, c: (y, x, z ^ 1, c))
OUTWARD = [(a, b) for a, b in OUTWARD if (a % GRID_SEQ) // 2 in (1, 2)]
ALONG_Z = {k: pairs(lambda y, x, z, c, k=k: (y, x, z ^ k, c)) for k in (1, 2, 3)}
CORES = pairs(lambda y, x, z, c: (y, x, z, 1 - c))
FIRST = pairs(lambda y, x, z, c: (y, 1 - x, z, c) if c == 0 else (1 - y, x, z, c))
SECOND = pairs(lambda y, x, z, c: (1 - y, x, z, c) if c == 0 else (y, 1 - x, z, c))


def send(value, perm, tag="send"):
    with jax.named_scope("t_" + tag):
        return lax.ppermute(value, AXES, perm)


def nn(a, b, precision=None):
    return lax.dot_general(
        a, b, (((1,), (0,)), ((), ())), precision=precision, preferred_element_type=f32
    )


def nt(a, b, precision=None):
    return lax.dot_general(
        a, b, (((1,), (1,)), ((), ())), precision=precision, preferred_element_type=f32
    )


def work(micros):
    return pl.CostEstimate(flops=int(micros * 1.16e9), bytes_accessed=0, transcendentals=0)


def here():
    dp, seq = lax.axis_index("dp"), lax.axis_index("seq")
    y, x, z, c = dp // 2, dp % 2, seq // 2, seq % 2
    return z, c, jnp.where(c == 0, x, y), jnp.where(c == 0, y, x)


def kernel_call(body, outs, args, scratch=(), name=None, micros=2, room=16, far=(), out=(), order=None, early=(), onto=(), where=pltpu.VMEM):
    vmem = pl.BlockSpec(memory_space=pltpu.VMEM)
    args = list(args)
    staged = len(args)
    args += list(onto)
    held = len(args)
    args += list(early) + list(order or ())
    ignored = len(args) - held
    outs = [*outs, ((8, 128), f32)]
    shapes = [
        jax.ShapeDtypeStruct(s, d) if n in far or n in out else pltpu.VMEM(s, d) for n, (s, d) in enumerate(outs)
    ]
    specs = [pl.BlockSpec(memory_space=pl.ANY) if n in far else vmem for n in range(len(outs))]
    results = len(outs) - 1

    def whole(*refs):
        refs, mark, rest = refs[: held + ignored + results], refs[held + ignored + results], refs[held + ignored + results + 1 :]
        mark[...] = jnp.zeros((8, 128), f32)
        body(*refs[:held], *refs[held + ignored :], *rest)

    *values, mark = pl.pallas_call(
        whole,
        out_shape=shapes,
        in_specs=[pl.BlockSpec(memory_space=pl.ANY) if staged <= n < held else vmem for n in range(len(args))],
        out_specs=specs,
        scratch_shapes=list(scratch),
        input_output_aliases={staged + n: n for n in range(len(onto))},
        compiler_params=pltpu.CompilerParams(vmem_limit_bytes=room * 2**20),
        name=name,
        cost_estimate=work(micros),
    )(*[a if staged <= n < held else pltpu.with_memory_space_constraint(a, where) for n, a in enumerate(args)])
    if order is not None:
        order[:] = [mark]
    return values


def pick(v, bit):
    return jnp.where(bit == 0, v[:, 0:64], v[:, 64:128])


def normalise(v):
    mean = jnp.mean(v, axis=-1, keepdims=True)
    centred = v - mean
    inv = lax.rsqrt(jnp.mean(centred * centred, axis=-1, keepdims=True) + eps)
    return centred * inv, inv


def normalise_back(e, n, inv):
    return (e - jnp.mean(e, axis=-1, keepdims=True) - n * jnp.mean(e * n, axis=-1, keepdims=True)) * inv


def doc_numbers(doc):
    at = lax.broadcasted_iota(jnp.int32, (128, 128), 0)
    to = lax.broadcasted_iota(jnp.int32, (128, 128), 1)
    upper = (at <= to).astype(f32)
    a8 = lax.broadcasted_iota(jnp.int32, (8, 8), 0)
    t8 = lax.broadcasted_iota(jnp.int32, (8, 8), 1)
    before = (t8 < a8).astype(f32)
    spread = jnp.broadcast_to(jnp.sum(doc, axis=1, keepdims=True), (8, 128))
    high = lax.Precision.HIGHEST
    rows = nn(doc, upper, high) + nn(before, spread, high)
    eye = (at == to).astype(f32)
    cols = nt(eye, rows, high)
    return rows, cols


def row_of(rows, lo, hi):
    return jnp.concatenate([rows[j : j + 1, :] for j in range(lo, hi)], axis=1)


def col_of(cols, lo, hi):
    return jnp.concatenate([cols[:, j : j + 1] for j in range(lo, hi)], axis=0)


def gelu_parts(u):
    return 0.5 + 0.5 * lax.erf(u * 0.7071067811865476), jnp.exp(-0.5 * u * u) * 0.3989422804014327


def prepare(tokens, doc, cot, message, cot_o):
    message[0:128, :] = tokens[...].astype(f32)
    message[128:136, :] = jnp.zeros((8, 512), f32)
    message[128:129, 0:128] = doc[...].astype(f32)
    cot_o[...] = cot[...].astype(f32)


def join(*refs):
    at = 0
    out = refs[-1]
    for ref in refs[:-1]:
        out[at : at + ref.shape[0]] = ref[...]
        at += ref.shape[0]


def joined(order, *values, early=()):
    values = [v[None] if v.ndim == 2 else v for v in values]
    shape = (sum(v.shape[0] for v in values),) + values[0].shape[1:]
    return kernel_call(join, [(shape, f32)], values, name="join", micros=0, order=order, early=early)[0]


def gate(*refs):
    half = len(refs) // 2
    for ref, out in zip(refs[:half], refs[half:]):
        out[...] = ref[...]


def choose_far(near, far, out):
    z, _, _, _ = here()
    inner = (z == 1) | (z == 2)
    for n in range(2):
        out[n] = jnp.where(inner, near[1 - n], far[n])


def head_forward(t0, t1, t2, t3, p0, p1, p2, p3, gain, w, omega,
                 keep, give, phq_o, phk_o, qk_o, v_o, mxd_o, doc_o, nt_o, low):
    z, c, _, _ = here()
    wh = jnp.concatenate([pick(w[:, pl.ds(pl.multiple_of(part * 512 + z * 128, 128), 128)], c) for part in range(3)], axis=1)
    g = gain[...]
    for k, (mine, theirs) in enumerate(((t0, p0), (t1, p1), (t2, p2), (t3, p3))):
        for ref, core in ((mine, c), (theirs, 1 - c)):
            chunk = 2 * jnp.bitwise_xor(z, k) + core
            n, _ = normalise(ref[0:128, :])
            low[pl.ds(pl.multiple_of(chunk * 128, 128), 128), :] = (n * g).astype(bf16)
            doc_o[pl.ds(chunk, 1), :] = ref[128:129, 0:128]
    rows, cols = doc_numbers(doc_o[...])
    nt_o[...] = jnp.transpose(low[:, pl.ds(pl.multiple_of(c * 256, 256), 256)])
    s = 64 ** -0.25
    om = omega[2 * z + c]
    oh = om.astype(bf16)
    ol = (om - oh.astype(f32)).astype(bf16)
    stack = jnp.concatenate([oh, oh, ol], axis=0)

    def feature(v):
        v = v * s
        hi = v.astype(bf16)
        lo = (v - hi.astype(f32)).astype(bf16)
        proj = nn(jnp.concatenate([hi, lo, hi], axis=1), stack)
        return jnp.exp(proj - 0.5 * jnp.sum(v * v, axis=-1, keepdims=True))

    for b in range(4):
        at = pl.ds(256 * b, 256)
        pr = nn(low[at, :], wh)
        qk_o[at, :] = pr[:, 0:128]
        v_o[at, :] = pr[:, 128:192].astype(bf16)
        phq_o[at, :] = feature(pr[:, 0:64]).astype(bf16)
        phk_o[at, :] = feature(pr[:, 64:128]).astype(bf16)
    for b in range(4):
        at = pl.ds(256 * b, 256)
        n = 256 * (b + 1)
        scores = nt(phq_o[at, :], phk_o[0:n, :])
        i = lax.broadcasted_iota(jnp.int32, (256, n), 0) + 256 * b
        j = lax.broadcasted_iota(jnp.int32, (256, n), 1)
        same = (col_of(cols, 2 * b, 2 * b + 2) == row_of(rows, 0, 2 * b + 2)) & (i >= j)
        scores = jnp.where(same, scores, 0.0)
        inv = 1.0 / jnp.sum(scores, axis=-1, keepdims=True)
        mixed = nn(scores.astype(bf16), v_o[0:n, :]) * inv
        mxd_o[at, :] = jnp.concatenate([mixed, jnp.broadcast_to(inv, (256, 64))], axis=1)
        top, bottom = mixed[0:128, :], mixed[128:256, :]
        keep[b] = jnp.where(c == 0, top, bottom)
        give[b] = jnp.where(c == 0, bottom, top)


def pack_pairs(keep, got, b0, b1, b2, b3):
    z, c, _, _ = here()
    for k, out in enumerate((b0, b1, b2, b3)):
        j = jnp.bitwise_xor(z, k)
        a, b = keep[j], got[j]
        out[...] = jnp.where(c == 0, jnp.concatenate([a, b], axis=1), jnp.concatenate([b, a], axis=1))


def unpack_pairs(b0, b1, b2, b3, keep, give):
    z, c, _, _ = here()
    for k, ref in enumerate((b0, b1, b2, b3)):
        j = jnp.bitwise_xor(z, k)
        a, b = ref[:, 0:64], ref[:, 64:128]
        keep[j] = jnp.where(c == 0, a, b)
        give[j] = jnp.where(c == 0, b, a)


def middle_part(b0, b1, b2, b3, tokens, wo, gain, mixed_o, middle_o, normed_o):
    z, _, _, _ = here()
    for k, ref in enumerate((b0, b1, b2, b3)):
        j = jnp.bitwise_xor(z, k)
        mixed_o[:, pl.ds(pl.multiple_of(j * 128, 128), 128)] = ref[...].astype(bf16)
    middle = tokens[...].astype(f32) + nn(mixed_o[...], wo[...])
    middle_o[...] = middle
    n, _ = normalise(middle)
    normed_o[...] = (n * gain[...]).astype(bf16).astype(f32)


def feed_forward(mixed, middle, normed, cot, wu, wd, wo, gain,
                 out_o, mg_o, ml_o, ex0, ex1, ex2, b0, b1, b2, b3, scr):
    z, c, _, _ = here()
    x = normed[...].astype(bf16)
    inc = cot[...]
    total = middle[...]
    back = jnp.zeros((128, 512), f32)
    for u in range(4):
        at = pl.ds(512 * u, 512)
        wub, wdb = wu[:, at], wd[at, :]
        up = nn(x, wub)
        cdf, pdf = gelu_parts(up)
        total = total + nn((up * cdf).astype(bf16), wdb)
        ug = ((cdf + up * pdf) * nt(inc, wdb)).astype(bf16)
        back = back + nt(ug, wub)
    out_o[...] = total.astype(bf16)
    n, inv = normalise(middle[...])
    mg = inc.astype(f32) + normalise_back(gain[...] * back, n, inv)
    mg_o[...] = mg
    low = mg.astype(bf16)
    ml_o[...] = low
    ex0[...] = mixed[:, pl.ds(pl.multiple_of((1 - c) * 256, 256), 256)].astype(f32)
    ex1[...] = low[:, 0:256].astype(f32)
    ex2[...] = low[:, 256:512].astype(f32)
    scr[...] = nt(low, wo[...])
    for k, ref in enumerate((b0, b1, b2, b3)):
        j = jnp.bitwise_xor(z, k)
        ref[...] = scr[:, pl.ds(pl.multiple_of(j * 128, 128), 128)]


def out_part(mixed, mlow, got0, got1, got2, keep, give, scr):
    _, c, first, _ = here()
    mine = mixed[:, pl.ds(pl.multiple_of(c * 256, 256), 256)].astype(f32)
    left = jnp.transpose(jnp.concatenate([mine, got0[...]], axis=0)).astype(bf16)
    theirs = jnp.concatenate([got1[...], got2[...]], axis=1).astype(bf16)
    right = jnp.concatenate([mlow[...], theirs], axis=0)
    scr[...] = nn(left, right)
    keep[...] = scr[pl.ds(pl.multiple_of(first * 128, 128), 128), :]
    give[...] = scr[pl.ds(pl.multiple_of((1 - first) * 128, 128), 128), :]


def add_last(mine, got, out):
    out[...] = (mine[...] + got[...]) * (1.0 / 32)


def join_pieces(p0, p1, p2, p3, out):
    z, _, _, _ = here()
    parts = (p0, p1, p2, p3)
    total = (p0[:, 384:896] + p1[:, 384:896]) + (p2[:, 384:896] + p3[:, 384:896])
    for k, ref in enumerate(parts):
        j = jnp.bitwise_xor(z, k)
        out[k, :, 0:384] = ref[:, 0:384]
        block = total[:, 0:128]
        for n in range(1, 4):
            block = jnp.where(j == n, total[:, 128 * n : 128 * n + 128], block)
        out[k, :, 384:512] = block


def head_backward(keep, got, phq, phk, qk, v, mxd, doc, omega, pg0, pg1, pg2, r_scr, m_scr, pg_o):
    z, c, _, _ = here()
    for b in range(4):
        a, g = keep[b], got[b]
        at = pl.ds(256 * b, 256)
        dm = jnp.concatenate([jnp.where(c == 0, a, g), jnp.where(c == 0, g, a)], axis=0)
        r = dm * mxd[at, 64:128]
        r_scr[at, :] = r.astype(bf16)
        m_scr[at, :] = r * mxd[at, 0:64]
    rows, cols = doc_numbers(doc[...])
    ones = jnp.ones((8, 64), f32)
    s = 64 ** -0.25
    om = omega[2 * z + c].astype(bf16)

    def feature_back(ph, grad, base):
        a = ph.astype(f32) * grad
        return s * nt(a.astype(bf16), om) - (s * s) * base * jnp.sum(a, axis=-1, keepdims=True)

    for b in range(4):
        at = pl.ds(256 * b, 256)
        n = 256 * (b + 1)
        i = lax.broadcasted_iota(jnp.int32, (256, n), 0) + 256 * b
        j = lax.broadcasted_iota(jnp.int32, (256, n), 1)
        same = (col_of(cols, 2 * b, 2 * b + 2) == row_of(rows, 0, 2 * b + 2)) & (i >= j)
        ds = nt(r_scr[at, :], v[0:n, :]) - jnp.sum(m_scr[at, :], axis=-1, keepdims=True)
        ds = jnp.where(same, ds, 0.0).astype(bf16)
        qg = feature_back(phq[at, :], nn(ds, phk[0:n, :]), qk[at, 0:64])
        m = 1024 - 256 * b
        later = pl.ds(256 * b, m)
        j2 = lax.broadcasted_iota(jnp.int32, (256, m), 0)
        i2 = lax.broadcasted_iota(jnp.int32, (256, m), 1)
        same2 = (col_of(cols, 2 * b, 2 * b + 2) == row_of(rows, 2 * b, 8)) & (i2 >= j2)
        scores = jnp.where(same2, nt(phk[at, :], phq[later, :]), 0.0).astype(bf16)
        vg = nn(scores, r_scr[later, :])
        mr = nt(ones, m_scr[later, :], lax.Precision.HIGHEST)[0:1, :]
        ds2 = jnp.where(same2, nt(v[at, :], r_scr[later, :]) - mr, 0.0).astype(bf16)
        kg = feature_back(phk[at, :], nn(ds2, phq[later, :]), qk[at, 64:128])
        rnd = lambda t: t.astype(bf16).astype(f32)
        pg_o[at, :] = rnd(jnp.concatenate([qg, kg], axis=1))
        pg_o[pl.ds(1024 + 256 * (b % 2), 256), 64 * (b // 2) : 64 * (b // 2) + 64] = rnd(vg)
    for n, out in enumerate((pg0, pg1, pg2)):
        out[...] = pg_o[512 * n : 512 * n + 512, :]


def weight_part(m0, m1, m2, t0, t1, t2, nt_low, okeep, ogive, q0, q1, q2, q3, keep, give, scr, g_scr):
    z, c, first, _ = here()
    for b in range(4):
        at = pl.ds(256 * b, 256)
        half = pl.ds(256 * (b % 2), 256)
        lanes = slice(64 * (b // 2), 64 * (b // 2) + 64)
        a, t = ((m0, t0), (m1, t1))[b // 2]
        a, t = a[half, :], t[half, :]
        av, tv = m2[half, lanes], t2[half, lanes]
        h0 = jnp.where(c == 0, a, t)
        h1 = jnp.where(c == 0, t, a)
        scr[at, 0:128] = jnp.concatenate([h0[:, 0:64], h1[:, 0:64]], axis=1)
        scr[at, 128:256] = jnp.concatenate([h0[:, 64:128], h1[:, 64:128]], axis=1)
        scr[at, 256:384] = jnp.concatenate([jnp.where(c == 0, av, tv), jnp.where(c == 0, tv, av)], axis=1)
    for k, ref in enumerate((q0, q1, q2, q3)):
        chunk = 2 * jnp.bitwise_xor(z, k) + c
        ref[...] = scr[pl.ds(pl.multiple_of(chunk * 128, 128), 128), :]
    g_scr[...] = nn(nt_low[...], scr[...].astype(bf16))
    keep[:, 0:384] = g_scr[pl.ds(pl.multiple_of(first * 128, 128), 128), :]
    give[:, 0:384] = g_scr[pl.ds(pl.multiple_of((1 - first) * 128, 128), 128), :]
    keep[:, 384:896] = okeep[...]
    give[:, 384:896] = ogive[...]


def tokens_part(q0, q1, q2, q3, mg, tokens, w, gain, out_o, scr):
    z, _, _, _ = here()
    for k, ref in enumerate((q0, q1, q2, q3)):
        j = jnp.bitwise_xor(z, k)
        for part in range(3):
            scr[:, pl.ds(pl.multiple_of(part * 512 + j * 128, 128), 128)] = ref[:, 128 * part : 128 * part + 128].astype(bf16)
    n, inv = normalise(tokens[...].astype(f32))
    e = gain[...] * nt(scr[...], w[...])
    out_o[...] = mg[...] + normalise_back(e, n, inv)


def add_split(mine, got, keep, give):
    _, _, _, second = here()
    a = pl.ds(pl.multiple_of(second * 64, 64), 64)
    b = pl.ds(pl.multiple_of((1 - second) * 64, 64), 64)
    keep[...] = mine[a, :] + got[a, :]
    give[...] = mine[b, :] + got[b, :]


def ffn_narrow(count, *refs):
    xs, cs, (xb, cb) = refs[:count], refs[count : 2 * count], refs[2 * count :]
    at = 0
    for x, cc in zip(xs, cs):
        for i in range(x.shape[0]):
            xb[pl.ds(at, 128), :] = x[i].astype(bf16)
            cb[pl.ds(at, 128), :] = cc[i].astype(bf16)
            at += 128


def ffn_weights(unit, mine, first, last, xb, cb, wu, wd, *refs):
    if not first:
        before, *refs = refs
    if last:
        theirs, out, up_o = refs
    else:
        (out,) = refs
    _, c, _, _ = here()
    core = c if mine else 1 - c
    place = pl.ds(pl.multiple_of(core * 1024 + 256 * unit, 256), 256)
    wut, wdu = jnp.transpose(wu[:, place]), wd[place, :]
    x, inc = xb[...], cb[...]
    up = nt(wut, x)
    hg = nt(wdu, inc)
    cdf, pdf = gelu_parts(up)
    total_up = nn(((cdf + up * pdf) * hg).astype(bf16), x)
    total_down = nn((up * cdf).astype(bf16), inc)
    if not first:
        total_up = total_up + before[0:256, :]
        total_down = total_down + before[256:512, :]
    if last:
        total_up = (total_up + theirs[0:256, :]) * (1.0 / 32)
        total_down = (total_down + theirs[256:512, :]) * (1.0 / 32)
        up_o[...] = jnp.transpose(total_up)
        part = jnp.sum(total_up * wut.astype(f32), axis=0, keepdims=True)
        out[512:520, :] = jnp.broadcast_to(part, (8, 512))
    out[0:256, :] = total_up
    out[256:512, :] = total_down


def place_mine(*refs):
    ups, both = refs[0:4], refs[4:8]
    up_o, down_o, sems = refs[8:]
    _, c, _, _ = here()
    copies = []
    for n in range(4):
        at = pl.ds(pl.multiple_of(c * 1024 + 256 * n, 256), 256)
        copies.append(pltpu.make_async_copy(ups[n], up_o.at[:, at], sems.at[2 * n]))
        copies.append(pltpu.make_async_copy(both[n].at[256:512, :], down_o.at[at, :], sems.at[2 * n + 1]))
    for copy in copies:
        copy.start()
    for copy in copies:
        copy.wait()


def place_theirs(m0, m1, m2, m3, b0, b1, b2, b3, gain2, up_in, down_in, up_o, down_o, gain_o, ups, sems):
    _, c, _, _ = here()
    copies = []
    for n, both in enumerate((b0, b1, b2, b3)):
        at = pl.ds(pl.multiple_of((1 - c) * 1024 + 256 * n, 256), 256)
        copies.append(pltpu.make_async_copy(both.at[256:512, :], down_o.at[at, :], sems.at[2 * n]))
        copies[-1].start()
    for n, both in enumerate((b0, b1, b2, b3)):
        at = pl.ds(pl.multiple_of((1 - c) * 1024 + 256 * n, 256), 256)
        ups[n] = jnp.transpose(both[0:256, :])
        copies.append(pltpu.make_async_copy(ups.at[n], up_o.at[:, at], sems.at[2 * n + 1]))
        copies[-1].start()
    total = jnp.zeros((1, 512), f32)
    for ref in (m0, m1, m2, m3, b0, b1, b2, b3):
        total = total + ref[512:513, :]
    gain_o[...] = total / gain2[...]
    for copy in copies:
        copy.wait()


def finish(a, b, ca, cb, w, gain, qkv_o, out_o, gain_o):
    z, c, first, second = here()
    for n in range(4):
        for core, ref, r1, r2 in ((c, (a, b)[n // 2], first, second), (1 - c, (ca, cb)[n // 2], second, first)):
            row = core * 256 + jnp.bitwise_xor(r1, n % 2) * 128 + jnp.bitwise_xor(r2, n // 2) * 64
            rows = pl.ds(pl.multiple_of(row, 64), 64)
            for k in range(4):
                j = jnp.bitwise_xor(z, k)
                piece = ref.at[4 * (n % 2) + k]
                for part in range(3):
                    at = pl.ds(pl.multiple_of(part * 512 + j * 128, 128), 128)
                    qkv_o[rows, at] = piece[:, 128 * part : 128 * part + 128]
                out_o[rows, pl.ds(pl.multiple_of(j * 128, 128), 128)] = piece[:, 384:512]
    for r in range(4):
        rows = pl.ds(128 * r, 128)
        acc = jnp.zeros((128, 128), f32)
        for j in range(12):
            lanes = pl.ds(128 * j, 128)
            acc = acc + w[rows, lanes].astype(f32) * qkv_o[rows, lanes]
        lanes = pl.ds(128 * r, 128)
        gain_o[0:1, lanes] = jnp.sum(jnp.transpose(acc), axis=0, keepdims=True) / gain[0:1, lanes]


def across(values):
    return [send(v, CORES) for v in values]


def local_fast(tokens, doc_start, norm1_gain, qkv_weight, out_weight, norm2_gain, up_weight, down_weight, omega, cotangent):
    g1, g2 = norm1_gain.reshape(1, 512), norm2_gain.reshape(1, 512)
    tok, cot = tokens[0], cotangent[0]
    order = []
    call = functools.partial(kernel_call, order=order)
    join = functools.partial(joined, order)
    block = ((128, 128), f32)

    def later(*values):
        return call(gate, [(v.shape, v.dtype) for v in values], values, name="gate", micros=0)

    def wait(*values):
        call(gate, [], [], name="gate", micros=0, early=values)

    def pause(micros):
        call(gate, [], [], name="pause", micros=micros)

    def narrow(xs, cs):
        rows = 128 * sum(v.shape[0] for v in xs)
        return call(functools.partial(ffn_narrow, len(xs)), [((rows, 512), bf16)] * 2, [*xs, *cs], name="ffn_narrow", micros=0)

    def ffn(unit, mine, xc, before=None, theirs=None, micros=0):
        first, last = before is None, theirs is not None
        outs = [((520, 512), f32), ((512, 256), f32)] if last else [((512, 512), f32)]
        more = ([] if first else [before]) + ([theirs] if last else [])
        got = call(
            functools.partial(ffn_weights, unit, mine, first, last), outs, [*xc, up_weight, down_weight, *more],
            (), "ffn_weights", micros, 24,
        )
        return got if last else got[0]

    message, cot_wide = call(prepare, [((136, 512), f32), ((128, 512), f32)], [tok, doc_start, cot], name="prepare", where=pltpu.HBM)
    t = [message] + [send(message, ALONG_Z[k], "tok") for k in (1, 2, 3)]
    ca = join(cot_wide, send(cot_wide, ALONG_Z[1], "c1"), early=t)
    p = [send(v, CORES, "tok") for v in t]
    ca_first = send(ca, FIRST, "ca")
    keep, give, phq, phk, qk, v, mxd, doc, nt_low = call(
        head_forward,
        [((4, 128, 64), f32), ((4, 128, 64), f32), ((1024, 256), bf16), ((1024, 256), bf16), ((1024, 128), f32),
         ((1024, 64), bf16), ((1024, 128), f32), ((8, 128), f32), ((256, 1024), bf16)],
        [*t, *p, g1, qkv_weight, omega], [pltpu.VMEM((1024, 512), bf16)], "head_forward", 2,
    )
    b = call(pack_pairs, [block] * 4, [keep, send(give, CORES, "give")], name="pack_pairs", micros=0)
    b = [b[0]] + [send(b[k], ALONG_Z[k], "mixed") for k in (1, 2, 3)]
    pause(0.8)
    ca_two = join(ca, ca_first, early=[up_weight, down_weight, out_weight])
    ca_other = send(ca_two, SECOND, "ca")
    mixed, middle, normed = call(
        middle_part, [((128, 512), bf16), ((128, 512), f32), ((128, 512), f32)], [*b, tok, out_weight, g2],
        name="middle_part", micros=2.5,
    )
    output, mg, mlow, ex0, ex1, ex2, *b = call(
        feed_forward,
        [((128, 512), bf16), ((128, 512), f32), ((128, 512), bf16)] + [((128, 256), f32)] * 3 + [block] * 4,
        [mixed, middle, normed, cot, up_weight, down_weight, out_weight, g2], [pltpu.VMEM((128, 512), f32)],
        "feed_forward", 1.2, out=(0,),
    )
    b = [b[0]] + [send(b[k], ALONG_Z[k], "mg") for k in (1, 2, 3)]
    ex_other = [send(w, CORES, "ex") for w in (ex0, ex1, ex2)]
    pause(1.5)
    okeep, ogive = call(out_part, [((128, 512), f32)] * 2, [mixed, mlow, *ex_other],
                        [pltpu.VMEM((256, 512), f32)], "out_part", micros=0)
    ca_late, normed = later(ca, normed)
    keep, give = call(unpack_pairs, [((4, 128, 64), f32)] * 2, b, name="unpack_pairs", micros=0)
    got = send(give, CORES, "give")
    x1 = send(normed, ALONG_Z[1], "x1")
    c_inner = send(ca_late, INNER, "c")
    pg = call(
        head_backward, [((512, 128), f32)] * 3, [keep, got, phq, phk, qk, v, mxd, doc, omega],
        [pltpu.VMEM((1024, 64), bf16), pltpu.VMEM((1024, 64), f32), pltpu.VMEM((1536, 128), f32)], "head_backward", 4,
    )
    pg_other = [send(w, CORES, "pg") for w in pg]
    c_a = later(ca_two, ca_other)
    xa = join(normed, x1)
    xa_first = send(xa, FIRST, "xa")
    *q, keep, give = call(
        weight_part, [((128, 384), f32)] * 4 + [((128, 896), f32)] * 2, [*pg, *pg_other, nt_low, okeep, ogive],
        [pltpu.VMEM((1024, 384), f32), pltpu.VMEM((256, 384), f32)], "weight_part", micros=0,
    )
    got = send(give, FIRST, "rs")
    c_inner, xa_late = later(c_inner, xa)
    c_outer = send(c_inner, OUTWARD, "c")
    x_inner = send(xa_late, INNER, "x")
    pause(4.7)
    keep, give = call(add_split, [((64, 896), f32)] * 2, [keep, got], name="add_split", micros=0)
    got = send(give, SECOND, "rs")
    xa_two = join(xa, xa_first)
    xa_other = send(xa_two, SECOND, "xa")
    pause(2.4)
    (cb,) = call(choose_far, [((2, 128, 512), f32)], [c_inner, c_outer], name="choose_far", micros=0)
    cb_first = send(cb, FIRST, "cb")
    (x_inner,) = later(x_inner)
    x_outer = send(x_inner, OUTWARD, "x")
    (piece,) = call(add_last, [((64, 896), f32)], [keep, got], name="add_last", micros=0)
    pause(8.2)
    x_a = later(xa_two, xa_other)
    cb_two = join(cb, cb_first)
    cb_other = send(cb_two, SECOND, "cb")
    (piece,) = later(piece)
    piece_line = [send(piece, ALONG_Z[k], "piece") for k in (1, 2, 3)]
    x_now = narrow(x_a, c_a)
    total = {}
    for u in range(4):
        total[u, False] = ffn(u, False, x_now)
    (xb,) = call(choose_far, [((2, 128, 512), f32)], [x_inner, x_outer], name="choose_far", micros=0)
    xb_first = send(xb, FIRST, "xb")
    for u in range(4):
        total[u, True] = ffn(u, True, x_now)
    (pieces,) = call(join_pieces, [((4, 64, 512), f32)], [piece, *piece_line], name="join_pieces", micros=4.6)
    pieces_first = send(pieces, FIRST, "piece")
    xb_two = join(xb, xb_first)
    xb_other = send(xb_two, SECOND, "xb")
    pause(2.5)
    c_b = later(cb_two, cb_other)
    pause(6.4)
    q = [q[0]] + [send(w, ALONG_Z[k], "q") for k, w in zip((1, 2, 3), later(*q[1:]))]
    x_now = narrow([xb_two], c_b[:1])
    total = {key: ffn(*key, x_now, value) for key, value in total.items()}
    pieces = [join(pieces, pieces_first)]
    pieces.append(send(pieces[0], SECOND, "piece"))
    (tokens_grad,) = call(
        tokens_part, [((128, 512), f32)], [*q, mg, tok, qkv_weight, g1], [pltpu.VMEM((128, 1536), bf16)],
        "tokens_part", micros=0, out=(0,),
    )
    pause(3.5)
    x_b = later(xb_other)
    x_now = narrow(x_b, c_b[1:])
    others = [send(ffn(u, False, x_now, total[u, False], micros=0.3), CORES, "part") for u in range(4)]
    wait(pieces[1])
    both, ups = zip(*[ffn(u, True, x_now, total[u, True], others[u], micros=1.2) for u in range(4)])
    both_other = [send(w, CORES, "both") for w in both]
    dma = [pltpu.SemaphoreType.DMA((8,))]
    up_grad, down_grad = call(
        place_mine, [((512, 2048), f32), ((2048, 512), f32)], [*ups, *both], dma, "place_mine", 0, far=(0, 1),
    )
    qkv_grad, out_grad, norm1_grad = call(
        finish, [((512, 1536), f32), ((512, 512), f32), ((1, 512), f32)],
        [*pieces, *[send(w, CORES, "piece") for w in pieces], qkv_weight, g1], (), "finish", 0, out=(0, 1, 2),
    )
    up_grad, down_grad, norm2_grad = call(
        place_theirs, [((512, 2048), f32), ((2048, 512), f32), ((1, 512), f32)], [*both, *both_other, g2],
        [pltpu.VMEM((4, 512, 256), f32), *dma], "place_theirs", 0, far=(0, 1), out=(2,), onto=(up_grad, down_grad),
    )
    return (output[None], tokens_grad[None], norm1_grad[0], qkv_grad, out_grad, norm2_grad[0], up_grad, down_grad)


def solution(mesh):
    placed = (
        P("dp", "seq", None),
        P("dp", "seq"),
        P(),
        P(),
        P(),
        P(),
        P(),
        P(),
        P(),
        P("dp", "seq", None),
    )
    fits = mesh.shape["dp"] == GRID_DP and mesh.shape["seq"] == GRID_SEQ
    return jax.shard_map(
        local_fast if fits else local,
        mesh=mesh,
        in_specs=placed,
        out_specs=(P("dp", "seq", None), P("dp", "seq", None), P(), P(), P(), P(), P(), P()),
        check_vma=False,
    )
```

```python
import functools

import jax
import jax.numpy as jnp
from jax import lax
from jax.experimental import pallas as pl
from jax.experimental.pallas import tpu as pltpu
from jax.sharding import PartitionSpec as P

norm_eps = 1e-05
highest_precision = lax.Precision.HIGHEST


def entering(value, axis, join, neutral, backward):
    count, mine = (lax.axis_size(axis), lax.axis_index(axis))
    pieces = jax.tree.map(lambda part: lax.all_gather(part, axis), value)
    if backward:
        pieces = jax.tree.map(lambda part: part[::-1], pieces)
        mine = count - 1 - mine
    running = jax.tree.map(
        lambda part, zero: jnp.full_like(part, 0) + jnp.asarray(zero, part.dtype), value, neutral
    )

    def hop(position, running):
        longer = join(running, jax.tree.map(lambda part: part[position], pieces))
        return jax.tree.map(lambda new, old: jnp.where(position < mine, new, old), longer, running)

    return lax.fori_loop(0, count - 1, hop, running)


def layer_norm(values, gain):
    average = jnp.mean(values, axis=-1, keepdims=True)
    centred = values - average
    spread_sq = jnp.mean(centred * centred, axis=-1, keepdims=True)
    return centred * lax.rsqrt(spread_sq + norm_eps) * gain


def features(head_values, omega):
    width_dim = head_values.shape[-1]
    scaled = head_values * width_dim ** (-0.25)
    projection = jnp.einsum("...hd,hdm->...hm", scaled, omega, precision=highest_precision)
    half_square = 0.5 * jnp.sum(scaled * scaled, axis=-1, keepdims=True)
    return jnp.exp(projection - half_square)


def exact_gelu(values):
    return jax.nn.gelu(values, approximate=False)


def row_masks(doc_start):
    stretch_len = doc_start.shape[1]
    doc_index = jnp.cumsum(doc_start, axis=1)
    position = jnp.arange(stretch_len, dtype=jnp.int32)
    same_doc = (doc_index[:, :, None] == doc_index[:, None, :]) & (
        position[None, :, None] >= position[None, None, :]
    )
    leading_document = (doc_index == 0).astype(jnp.float32)
    last_doc = (doc_index == doc_index[:, -1:]).astype(jnp.float32)
    document_marker = (doc_index[:, -1] > 0).astype(jnp.float32)
    return (same_doc.astype(jnp.float32), leading_document, last_doc, document_marker)


def mix_rows(
    query_features, key_feat, value_heads, running_state, carry_norm, same_doc, leading_document
):
    scores = (
        jnp.einsum("rihm,rjhm->rhij", query_features, key_feat, precision=highest_precision)
        * same_doc[:, None]
    )
    attention_numerator = jnp.einsum(
        "rhij,rjhd->rihd", scores, value_heads, precision=highest_precision
    )
    attention_numerator = attention_numerator + leading_document[:, :, None, None] * jnp.einsum(
        "rihm,rhmd->rihd", query_features, running_state, precision=highest_precision
    )
    denominator = jnp.transpose(jnp.sum(scores, axis=-1), (0, 2, 1))
    denominator = denominator + leading_document[:, :, None] * jnp.einsum(
        "rihm,rhm->rih", query_features, carry_norm, precision=highest_precision
    )
    return attention_numerator / denominator[..., None]


def stretch_totals(key_feat, value_heads, last_doc):
    key_masked_rows = key_feat * last_doc[:, :, None, None]
    state_sum = jnp.einsum(
        "rchm,rchd->rhmd", key_masked_rows, value_heads, precision=highest_precision
    )
    return (state_sum, jnp.sum(key_masked_rows, axis=1))


def carry_on(earlier, later):
    state_sum, norm_sum, document_marker = later
    pass_on = 1.0 - document_marker
    return (
        state_sum + pass_on[:, None, None, None] * earlier[0],
        norm_sum + pass_on[:, None, None] * earlier[1],
        jnp.maximum(earlier[2], document_marker),
    )


def local(
    tokens,
    doc_start,
    norm1_gain,
    qkv_weight,
    out_weight,
    norm2_gain,
    up_weight,
    down_weight,
    omega,
    cotangent,
):
    row_count, stretch_len, model_width = tokens.shape
    head_count = omega.shape[0]
    head_dim = omega.shape[1]
    token_count = row_count * stretch_len
    stream = tokens.astype(jnp.float32).reshape(token_count, model_width)
    same_doc, leading_document, last_doc, document_marker = row_masks(doc_start)
    normed_one, norm1_back = jax.vjp(layer_norm, stream, norm1_gain)
    normed_one_low = normed_one.astype(jnp.bfloat16)
    projected = jnp.dot(normed_one_low, qkv_weight, preferred_element_type=jnp.float32)
    head_split = projected.reshape(row_count, stretch_len, 3, head_count, head_dim)
    query_heads = head_split[:, :, 0]
    key_heads = head_split[:, :, 1]
    value_heads = head_split[:, :, 2]

    def both_features(query_part, key_part):
        return (features(query_part, omega), features(key_part, omega))

    (query_features, key_feat), feature_back = jax.vjp(both_features, query_heads, key_heads)

    def local_totals(key_part, value_part):
        return stretch_totals(key_part, value_part, last_doc)

    (state_sum, norm_sum), totals_back = jax.vjp(local_totals, key_feat, value_heads)
    empty_state = jnp.zeros_like(state_sum)
    empty_norm = jnp.zeros_like(norm_sum)
    empty_flag = jnp.zeros_like(document_marker)
    running_state, carry_norm, unused_flag = entering(
        (state_sum, norm_sum, document_marker),
        "seq",
        carry_on,
        (empty_state, empty_norm, empty_flag),
        False,
    )

    def local_mix(query_part, key_part, value_part, state_part, norm_part):
        return mix_rows(
            query_part, key_part, value_part, state_part, norm_part, same_doc, leading_document
        )

    mixed, mix_back = jax.vjp(
        local_mix, query_features, key_feat, value_heads, running_state, carry_norm
    )
    mixed_low = mixed.reshape(token_count, model_width).astype(jnp.bfloat16)
    branch = jnp.dot(mixed_low, out_weight, preferred_element_type=jnp.float32)
    middle = stream + branch
    normed_two, norm2_back = jax.vjp(layer_norm, middle, norm2_gain)
    normed_two_low = normed_two.astype(jnp.bfloat16)
    up_values = jnp.dot(normed_two_low, up_weight, preferred_element_type=jnp.float32)
    gelu_out, gelu_back = jax.vjp(exact_gelu, up_values)
    hidden = gelu_out.astype(jnp.bfloat16)
    ffn_out = jnp.dot(hidden, down_weight, preferred_element_type=jnp.float32)
    output = (middle + ffn_out).astype(jnp.bfloat16).reshape(row_count, stretch_len, model_width)
    incoming = cotangent.reshape(token_count, model_width)
    down_grad = jnp.einsum("tf,td->fd", hidden, incoming, preferred_element_type=jnp.float32)
    hidden_grad = jnp.einsum("td,fd->tf", incoming, down_weight, preferred_element_type=jnp.float32)
    (up_full,) = gelu_back(hidden_grad)
    up_grad_low = up_full.astype(jnp.bfloat16)
    up_grad = jnp.einsum(
        "td,tf->df", normed_two_low, up_grad_low, preferred_element_type=jnp.float32
    )
    normed_two_grad = jnp.einsum(
        "tf,df->td", up_grad_low, up_weight, preferred_element_type=jnp.float32
    )
    middle_part, norm2_grad = norm2_back(normed_two_grad)
    middle_grad = incoming.astype(jnp.float32) + middle_part
    middle_low = middle_grad.astype(jnp.bfloat16)
    out_grad = jnp.einsum("td,te->de", mixed_low, middle_low, preferred_element_type=jnp.float32)
    mixed_grad = jnp.einsum("te,de->td", middle_low, out_weight, preferred_element_type=jnp.float32)
    mixed_grad = mixed_grad.reshape(row_count, stretch_len, head_count, head_dim)
    query_feat_grad, key_feat_mix, value_mix, carry_state_grad, carry_norm_grad = mix_back(
        mixed_grad
    )
    later_state, later_norm, unused_later = entering(
        (carry_state_grad, carry_norm_grad, document_marker),
        "seq",
        carry_on,
        (empty_state, empty_norm, empty_flag),
        True,
    )
    key_feat_tot, value_tot = totals_back((later_state, later_norm))
    query_grad, key_grad = feature_back((query_feat_grad, key_feat_mix + key_feat_tot))
    value_grad = value_mix + value_tot
    projected_grad = jnp.stack((query_grad, key_grad, value_grad), axis=2)
    projected_grad = projected_grad.reshape(token_count, 3 * model_width).astype(jnp.bfloat16)
    qkv_grad = jnp.einsum(
        "td,te->de", normed_one_low, projected_grad, preferred_element_type=jnp.float32
    )
    normed_one_grad = jnp.einsum(
        "te,de->td", projected_grad, qkv_weight, preferred_element_type=jnp.float32
    )
    stream_part, norm1_grad = norm1_back(normed_one_grad)
    tokens_grad = (middle_grad + stream_part).reshape(row_count, stretch_len, model_width)
    device_count = lax.axis_size("dp") * lax.axis_size("seq")
    qkv_sum, out_sum, up_sum, down_sum, norm1_sum, norm2_sum = lax.psum(
        (qkv_grad, out_grad, up_grad, down_grad, norm1_grad, norm2_grad), ("dp", "seq")
    )
    return (
        output,
        tokens_grad,
        norm1_sum / device_count,
        qkv_sum / device_count,
        out_sum / device_count,
        norm2_sum / device_count,
        up_sum / device_count,
        down_sum / device_count,
    )


eps = 1e-05
f32 = jnp.float32
bf16 = jnp.bfloat16
AXES = ("dp", "seq")
GRID_DP, GRID_SEQ = 4, 8
ROOM = 56 * 2**20


def place(y, x, z, c):
    return (y * 2 + x) * GRID_SEQ + z * 2 + c


def pairs(move):
    return [
        (place(y, x, z, c), place(*move(y, x, z, c)))
        for y in range(2)
        for x in range(2)
        for z in range(4)
        for c in range(2)
    ]


INNER = pairs(lambda y, x, z, c: (y, x, 3 - z, c))
INNER = [(a, b) for a, b in INNER if (a % GRID_SEQ) // 2 in (1, 2)]
OUTWARD = pairs(lambda y, x, z, c: (y, x, z ^ 1, c))
OUTWARD = [(a, b) for a, b in OUTWARD if (a % GRID_SEQ) // 2 in (1, 2)]
ALONG_Z = {k: pairs(lambda y, x, z, c, k=k: (y, x, z ^ k, c)) for k in (1, 2, 3)}
CORES = pairs(lambda y, x, z, c: (y, x, z, 1 - c))
FIRST = pairs(lambda y, x, z, c: (y, 1 - x, z, c) if c == 0 else (1 - y, x, z, c))
SECOND = pairs(lambda y, x, z, c: (1 - y, x, z, c) if c == 0 else (y, 1 - x, z, c))


def send(value, perm, tag="send"):
    with jax.named_scope("t_" + tag):
        return lax.ppermute(value, AXES, perm)


def nn(a, b, precision=None):
    return lax.dot_general(
        a, b, (((1,), (0,)), ((), ())), precision=precision, preferred_element_type=f32
    )


def nt(a, b, precision=None):
    return lax.dot_general(
        a, b, (((1,), (1,)), ((), ())), precision=precision, preferred_element_type=f32
    )


def work(micros):
    return pl.CostEstimate(flops=int(micros * 1.16e9), bytes_accessed=0, transcendentals=0)


def here():
    dp, seq = lax.axis_index("dp"), lax.axis_index("seq")
    y, x, z, c = dp // 2, dp % 2, seq // 2, seq % 2
    return z, c, jnp.where(c == 0, x, y), jnp.where(c == 0, y, x)


def kernel_call(body, outs, args, scratch=(), name=None, micros=2, room=16, far=(), out=(), order=None, early=(), onto=(), where=pltpu.VMEM):
    vmem = pl.BlockSpec(memory_space=pltpu.VMEM)
    args = list(args)
    staged = len(args)
    args += list(onto)
    held = len(args)
    args += list(early) + list(order or ())
    ignored = len(args) - held
    outs = [*outs, ((8, 128), f32)]
    shapes = [
        jax.ShapeDtypeStruct(s, d) if n in far or n in out else pltpu.VMEM(s, d) for n, (s, d) in enumerate(outs)
    ]
    specs = [pl.BlockSpec(memory_space=pl.ANY) if n in far else vmem for n in range(len(outs))]
    results = len(outs) - 1

    def whole(*refs):
        refs, mark, rest = refs[: held + ignored + results], refs[held + ignored + results], refs[held + ignored + results + 1 :]
        mark[...] = jnp.zeros((8, 128), f32)
        body(*refs[:held], *refs[held + ignored :], *rest)

    *values, mark = pl.pallas_call(
        whole,
        out_shape=shapes,
        in_specs=[pl.BlockSpec(memory_space=pl.ANY) if staged <= n < held else vmem for n in range(len(args))],
        out_specs=specs,
        scratch_shapes=list(scratch),
        input_output_aliases={staged + n: n for n in range(len(onto))},
        compiler_params=pltpu.CompilerParams(vmem_limit_bytes=room * 2**20),
        name=name,
        cost_estimate=work(micros),
    )(*[a if staged <= n < held else pltpu.with_memory_space_constraint(a, where) for n, a in enumerate(args)])
    if order is not None:
        order[:] = [mark]
    return values


def pick(v, bit):
    return jnp.where(bit == 0, v[:, 0:64], v[:, 64:128])


def normalise(v):
    mean = jnp.mean(v, axis=-1, keepdims=True)
    centred = v - mean
    inv = lax.rsqrt(jnp.mean(centred * centred, axis=-1, keepdims=True) + eps)
    return centred * inv, inv


def normalise_back(e, n, inv):
    return (e - jnp.mean(e, axis=-1, keepdims=True) - n * jnp.mean(e * n, axis=-1, keepdims=True)) * inv


def doc_numbers(doc):
    at = lax.broadcasted_iota(jnp.int32, (128, 128), 0)
    to = lax.broadcasted_iota(jnp.int32, (128, 128), 1)
    upper = (at <= to).astype(f32)
    a8 = lax.broadcasted_iota(jnp.int32, (8, 8), 0)
    t8 = lax.broadcasted_iota(jnp.int32, (8, 8), 1)
    before = (t8 < a8).astype(f32)
    spread = jnp.broadcast_to(jnp.sum(doc, axis=1, keepdims=True), (8, 128))
    high = lax.Precision.HIGHEST
    rows = nn(doc, upper, high) + nn(before, spread, high)
    eye = (at == to).astype(f32)
    cols = nt(eye, rows, high)
    return rows, cols


def row_of(rows, lo, hi):
    return jnp.concatenate([rows[j : j + 1, :] for j in range(lo, hi)], axis=1)


def col_of(cols, lo, hi):
    return jnp.concatenate([cols[:, j : j + 1] for j in range(lo, hi)], axis=0)


def gelu_parts(u):
    return 0.5 + 0.5 * lax.erf(u * 0.7071067811865476), jnp.exp(-0.5 * u * u) * 0.3989422804014327


def prepare(tokens, doc, cot, message, cot_o):
    message[0:128, :] = tokens[...].astype(f32)
    message[128:136, :] = jnp.zeros((8, 512), f32)
    message[128:129, 0:128] = doc[...].astype(f32)
    cot_o[...] = cot[...].astype(f32)


def join(*refs):
    at = 0
    out = refs[-1]
    for ref in refs[:-1]:
        out[at : at + ref.shape[0]] = ref[...]
        at += ref.shape[0]


def joined(order, *values, early=()):
    values = [v[None] if v.ndim == 2 else v for v in values]
    shape = (sum(v.shape[0] for v in values),) + values[0].shape[1:]
    return kernel_call(join, [(shape, f32)], values, name="join", micros=0, order=order, early=early)[0]


def gate(*refs):
    half = len(refs) // 2
    for ref, out in zip(refs[:half], refs[half:]):
        out[...] = ref[...]


def choose_far(near, far, out):
    z, _, _, _ = here()
    inner = (z == 1) | (z == 2)
    for n in range(2):
        out[n] = jnp.where(inner, near[1 - n], far[n])


def head_forward(t0, t1, t2, t3, p0, p1, p2, p3, gain, w, omega,
                 keep, give, phq_o, phk_o, qk_o, v_o, mxd_o, doc_o, nt_o, low):
    z, c, _, _ = here()
    wh = jnp.concatenate([pick(w[:, pl.ds(pl.multiple_of(part * 512 + z * 128, 128), 128)], c) for part in range(3)], axis=1)
    g = gain[...]
    for k, (mine, theirs) in enumerate(((t0, p0), (t1, p1), (t2, p2), (t3, p3))):
        for ref, core in ((mine, c), (theirs, 1 - c)):
            chunk = 2 * jnp.bitwise_xor(z, k) + core
            n, _ = normalise(ref[0:128, :])
            low[pl.ds(pl.multiple_of(chunk * 128, 128), 128), :] = (n * g).astype(bf16)
            doc_o[pl.ds(chunk, 1), :] = ref[128:129, 0:128]
    rows, cols = doc_numbers(doc_o[...])
    nt_o[...] = jnp.transpose(low[:, pl.ds(pl.multiple_of(c * 256, 256), 256)])
    s = 64 ** -0.25
    om = omega[2 * z + c]
    oh = om.astype(bf16)
    ol = (om - oh.astype(f32)).astype(bf16)
    stack = jnp.concatenate([oh, oh, ol], axis=0)

    def feature(v):
        v = v * s
        hi = v.astype(bf16)
        lo = (v - hi.astype(f32)).astype(bf16)
        proj = nn(jnp.concatenate([hi, lo, hi], axis=1), stack)
        return jnp.exp(proj - 0.5 * jnp.sum(v * v, axis=-1, keepdims=True))

    for b in range(4):
        at = pl.ds(256 * b, 256)
        pr = nn(low[at, :], wh)
        qk_o[at, :] = pr[:, 0:128]
        v_o[at, :] = pr[:, 128:192].astype(bf16)
        phq_o[at, :] = feature(pr[:, 0:64]).astype(bf16)
        phk_o[at, :] = feature(pr[:, 64:128]).astype(bf16)
    for b in range(4):
        at = pl.ds(256 * b, 256)
        n = 256 * (b + 1)
        scores = nt(phq_o[at, :], phk_o[0:n, :])
        i = lax.broadcasted_iota(jnp.int32, (256, n), 0) + 256 * b
        j = lax.broadcasted_iota(jnp.int32, (256, n), 1)
        same = (col_of(cols, 2 * b, 2 * b + 2) == row_of(rows, 0, 2 * b + 2)) & (i >= j)
        scores = jnp.where(same, scores, 0.0)
        inv = 1.0 / jnp.sum(scores, axis=-1, keepdims=True)
        mixed = nn(scores.astype(bf16), v_o[0:n, :]) * inv
        mxd_o[at, :] = jnp.concatenate([mixed, jnp.broadcast_to(inv, (256, 64))], axis=1)
        top, bottom = mixed[0:128, :], mixed[128:256, :]
        keep[b] = jnp.where(c == 0, top, bottom)
        give[b] = jnp.where(c == 0, bottom, top)


def pack_pairs(keep, got, b0, b1, b2, b3):
    z, c, _, _ = here()
    for k, out in enumerate((b0, b1, b2, b3)):
        j = jnp.bitwise_xor(z, k)
        a, b = keep[j], got[j]
        out[...] = jnp.where(c == 0, jnp.concatenate([a, b], axis=1), jnp.concatenate([b, a], axis=1))


def unpack_pairs(b0, b1, b2, b3, keep, give):
    z, c, _, _ = here()
    for k, ref in enumerate((b0, b1, b2, b3)):
        j = jnp.bitwise_xor(z, k)
        a, b = ref[:, 0:64], ref[:, 64:128]
        keep[j] = jnp.where(c == 0, a, b)
        give[j] = jnp.where(c == 0, b, a)


def middle_part(b0, b1, b2, b3, tokens, wo, gain, mixed_o, middle_o, normed_o):
    z, _, _, _ = here()
    for k, ref in enumerate((b0, b1, b2, b3)):
        j = jnp.bitwise_xor(z, k)
        mixed_o[:, pl.ds(pl.multiple_of(j * 128, 128), 128)] = ref[...].astype(bf16)
    middle = tokens[...].astype(f32) + nn(mixed_o[...], wo[...])
    middle_o[...] = middle
    n, _ = normalise(middle)
    normed_o[...] = (n * gain[...]).astype(bf16).astype(f32)


def feed_forward(mixed, middle, normed, cot, wu, wd, wo, gain,
                 out_o, mg_o, ml_o, ex0, ex1, ex2, b0, b1, b2, b3, scr):
    z, c, _, _ = here()
    x = normed[...].astype(bf16)
    inc = cot[...]
    total = middle[...]
    back = jnp.zeros((128, 512), f32)
    for u in range(4):
        at = pl.ds(512 * u, 512)
        wub, wdb = wu[:, at], wd[at, :]
        up = nn(x, wub)
        cdf, pdf = gelu_parts(up)
        total = total + nn((up * cdf).astype(bf16), wdb)
        ug = ((cdf + up * pdf) * nt(inc, wdb)).astype(bf16)
        back = back + nt(ug, wub)
    out_o[...] = total.astype(bf16)
    n, inv = normalise(middle[...])
    mg = inc.astype(f32) + normalise_back(gain[...] * back, n, inv)
    mg_o[...] = mg
    low = mg.astype(bf16)
    ml_o[...] = low
    ex0[...] = mixed[:, pl.ds(pl.multiple_of((1 - c) * 256, 256), 256)].astype(f32)
    ex1[...] = low[:, 0:256].astype(f32)
    ex2[...] = low[:, 256:512].astype(f32)
    scr[...] = nt(low, wo[...])
    for k, ref in enumerate((b0, b1, b2, b3)):
        j = jnp.bitwise_xor(z, k)
        ref[...] = scr[:, pl.ds(pl.multiple_of(j * 128, 128), 128)]


def out_part(mixed, mlow, got0, got1, got2, keep, give, scr):
    _, c, first, _ = here()
    mine = mixed[:, pl.ds(pl.multiple_of(c * 256, 256), 256)].astype(f32)
    left = jnp.transpose(jnp.concatenate([mine, got0[...]], axis=0)).astype(bf16)
    theirs = jnp.concatenate([got1[...], got2[...]], axis=1).astype(bf16)
    right = jnp.concatenate([mlow[...], theirs], axis=0)
    scr[...] = nn(left, right)
    keep[...] = scr[pl.ds(pl.multiple_of(first * 128, 128), 128), :]
    give[...] = scr[pl.ds(pl.multiple_of((1 - first) * 128, 128), 128), :]


def add_last(mine, got, out):
    out[...] = (mine[...] + got[...]) * (1.0 / 32)


def join_pieces(p0, p1, p2, p3, out):
    z, _, _, _ = here()
    parts = (p0, p1, p2, p3)
    total = (p0[:, 384:896] + p1[:, 384:896]) + (p2[:, 384:896] + p3[:, 384:896])
    for k, ref in enumerate(parts):
        j = jnp.bitwise_xor(z, k)
        out[k, :, 0:384] = ref[:, 0:384]
        block = total[:, 0:128]
        for n in range(1, 4):
            block = jnp.where(j == n, total[:, 128 * n : 128 * n + 128], block)
        out[k, :, 384:512] = block


def head_backward(keep, got, phq, phk, qk, v, mxd, doc, omega, pg0, pg1, pg2, r_scr, m_scr, pg_o):
    z, c, _, _ = here()
    for b in range(4):
        a, g = keep[b], got[b]
        at = pl.ds(256 * b, 256)
        dm = jnp.concatenate([jnp.where(c == 0, a, g), jnp.where(c == 0, g, a)], axis=0)
        r = dm * mxd[at, 64:128]
        r_scr[at, :] = r.astype(bf16)
        m_scr[at, :] = r * mxd[at, 0:64]
    rows, cols = doc_numbers(doc[...])
    ones = jnp.ones((8, 64), f32)
    s = 64 ** -0.25
    om = omega[2 * z + c].astype(bf16)

    def feature_back(ph, grad, base):
        a = ph.astype(f32) * grad
        return s * nt(a.astype(bf16), om) - (s * s) * base * jnp.sum(a, axis=-1, keepdims=True)

    for b in range(4):
        at = pl.ds(256 * b, 256)
        n = 256 * (b + 1)
        i = lax.broadcasted_iota(jnp.int32, (256, n), 0) + 256 * b
        j = lax.broadcasted_iota(jnp.int32, (256, n), 1)
        same = (col_of(cols, 2 * b, 2 * b + 2) == row_of(rows, 0, 2 * b + 2)) & (i >= j)
        ds = nt(r_scr[at, :], v[0:n, :]) - jnp.sum(m_scr[at, :], axis=-1, keepdims=True)
        ds = jnp.where(same, ds, 0.0).astype(bf16)
        qg = feature_back(phq[at, :], nn(ds, phk[0:n, :]), qk[at, 0:64])
        m = 1024 - 256 * b
        later = pl.ds(256 * b, m)
        j2 = lax.broadcasted_iota(jnp.int32, (256, m), 0)
        i2 = lax.broadcasted_iota(jnp.int32, (256, m), 1)
        same2 = (col_of(cols, 2 * b, 2 * b + 2) == row_of(rows, 2 * b, 8)) & (i2 >= j2)
        scores = jnp.where(same2, nt(phk[at, :], phq[later, :]), 0.0).astype(bf16)
        vg = nn(scores, r_scr[later, :])
        mr = nt(ones, m_scr[later, :], lax.Precision.HIGHEST)[0:1, :]
        ds2 = jnp.where(same2, nt(v[at, :], r_scr[later, :]) - mr, 0.0).astype(bf16)
        kg = feature_back(phk[at, :], nn(ds2, phq[later, :]), qk[at, 64:128])
        rnd = lambda t: t.astype(bf16).astype(f32)
        pg_o[at, :] = rnd(jnp.concatenate([qg, kg], axis=1))
        pg_o[pl.ds(1024 + 256 * (b % 2), 256), 64 * (b // 2) : 64 * (b // 2) + 64] = rnd(vg)
    for n, out in enumerate((pg0, pg1, pg2)):
        out[...] = pg_o[512 * n : 512 * n + 512, :]


def weight_part(m0, m1, m2, t0, t1, t2, nt_low, okeep, ogive, q0, q1, q2, q3, keep, give, scr, g_scr):
    z, c, first, _ = here()
    for b in range(4):
        at = pl.ds(256 * b, 256)
        half = pl.ds(256 * (b % 2), 256)
        lanes = slice(64 * (b // 2), 64 * (b // 2) + 64)
        a, t = ((m0, t0), (m1, t1))[b // 2]
        a, t = a[half, :], t[half, :]
        av, tv = m2[half, lanes], t2[half, lanes]
        h0 = jnp.where(c == 0, a, t)
        h1 = jnp.where(c == 0, t, a)
        scr[at, 0:128] = jnp.concatenate([h0[:, 0:64], h1[:, 0:64]], axis=1)
        scr[at, 128:256] = jnp.concatenate([h0[:, 64:128], h1[:, 64:128]], axis=1)
        scr[at, 256:384] = jnp.concatenate([jnp.where(c == 0, av, tv), jnp.where(c == 0, tv, av)], axis=1)
    for k, ref in enumerate((q0, q1, q2, q3)):
        chunk = 2 * jnp.bitwise_xor(z, k) + c
        ref[...] = scr[pl.ds(pl.multiple_of(chunk * 128, 128), 128), :]
    g_scr[...] = nn(nt_low[...], scr[...].astype(bf16))
    keep[:, 0:384] = g_scr[pl.ds(pl.multiple_of(first * 128, 128), 128), :]
    give[:, 0:384] = g_scr[pl.ds(pl.multiple_of((1 - first) * 128, 128), 128), :]
    keep[:, 384:896] = okeep[...]
    give[:, 384:896] = ogive[...]


def tokens_part(q0, q1, q2, q3, mg, tokens, w, gain, out_o, scr):
    z, _, _, _ = here()
    for k, ref in enumerate((q0, q1, q2, q3)):
        j = jnp.bitwise_xor(z, k)
        for part in range(3):
            scr[:, pl.ds(pl.multiple_of(part * 512 + j * 128, 128), 128)] = ref[:, 128 * part : 128 * part + 128].astype(bf16)
    n, inv = normalise(tokens[...].astype(f32))
    e = gain[...] * nt(scr[...], w[...])
    out_o[...] = mg[...] + normalise_back(e, n, inv)


def add_split(mine, got, keep, give):
    _, _, _, second = here()
    a = pl.ds(pl.multiple_of(second * 64, 64), 64)
    b = pl.ds(pl.multiple_of((1 - second) * 64, 64), 64)
    keep[...] = mine[a, :] + got[a, :]
    give[...] = mine[b, :] + got[b, :]


def ffn_narrow(count, *refs):
    xs, cs, (xb, cb) = refs[:count], refs[count : 2 * count], refs[2 * count :]
    at = 0
    for x, cc in zip(xs, cs):
        for i in range(x.shape[0]):
            xb[pl.ds(at, 128), :] = x[i].astype(bf16)
            cb[pl.ds(at, 128), :] = cc[i].astype(bf16)
            at += 128


def ffn_weights(unit, mine, first, last, xb, cb, wu, wd, *refs):
    if not first:
        before, *refs = refs
    if last:
        theirs, out, up_o = refs
    else:
        (out,) = refs
    _, c, _, _ = here()
    core = c if mine else 1 - c
    place = pl.ds(pl.multiple_of(core * 1024 + 256 * unit, 256), 256)
    wut, wdu = jnp.transpose(wu[:, place]), wd[place, :]
    x, inc = xb[...], cb[...]
    up = nt(wut, x)
    hg = nt(wdu, inc)
    cdf, pdf = gelu_parts(up)
    total_up = nn(((cdf + up * pdf) * hg).astype(bf16), x)
    total_down = nn((up * cdf).astype(bf16), inc)
    if not first:
        total_up = total_up + before[0:256, :]
        total_down = total_down + before[256:512, :]
    if last:
        total_up = (total_up + theirs[0:256, :]) * (1.0 / 32)
        total_down = (total_down + theirs[256:512, :]) * (1.0 / 32)
        up_o[...] = jnp.transpose(total_up)
        part = jnp.sum(total_up * wut.astype(f32), axis=0, keepdims=True)
        out[512:520, :] = jnp.broadcast_to(part, (8, 512))
    out[0:256, :] = total_up
    out[256:512, :] = total_down


def place_mine(*refs):
    ups, both = refs[0:4], refs[4:8]
    up_o, down_o, sems = refs[8:]
    _, c, _, _ = here()
    copies = []
    for n in range(4):
        at = pl.ds(pl.multiple_of(c * 1024 + 256 * n, 256), 256)
        copies.append(pltpu.make_async_copy(ups[n], up_o.at[:, at], sems.at[2 * n]))
        copies.append(pltpu.make_async_copy(both[n].at[256:512, :], down_o.at[at, :], sems.at[2 * n + 1]))
    for copy in copies:
        copy.start()
    for copy in copies:
        copy.wait()


def place_theirs(m0, m1, m2, m3, b0, b1, b2, b3, gain2, up_in, down_in, up_o, down_o, gain_o, ups, sems):
    _, c, _, _ = here()
    copies = []
    for n, both in enumerate((b0, b1, b2, b3)):
        at = pl.ds(pl.multiple_of((1 - c) * 1024 + 256 * n, 256), 256)
        copies.append(pltpu.make_async_copy(both.at[256:512, :], down_o.at[at, :], sems.at[2 * n]))
        copies[-1].start()
    for n, both in enumerate((b0, b1, b2, b3)):
        at = pl.ds(pl.multiple_of((1 - c) * 1024 + 256 * n, 256), 256)
        ups[n] = jnp.transpose(both[0:256, :])
        copies.append(pltpu.make_async_copy(ups.at[n], up_o.at[:, at], sems.at[2 * n + 1]))
        copies[-1].start()
    total = jnp.zeros((1, 512), f32)
    for ref in (m0, m1, m2, m3, b0, b1, b2, b3):
        total = total + ref[512:513, :]
    gain_o[...] = total / gain2[...]
    for copy in copies:
        copy.wait()


def finish(a, b, ca, cb, w, gain, qkv_o, out_o, gain_o):
    z, c, first, second = here()
    for n in range(4):
        for core, ref, r1, r2 in ((c, (a, b)[n // 2], first, second), (1 - c, (ca, cb)[n // 2], second, first)):
            row = core * 256 + jnp.bitwise_xor(r1, n % 2) * 128 + jnp.bitwise_xor(r2, n // 2) * 64
            rows = pl.ds(pl.multiple_of(row, 64), 64)
            for k in range(4):
                j = jnp.bitwise_xor(z, k)
                piece = ref.at[4 * (n % 2) + k]
                for part in range(3):
                    at = pl.ds(pl.multiple_of(part * 512 + j * 128, 128), 128)
                    qkv_o[rows, at] = piece[:, 128 * part : 128 * part + 128]
                out_o[rows, pl.ds(pl.multiple_of(j * 128, 128), 128)] = piece[:, 384:512]
    for r in range(4):
        rows = pl.ds(128 * r, 128)
        acc = jnp.zeros((128, 128), f32)
        for j in range(12):
            lanes = pl.ds(128 * j, 128)
            acc = acc + w[rows, lanes].astype(f32) * qkv_o[rows, lanes]
        lanes = pl.ds(128 * r, 128)
        gain_o[0:1, lanes] = jnp.sum(jnp.transpose(acc), axis=0, keepdims=True) / gain[0:1, lanes]


def across(values):
    return [send(v, CORES) for v in values]


def local_fast(tokens, doc_start, norm1_gain, qkv_weight, out_weight, norm2_gain, up_weight, down_weight, omega, cotangent):
    g1, g2 = norm1_gain.reshape(1, 512), norm2_gain.reshape(1, 512)
    tok, cot = tokens[0], cotangent[0]
    order = []
    call = functools.partial(kernel_call, order=order)
    join = functools.partial(joined, order)
    block = ((128, 128), f32)

    def later(*values):
        return call(gate, [(v.shape, v.dtype) for v in values], values, name="gate", micros=0)

    def wait(*values):
        call(gate, [], [], name="gate", micros=0, early=values)

    def pause(micros):
        call(gate, [], [], name="pause", micros=micros)

    def narrow(xs, cs):
        rows = 128 * sum(v.shape[0] for v in xs)
        return call(functools.partial(ffn_narrow, len(xs)), [((rows, 512), bf16)] * 2, [*xs, *cs], name="ffn_narrow", micros=0)

    def ffn(unit, mine, xc, before=None, theirs=None, micros=0):
        first, last = before is None, theirs is not None
        outs = [((520, 512), f32), ((512, 256), f32)] if last else [((512, 512), f32)]
        more = ([] if first else [before]) + ([theirs] if last else [])
        got = call(
            functools.partial(ffn_weights, unit, mine, first, last), outs, [*xc, up_weight, down_weight, *more],
            (), "ffn_weights", micros, 24,
        )
        return got if last else got[0]

    message, cot_wide = call(prepare, [((136, 512), f32), ((128, 512), f32)], [tok, doc_start, cot], name="prepare", where=pltpu.HBM)
    t = [message] + [send(message, ALONG_Z[k], "tok") for k in (1, 2, 3)]
    ca = join(cot_wide, send(cot_wide, ALONG_Z[1], "c1"), early=t)
    p = [send(v, CORES, "tok") for v in t]
    ca_first = send(ca, FIRST, "ca")
    keep, give, phq, phk, qk, v, mxd, doc, nt_low = call(
        head_forward,
        [((4, 128, 64), f32), ((4, 128, 64), f32), ((1024, 256), bf16), ((1024, 256), bf16), ((1024, 128), f32),
         ((1024, 64), bf16), ((1024, 128), f32), ((8, 128), f32), ((256, 1024), bf16)],
        [*t, *p, g1, qkv_weight, omega], [pltpu.VMEM((1024, 512), bf16)], "head_forward", 2,
    )
    b = call(pack_pairs, [block] * 4, [keep, send(give, CORES, "give")], name="pack_pairs", micros=0)
    b = [b[0]] + [send(b[k], ALONG_Z[k], "mixed") for k in (1, 2, 3)]
    pause(0.8)
    ca_two = join(ca, ca_first, early=[up_weight, down_weight, out_weight])
    ca_other = send(ca_two, SECOND, "ca")
    mixed, middle, normed = call(
        middle_part, [((128, 512), bf16), ((128, 512), f32), ((128, 512), f32)], [*b, tok, out_weight, g2],
        name="middle_part", micros=2.5,
    )
    output, mg, mlow, ex0, ex1, ex2, *b = call(
        feed_forward,
        [((128, 512), bf16), ((128, 512), f32), ((128, 512), bf16)] + [((128, 256), f32)] * 3 + [block] * 4,
        [mixed, middle, normed, cot, up_weight, down_weight, out_weight, g2], [pltpu.VMEM((128, 512), f32)],
        "feed_forward", 1.2, out=(0,),
    )
    b = [b[0]] + [send(b[k], ALONG_Z[k], "mg") for k in (1, 2, 3)]
    ex_other = [send(w, CORES, "ex") for w in (ex0, ex1, ex2)]
    pause(1.5)
    okeep, ogive = call(out_part, [((128, 512), f32)] * 2, [mixed, mlow, *ex_other],
                        [pltpu.VMEM((256, 512), f32)], "out_part", micros=0)
    ca_late, normed = later(ca, normed)
    keep, give = call(unpack_pairs, [((4, 128, 64), f32)] * 2, b, name="unpack_pairs", micros=0)
    got = send(give, CORES, "give")
    x1 = send(normed, ALONG_Z[1], "x1")
    c_inner = send(ca_late, INNER, "c")
    pg = call(
        head_backward, [((512, 128), f32)] * 3, [keep, got, phq, phk, qk, v, mxd, doc, omega],
        [pltpu.VMEM((1024, 64), bf16), pltpu.VMEM((1024, 64), f32), pltpu.VMEM((1536, 128), f32)], "head_backward", 4,
    )
    pg_other = [send(w, CORES, "pg") for w in pg]
    c_a = later(ca_two, ca_other)
    xa = join(normed, x1)
    xa_first = send(xa, FIRST, "xa")
    *q, keep, give = call(
        weight_part, [((128, 384), f32)] * 4 + [((128, 896), f32)] * 2, [*pg, *pg_other, nt_low, okeep, ogive],
        [pltpu.VMEM((1024, 384), f32), pltpu.VMEM((256, 384), f32)], "weight_part", micros=0,
    )
    got = send(give, FIRST, "rs")
    c_inner, xa_late = later(c_inner, xa)
    c_outer = send(c_inner, OUTWARD, "c")
    x_inner = send(xa_late, INNER, "x")
    pause(4.7)
    keep, give = call(add_split, [((64, 896), f32)] * 2, [keep, got], name="add_split", micros=0)
    got = send(give, SECOND, "rs")
    xa_two = join(xa, xa_first)
    xa_other = send(xa_two, SECOND, "xa")
    pause(2.4)
    (cb,) = call(choose_far, [((2, 128, 512), f32)], [c_inner, c_outer], name="choose_far", micros=0)
    cb_first = send(cb, FIRST, "cb")
    (x_inner,) = later(x_inner)
    x_outer = send(x_inner, OUTWARD, "x")
    (piece,) = call(add_last, [((64, 896), f32)], [keep, got], name="add_last", micros=0)
    pause(8.2)
    x_a = later(xa_two, xa_other)
    cb_two = join(cb, cb_first)
    cb_other = send(cb_two, SECOND, "cb")
    (piece,) = later(piece)
    piece_line = [send(piece, ALONG_Z[k], "piece") for k in (1, 2, 3)]
    x_now = narrow(x_a, c_a)
    (xb,) = call(choose_far, [((2, 128, 512), f32)], [x_inner, x_outer], name="choose_far", micros=0)
    xb_first = send(xb, FIRST, "xb")
    total = {}
    for u in range(4):
        total[u, False] = ffn(u, False, x_now)
    for u in range(4):
        total[u, True] = ffn(u, True, x_now)
    (pieces,) = call(join_pieces, [((4, 64, 512), f32)], [piece, *piece_line], name="join_pieces", micros=4.6)
    pieces_first = send(pieces, FIRST, "piece")
    xb_two = join(xb, xb_first)
    xb_other = send(xb_two, SECOND, "xb")
    pause(2.5)
    c_b = later(cb_two, cb_other)
    pause(6.4)
    q = [q[0]] + [send(w, ALONG_Z[k], "q") for k, w in zip((1, 2, 3), later(*q[1:]))]
    x_now = narrow([xb_two], c_b[:1])
    keys = list(total)
    for key in keys[:5]:
        total[key] = ffn(*key, x_now, total[key])
    pieces = [join(pieces, pieces_first)]
    pieces.append(send(pieces[0], SECOND, "piece"))
    for key in keys[5:]:
        total[key] = ffn(*key, x_now, total[key])
    (tokens_grad,) = call(
        tokens_part, [((128, 512), f32)], [*q, mg, tok, qkv_weight, g1], [pltpu.VMEM((128, 1536), bf16)],
        "tokens_part", micros=0, out=(0,),
    )
    pause(3.5)
    x_b = later(xb_other)
    x_now = narrow(x_b, c_b[1:])
    others = [send(ffn(u, False, x_now, total[u, False], micros=0.3), CORES, "part") for u in range(4)]
    wait(pieces[1])
    both, ups = zip(*[ffn(u, True, x_now, total[u, True], others[u], micros=1.2) for u in range(4)])
    both_other = [send(w, CORES, "both") for w in both]
    dma = [pltpu.SemaphoreType.DMA((8,))]
    up_grad, down_grad = call(
        place_mine, [((512, 2048), f32), ((2048, 512), f32)], [*ups, *both], dma, "place_mine", 0, far=(0, 1),
    )
    qkv_grad, out_grad, norm1_grad = call(
        finish, [((512, 1536), f32), ((512, 512), f32), ((1, 512), f32)],
        [*pieces, *[send(w, CORES, "piece") for w in pieces], qkv_weight, g1], (), "finish", 0, out=(0, 1, 2),
    )
    up_grad, down_grad, norm2_grad = call(
        place_theirs, [((512, 2048), f32), ((2048, 512), f32), ((1, 512), f32)], [*both, *both_other, g2],
        [pltpu.VMEM((4, 512, 256), f32), *dma], "place_theirs", 0, far=(0, 1), out=(2,), onto=(up_grad, down_grad),
    )
    return (output[None], tokens_grad[None], norm1_grad[0], qkv_grad, out_grad, norm2_grad[0], up_grad, down_grad)


def solution(mesh):
    placed = (
        P("dp", "seq", None),
        P("dp", "seq"),
        P(),
        P(),
        P(),
        P(),
        P(),
        P(),
        P(),
        P("dp", "seq", None),
    )
    fits = mesh.shape["dp"] == GRID_DP and mesh.shape["seq"] == GRID_SEQ
    return jax.shard_map(
        local_fast if fits else local,
        mesh=mesh,
        in_specs=placed,
        out_specs=(P("dp", "seq", None), P("dp", "seq", None), P(), P(), P(), P(), P(), P()),
        check_vma=False,
    )
```
